32 devices in a mesh: section: 2 (over core), dp: 4 (over z), mp: 2 (over x), rep: 2 (over y).
Axes of the slice: x: 2, y: 2, z: 4, core: 2. Of those that a mesh axis runs over, the one named last changes fastest.
Arguments:
- block_input: bfloat16 [3, 16, 160, 768], P(None, ('dp', 'rep')), may hold values from -6 to 6
- cotangent: bfloat16 [3, 16, 160, 768], P(None, ('dp', 'rep')), may hold values from -6 to 6
- lengths: int32 [3, 16], P(None, ('dp', 'rep')), may hold values from 1 to 160, 1920 in all within a row
- tags: int32 [3, 16], P(None, ('dp', 'rep')), may hold values from 0 to 1, as said below
- w_qkv: bfloat16 [2, 2, 3, 768, 768], P('section', None, None, None, 'mp'), may hold values from -0.21875 to 0.21875
- w_o: bfloat16 [2, 2, 768, 768], P('section', None, 'mp'), may hold values from -1.25 to 1.25
- w_in: bfloat16 [2, 2, 768, 3072], P('section', None, None, 'mp'), may hold values from -0.21875 to 0.21875
- w_out: bfloat16 [2, 2, 3072, 768], P('section', None, 'mp'), may hold values from -0.109375 to 0.109375
- b_qv: float32 [2, 2, 2, 768], P('section', None, None, 'mp'), may hold values from -3 to 3
- b_in: float32 [2, 2, 3072], P('section', None, 'mp'), may hold values from -3 to 3
- gains: float32 [2, 2, 2, 768], P('section'), may hold values from 0.5 to 1.5
- shifts: float32 [2, 2, 4, 768], P('section'), may hold values from -2 to 2
Outputs:
- layer_outputs: bfloat16 [2, 3, 16, 160, 768], P('section', None, ('dp', 'rep'))
- input_grads: bfloat16 [2, 3, 16, 160, 768], P('section', None, ('dp', 'rep'))
- grad_w_qkv: float32 [2, 2, 3, 768, 768], P('section', None, None, 'dp', 'mp')
- grad_w_o: float32 [2, 2, 768, 768], P('section', None, 'mp', 'dp')
- grad_w_in: float32 [2, 2, 768, 3072], P('section', None, 'dp', 'mp')
- grad_w_out: float32 [2, 2, 3072, 768], P('section', None, 'mp', 'dp')
- grad_b_qv: float32 [2, 2, 2, 768], P('section', None, None, 'mp')
- grad_b_in: float32 [2, 2, 3072], P('section', None, 'mp')
- grad_gains: float32 [2, 2, 2, 768], P('section')
- grad_shifts: float32 [2, 2, 4, 768], P('section')
The draws below stay inside these ranges and needn't reach their ends.
Inputs may be any that keep to these rules, and one draw needn't show every extreme that they name: `lengths`: the longest chain of each micro-batch has exactly 160 valid tokens. `tags`: in each micro-batch, the 2 chains of one index of dp and rep (aligned blocks of 2 chains) hold at most 2 heavy and at most 2 light chains; in every draw some such block holds exactly 2 heavy chains and some holds exactly 2 light chains.
All inputs are finite; a program needn't handle non-finite values. No bound on the sum of `lengths` on one device may be relied on, other than what follows from the above.
Results may differ from the reference program's by a relative error of at most 0.028.
Values may be sent and summed in bfloat16 or wider, within the bound.
No kernel may reach another device: no remote copies, remote signals or barrier semaphores. Data moves between devices by JAX's collectives and lax.ppermute only.
A program may use at most 320 MiB of HBM per device.

```python
import math
import jax
import jax.numpy as jnp
import numpy as np
from jax import lax

D = 768
H = 12
HD = 64
FF = 3072
LEN = 160
MB = 3
CPD = 2
CHAINS = 16
LAYERS = 2


def draw_tags(key, part):
    key = jax.random.fold_in(key, 11)
    blocks = MB * CHAINS // CPD
    fewest = CPD // 4
    most_heavy = CPD - CPD // 4
    key_one, key_two, key_three, key_four = jax.random.split(key, 4)
    first_draw = jax.random.randint(key_one, (blocks,), fewest, most_heavy + 1)
    second_draw = jax.random.randint(key_two, (blocks,), fewest, most_heavy + 1)
    heavy_counts = jnp.maximum(first_draw, second_draw)
    block_order = jax.random.permutation(key_three, blocks)
    heavy_counts = heavy_counts.at[block_order[0]].set(most_heavy)
    heavy_counts = heavy_counts.at[block_order[1]].set(fewest)
    positions = jax.vmap(lambda sub_key: jax.random.permutation(sub_key, CPD))(jax.random.split(key_four, blocks))
    labels = (positions >= heavy_counts[:, None]).astype(jnp.int32)
    return labels.reshape(MB, CHAINS)


def level_of(key, shape, cuts, least, top_value):
    level = 1.0
    for dim, blocks in cuts:
        draws = jax.random.uniform(jax.random.fold_in(jax.random.fold_in(key, 6), dim), (blocks,), jnp.float32, least / len(cuts), top_value / len(cuts))
        level = level * jnp.repeat(jnp.exp(draws), shape[dim] // blocks).reshape((-1,) + (1,) * (len(shape) - 1 - dim))
    return level


def profile(number_of, total, bound, lean):
    portions = [(1 << 20) // math.isqrt(grade ** lean) + 1 for grade in range(2, number_of + 1)]
    surplus, holding = total - bound - (number_of - 1), [1] * (number_of - 1)
    while surplus > 0:
        free = [i for i in range(number_of - 1) if holding[i] < bound]
        mass, remaining = sum([portions[i] for i in free]), surplus
        for i in free:
            extra = min(bound - holding[i], max(1, remaining * portions[i] // mass), surplus)
            holding[i] = holding[i] + extra
            surplus = surplus - extra
    return np.array([bound] + holding)


def ragged(own_key, count, total, most, lean):
    if count == 2:
        one = jax.random.randint(own_key, (), max(1, total - most), min(most, total - 1) + 1)
        return jnp.stack([one, total - one])
    tallies = jnp.asarray(profile(count, total, most, lean), jnp.int32)
    pairs = (count - 1) // 2
    giver, taker = tallies[1:1 + 2 * pairs:2], tallies[2:2 + 2 * pairs:2]
    margin = jnp.minimum(giver - 1, most - taker)
    passed = jax.random.randint(jax.random.fold_in(own_key, 1), (pairs,), 0, 1 << 20) % (margin + 1)
    tallies = tallies.at[1:1 + 2 * pairs:2].set(giver - passed).at[2:2 + 2 * pairs:2].set(taker + passed)
    return tallies[jax.random.permutation(jax.random.fold_in(own_key, 2), count)]


def bell_draw(own_key, dims, scale, limit, cuts=(), kind=jnp.bfloat16):
    level = level_of(own_key, dims, cuts, -0.22, 0.18) if cuts else 1.0
    result = jax.random.normal(own_key, dims, jnp.float32) * scale * level
    return jnp.minimum(jnp.maximum(result, -limit), limit).astype(kind)


def setup_inputs(seed: int = 0) -> dict:
    key_of = jax.random.split(jax.random.key(seed), 13)
    block_input = bell_draw(key_of[0], (MB, CHAINS, LEN, D), 1.0, 6.0, ((1, 8),))
    cotangent = bell_draw(key_of[1], (MB, CHAINS, LEN, D), 1.0, 6.0, ((1, 8),))
    lengths = jax.vmap(lambda own: ragged(own, CHAINS, CHAINS * LEN * 3 // 4, LEN, 1))(jax.random.split(key_of[2], MB)).reshape((MB, CHAINS)).astype(jnp.int32)
    tags = draw_tags(jax.random.fold_in(key_of[12], 71), 0)
    w_qkv = bell_draw(key_of[4], (LAYERS, 2, 3, D, D), D ** -0.5, 0.21875, ((0, 2), (4, 2)))
    w_o = bell_draw(key_of[5], (LAYERS, 2, D, D), (D // 32) ** -0.5, 1.25, ((0, 2), (2, 2)))
    w_in = bell_draw(key_of[6], (LAYERS, 2, D, FF), D ** -0.5, 0.21875, ((0, 2), (3, 2)))
    w_out = bell_draw(key_of[7], (LAYERS, 2, FF, D), FF ** -0.5, 0.109375, ((0, 2), (2, 2)))
    b_qv = bell_draw(key_of[8], (LAYERS, 2, 2, D), 0.5, 3.0, ((0, 2), (3, 2)), jnp.float32)
    b_in = bell_draw(key_of[9], (LAYERS, 2, FF), 0.5, 3.0, ((0, 2), (2, 2)), jnp.float32)
    gains = jnp.clip(1.0 + 0.1 * jax.random.normal(key_of[10], (LAYERS, 2, 2, D), jnp.float32), 0.5, 1.5)
    shifts = bell_draw(key_of[11], (LAYERS, 2, 4, D), 0.3, 2.0, ((0, 2),), jnp.float32)
    return dict(block_input=block_input, cotangent=cotangent, lengths=lengths, tags=tags, w_qkv=w_qkv, w_o=w_o, w_in=w_in, w_out=w_out, b_qv=b_qv, b_in=b_in, gains=gains, shifts=shifts)


EPS = 1e-05
HIGH = lax.Precision.HIGHEST

@jax.custom_vjp
def low(v):
    return lax.optimization_barrier(v.astype(jnp.bfloat16)).astype(jnp.float32)

@jax.custom_vjp
def low_back(v):
    return v

def low_keep(v):
    return (low(v), None)

def low_pass(kept, grad):
    return (grad,)

def back_keep(v):
    return (v, None)

def back_low(kept, grad):
    return (low(grad),)
low.defvjp(low_keep, low_pass)
low_back.defvjp(back_keep, back_low)

def project(stream, weight, is_light):
    return jnp.where(is_light, jnp.dot(stream, weight[1], precision=HIGH), jnp.dot(stream, weight[0], precision=HIGH))

def choose(vectors, is_light):
    return jnp.where(is_light, vectors[1], vectors[0])

def normalize(resid, gain, shift):
    mean = lax.optimization_barrier(jnp.mean(resid, -1, keepdims=True))
    centred = resid - mean
    spread = lax.optimization_barrier(jnp.mean(centred * centred, -1, keepdims=True))
    return centred * lax.rsqrt(spread + EPS) * gain + shift

def attend(group):
    query, key, value, key_mask = group
    scores = jnp.einsum('bqhe,bkhe->bhqk', query, key, precision=HIGH) * 0.125
    scores = low_back(scores)
    scores = jnp.where(key_mask[:, None, None, :], scores, -1e+30)
    probs = low(jax.nn.softmax(scores, axis=-1))
    return jnp.einsum('bhqk,bkhe->bqhe', probs, value, precision=HIGH)

def encoder_layer(stream, w_qkv, w_o, w_in, w_out, b_qv, b_in, gains, shifts, is_light, key_mask):
    stream = low_back(stream)
    query = low(low_back(project(stream, w_qkv[:, 0], is_light)) + choose(b_qv[:, 0], is_light))
    key = low(low_back(project(stream, w_qkv[:, 1], is_light)))
    value = low(low_back(project(stream, w_qkv[:, 2], is_light)) + choose(b_qv[:, 1], is_light))
    blocks = key_mask.shape[0] // 8
    layout = (blocks, 8, LEN, H, HD)
    mixed = lax.map(jax.checkpoint(attend), (query.reshape(layout), key.reshape(layout), value.reshape(layout), key_mask.reshape(blocks, 8, LEN)))
    attended = low(low_back(mixed.reshape(stream.shape)))
    branch = low_back(project(attended, w_o, is_light)) + choose(shifts[:, 0], is_light)
    hidden = normalize(stream + branch, choose(gains[:, 0], is_light), choose(shifts[:, 1], is_light))
    pre_act = low_back(project(low(hidden), w_in, is_light)) + choose(b_in, is_light)
    active = low(jax.nn.gelu(pre_act, approximate=False))
    feed = low_back(project(active, w_out, is_light)) + choose(shifts[:, 2], is_light)
    return low(normalize(hidden + feed, choose(gains[:, 1], is_light), choose(shifts[:, 3], is_light)))

def reference(block_input, cotangent, lengths, tags, w_qkv, w_o, w_in, w_out, b_qv, b_in, gains, shifts):
    tokens = MB * CHAINS * LEN
    weights = tuple((array.astype(jnp.float32) for array in (w_qkv, w_o, w_in, w_out, b_qv, b_in, gains, shifts)))
    stream = block_input.astype(jnp.float32).reshape(tokens, D)
    places = jnp.arange(LEN, dtype=jnp.int32)
    valid = places[None, None, :] < lengths[:, :, None]
    key_mask = valid.reshape(MB * CHAINS, LEN)
    is_light = jnp.broadcast_to((tags == 1)[:, :, None], (MB, CHAINS, LEN)).reshape(tokens, 1)

    def forward(first_in, second_delta, params):
        first_out = encoder_layer(first_in, *[param[0] for param in params], is_light, key_mask)
        second_out = encoder_layer(first_out + second_delta, *[param[1] for param in params], is_light, key_mask)
        return (first_out, second_out)
    outputs, pull = jax.vjp(forward, stream, jnp.zeros_like(stream), weights)
    target = cotangent.astype(jnp.float32).reshape(tokens, D) * valid.reshape(tokens, 1).astype(jnp.float32)
    grad_first, grad_second, grad_params = pull((jnp.zeros_like(stream), target))
    full = (MB, CHAINS, LEN, D)
    layer_outputs = jnp.stack([outputs[0].reshape(full), outputs[1].reshape(full)]).astype(jnp.bfloat16)
    input_grads = jnp.stack([grad_first.reshape(full), grad_second.reshape(full)]).astype(jnp.bfloat16)
    return (layer_outputs, input_grads, grad_params[0], grad_params[1], grad_params[2], grad_params[3], grad_params[4], grad_params[5], grad_params[6], grad_params[7])
```

```python
import functools

import jax
import jax.numpy as jnp
from jax import lax
from jax.experimental import pallas as pl
from jax.experimental.pallas import tpu as pltpu
from jax.sharding import PartitionSpec as P

HD = 64
EPS = 1e-05
BF = jnp.bfloat16
F32 = jnp.float32
VMEM_BYTES = 48 * 1024 * 1024

GAIN_ONE, GAIN_TWO = 0, 768
SHIFT = (1536, 2304, 3072, 3840)
BIAS_Q, BIAS_V, BIAS_IN = 4608, 4992, 5376
PACKED = 6912
WIDTH, LOCAL, HIDDEN, HALF = 768, 384, 1536, 768

NN = (((1,), (0,)), ((), ()))
NT = (((1,), (1,)), ((), ()))
TN = (((0,), (0,)), ((), ()))


def mm(left, right, dims=NN):
    return lax.dot_general(left, right, dims, preferred_element_type=F32)


def swap(block, axis):
    return lax.ppermute(block, axis, [(0, 1), (1, 0)])


def chain_scalars(meta, chain):
    return meta[2 + 2 * chain], meta[3 + 2 * chain]


def layer_norm(resid):
    mean = jnp.mean(resid, -1, keepdims=True)
    centred = resid - mean
    inverse = lax.rsqrt(jnp.mean(centred * centred, -1, keepdims=True) + EPS)
    return centred * inverse, inverse


def layer_norm_back(grad, gain, normed, inverse):
    scaled = grad * gain
    return inverse * (
        scaled
        - jnp.mean(scaled, -1, keepdims=True)
        - normed * jnp.mean(scaled * normed, -1, keepdims=True)
    )


def start_load(own, got, is_own, tag, place, sem):
    @pl.when(is_own)
    def _():
        pltpu.make_async_copy(own.at[tag], place, sem).start()

    @pl.when(jnp.logical_not(is_own))
    def _():
        pltpu.make_async_copy(got.at[tag], place, sem).start()


def wait_load(own, tag, place, sem):
    pltpu.make_async_copy(own.at[tag], place, sem).wait()


def vec_reader(vec, tag):
    return lambda at, extent=WIDTH: vec[pl.ds(tag, 1), at : at + extent]


def column_sum(values):
    return jnp.sum(values, axis=0, keepdims=True)


def half_mask(values, which):
    lanes = lax.broadcasted_iota(jnp.int32, values.shape, 1)
    keep = (lanes < HD) if which == 0 else (lanes >= HD)
    return jnp.where(keep, values, jnp.zeros_like(values))


def attend(x, vector, length, wq, out_qkv, out_probs, out_att):
    span = x.shape[0]
    parts = []
    for j in range(3):
        value = mm(x, wq[j])
        if j == 0:
            value = value + vector(BIAS_Q, LOCAL)
        if j == 2:
            value = value + vector(BIAS_V, LOCAL)
        value = value.astype(BF)
        out_qkv[:, j * LOCAL : (j + 1) * LOCAL] = value
        parts.append(value)
    query, key, value = parts
    keys = lax.broadcasted_iota(jnp.int32, (span, span), 0)
    usable = keys < length
    mixed = []
    for pair in range(LOCAL // 128):
        at = slice(pair * 128, pair * 128 + 128)
        total = None
        for which in range(2):
            scores = mm(half_mask(key[:, at], which), query[:, at], NT) * 0.125
            scores = jnp.where(usable, scores, -1e30)
            raised = jnp.exp(scores - jnp.max(scores, axis=0, keepdims=True))
            probs = (raised * (1.0 / jnp.sum(raised, axis=0, keepdims=True))).astype(BF)
            out_probs[2 * pair + which] = probs
            term = mm(probs, half_mask(value[:, at], which), TN)
            total = term if total is None else total + term
        mixed.append(total.astype(BF))
    att = jnp.concatenate(mixed, axis=1)
    out_att[...] = att
    return att


def attention_kernel(
    layer, chain, meta, *refs
):
    if layer == 0:
        x_ref, vec, own_q, got_q, own_o, got_o, *refs = refs
        out_qkv, out_probs, out_att, out_branch, wq, wo, sems = refs
    else:
        feed_own, feed_got, r1, vec_before, vec, own_q, got_q, own_o, got_o, *refs = refs
        out_x, out_r2, out_qkv, out_probs, out_att, out_branch, wq, wo, sems = refs
    length, tag = chain_scalars(meta, chain)
    is_own = meta[0] == layer
    start_load(own_q, got_q, is_own, tag, wq, sems.at[0])
    start_load(own_o, got_o, is_own, tag, wo, sems.at[1])
    vector = vec_reader(vec, tag)
    if layer == 0:
        x = x_ref[0, 0]
    else:
        before = vec_reader(vec_before, tag)
        normed, _ = layer_norm(r1[...])
        hidden = normed * before(GAIN_ONE) + before(SHIFT[1])
        r2 = hidden + ((feed_own[...].astype(F32) + feed_got[...].astype(F32)) + before(SHIFT[2]))
        out_r2[...] = r2
        normed, _ = layer_norm(r2)
        x = (normed * before(GAIN_TWO) + before(SHIFT[3])).astype(BF)
        out_x[...] = x
    wait_load(own_q, tag, wq, sems.at[0])
    att = attend(x, vector, length, wq, out_qkv, out_probs, out_att)
    wait_load(own_o, tag, wo, sems.at[1])
    out_branch[...] = mm(att, wo[...]).astype(BF)


def feed_kernel(layer, chain, meta, x_ref, own, got, vec, own_i, got_i, own_d, got_d, *refs):
    out_r1, out_low, out_act, out_slope, out_feed, wi, wd, sems = refs
    _, tag = chain_scalars(meta, chain)
    is_own = meta[0] == layer
    start_load(own_i, got_i, is_own, tag, wi, sems.at[0])
    start_load(own_d, got_d, is_own, tag, wd, sems.at[1])
    vector = vec_reader(vec, tag)
    x = x_ref[0, 0] if layer == 0 else x_ref[...]
    branch = (own[...].astype(F32) + got[...].astype(F32)) + vector(SHIFT[0])
    r1 = x.astype(F32) + branch
    out_r1[...] = r1
    normed, _ = layer_norm(r1)
    low = (normed * vector(GAIN_ONE) + vector(SHIFT[1])).astype(BF)
    out_low[...] = low
    wait_load(own_i, tag, wi, sems.at[0])
    step = 512
    for at in range(0, HIDDEN, step):
        pre = mm(low, wi[:, at : at + step]) + vector(BIAS_IN + at, step)
        cdf = 0.5 + 0.5 * lax.erf(pre * 0.7071067811865476)
        pdf = jnp.exp(pre * pre * -0.5) * 0.3989422804014327
        out_act[:, at : at + step] = (pre * cdf).astype(BF)
        out_slope[:, at : at + step] = (cdf + pre * pdf).astype(BF)
    wait_load(own_d, tag, wd, sems.at[1])
    out_feed[...] = mm(out_act[...], wd[...]).astype(BF)


def feed_back_kernel(layer, chain, meta, *refs):
    if layer == 1:
        own, got, r1, cot, vec, act_slope, own_i, got_i, own_d, got_d, *refs = refs
        out_y, out_dr2, out_df, out_du, out_dh, out_vec, wi, wd, sems = refs
    else:
        own, got, dr1, r2_ref, vec, act_slope, own_i, got_i, own_d, got_d, *refs = refs
        out_y, out_dr2, out_df, out_du, out_dh, out_vec, wi, wd, sems = refs
    length, tag = chain_scalars(meta, chain)
    is_own = meta[0] == layer
    start_load(own_d, got_d, is_own, tag, wd, sems.at[1])
    start_load(own_i, got_i, is_own, tag, wi, sems.at[0])
    vector = vec_reader(vec, tag)
    gain = vector(GAIN_TWO)
    both = own[...].astype(F32) + got[...].astype(F32)
    if layer == 1:
        normed, _ = layer_norm(r1[...])
        hidden = normed * vector(GAIN_ONE) + vector(SHIFT[1])
        normed, inverse = layer_norm(hidden + (both + vector(SHIFT[2])))
        out_y[...] = (normed * gain + vector(SHIFT[3])).astype(BF)
        tokens = lax.broadcasted_iota(jnp.int32, both.shape, 0)
        dy = jnp.where(tokens < length, cot[0, 0].astype(F32), 0.0)
    else:
        normed, inverse = layer_norm(r2_ref[...])
        low = (both + dr1[...]).astype(BF)
        out_y[...] = low
        dy = low.astype(F32)
    dr2 = layer_norm_back(dy, gain, normed, inverse)
    out_dr2[...] = dr2
    out_vec[:, 0:768] = column_sum(dy * normed)
    out_vec[:, 768:1536] = column_sum(dr2)
    out_vec[:, 1536:2304] = column_sum(dy)
    df = dr2.astype(BF)
    out_df[...] = df
    wait_load(own_d, tag, wd, sems.at[1])
    step = 512
    for at in range(0, HIDDEN, step):
        du = mm(df, wd[at : at + step, :], NT) * act_slope[:, at : at + step].astype(F32)
        out_vec[:, 2304 + at : 2304 + at + step] = column_sum(du)
        out_du[:, at : at + step] = du.astype(BF)
    wait_load(own_i, tag, wi, sems.at[0])
    out_dh[...] = mm(out_du[...], wi[...], NT).astype(BF)


def attention_back_kernel(
    layer, chain, meta, own, got, dr2, r1, vec, qkv, probs_ref, own_q, got_q, own_o, got_o, *refs
):
    out_dr1, out_dz, out_dqkv, out_dx, out_vec, wq, wo, sems = refs
    _, tag = chain_scalars(meta, chain)
    is_own = meta[0] == layer
    start_load(own_o, got_o, is_own, tag, wo, sems.at[1])
    start_load(own_q, got_q, is_own, tag, wq, sems.at[0])
    vector = vec_reader(vec, tag)
    dh = (own[...].astype(F32) + got[...].astype(F32)) + dr2[...]
    normed, inverse = layer_norm(r1[...])
    dr1 = layer_norm_back(dh, vector(GAIN_ONE), normed, inverse)
    out_dr1[...] = dr1
    out_vec[:, 0:768] = column_sum(dh * normed)
    out_vec[:, 768:1536] = column_sum(dr1)
    out_vec[:, 1536:2304] = column_sum(dh)
    dz = dr1.astype(BF)
    out_dz[...] = dz
    wait_load(own_o, tag, wo, sems.at[1])
    datt = mm(dz, wo[...], NT).astype(BF)
    query, key, value = (qkv[:, j * LOCAL : (j + 1) * LOCAL] for j in range(3))
    for pair in range(LOCAL // 128):
        at = slice(pair * 128, pair * 128 + 128)
        dv = dq = dk = None
        for which in range(2):
            probs = probs_ref[2 * pair + which]
            dv_term = mm(probs, half_mask(datt[:, at], which))
            dprobs = mm(half_mask(value[:, at], which), datt[:, at], NT)
            wide = probs.astype(F32)
            dscores = wide * (dprobs - jnp.sum(wide * dprobs, axis=0, keepdims=True))
            dscores = dscores.astype(BF)
            dk_term = mm(dscores, half_mask(query[:, at], which))
            dq_term = mm(dscores, half_mask(key[:, at], which), TN)
            dv = dv_term if dv is None else dv + dv_term
            dk = dk_term if dk is None else dk + dk_term
            dq = dq_term if dq is None else dq + dq_term
        dq = dq * 0.125
        dk = dk * 0.125
        low = pair * 128
        out_vec[:, 2304 + low : 2304 + low + 128] = column_sum(dq)
        out_vec[:, 2688 + low : 2688 + low + 128] = column_sum(dv)
        out_dqkv[:, low : low + 128] = dq.astype(BF)
        out_dqkv[:, LOCAL + low : LOCAL + low + 128] = dk.astype(BF)
        out_dqkv[:, 2 * LOCAL + low : 2 * LOCAL + low + 128] = dv.astype(BF)
    wait_load(own_q, tag, wq, sems.at[0])
    dx = None
    for j in range(3):
        term = mm(out_dqkv[:, j * LOCAL : (j + 1) * LOCAL], wq[j], NT)
        dx = term if dx is None else dx + term
    out_dx[...] = dx.astype(BF)


def token_tags(meta, chains, span):
    where = lax.broadcasted_iota(jnp.int32, (1, chains * span), 1)
    tags = jnp.full((1, chains * span), chain_scalars(meta, 0)[1], jnp.int32)
    for chain in range(1, chains):
        tags = jnp.where(where >= chain * span, chain_scalars(meta, chain)[1], tags)
    return tags


def feed_grad_kernel(chains, meta, *refs):
    df, act, low, du = (refs[i * chains : (i + 1) * chains] for i in range(4))
    keep_d, send_d, keep_i, send_i, act_all, du_all = refs[4 * chains :]
    span = act[0].shape[0]
    first = pl.program_id(0) == 0

    @pl.when(first)
    def _():
        for chain in range(chains):
            at = slice(chain * span, (chain + 1) * span)
            act_all[at, :] = act[chain][...]
            du_all[at, :] = du[chain][...]

    tags = token_tags(meta, chains, span)
    mine = tags == meta[0]
    for lefts, rights, keep, send in ((df, act_all, keep_d, send_d), (low, du_all, keep_i, send_i)):
        left = jnp.concatenate([ref[...] for ref in lefts], axis=0).T
        for mask, out in ((mine, keep), (jnp.logical_not(mine), send)):
            masked = jnp.where(mask, left, jnp.zeros_like(left))
            for half in range(2):
                slot = jnp.where(meta[1] == half, 0, 1)
                value = mm(masked, rights[:, half * HALF : (half + 1) * HALF])
                out[slot] = value.astype(BF)


def attention_grad_kernel(chains, meta, *refs):
    dz, att, x, dqkv = (refs[i * chains : (i + 1) * chains] for i in range(4))
    keep, send, att_all, dqkv_all = refs[4 * chains :]
    span = att[0].shape[0]
    first = pl.program_id(0) == 0

    @pl.when(first)
    def _():
        for chain in range(chains):
            at = slice(chain * span, (chain + 1) * span)
            att_all[at, :] = att[chain][...]
            dqkv_all[at, :] = dqkv[chain][...]

    tags = token_tags(meta, chains, span)
    mine = tags == meta[0]
    slots = [jnp.where(meta[1] == half, 0, 1) for half in range(2)]
    left_z = jnp.concatenate([ref[...] for ref in dz], axis=0).T
    left_x = jnp.concatenate([ref[...].reshape(span, -1) for ref in x], axis=0).T
    for mask, out in ((mine, keep), (jnp.logical_not(mine), send)):
        masked = jnp.where(mask, left_z, jnp.zeros_like(left_z))
        out[slots[0], :, 0:LOCAL] = mm(masked, att_all[...]).astype(BF)
        masked = jnp.where(mask, left_x, jnp.zeros_like(left_x))
        out[slots[0], :, LOCAL:HALF] = mm(masked, dqkv_all[:, 0:LOCAL]).astype(BF)
        out[slots[1], :, :] = mm(masked, dqkv_all[:, LOCAL : 3 * LOCAL]).astype(BF)


ANY = pl.BlockSpec(memory_space=pl.ANY)


def whole(shape):
    return pl.BlockSpec(shape, lambda i, meta: (0,) * len(shape))


def call(body, meta, operands, in_specs, outs, scratch, name, flops, steps=1, out_specs=None):
    shapes = [jax.ShapeDtypeStruct(shape, kind) for shape, kind in outs]
    if out_specs is None:
        out_specs = [whole(shape) for shape, _ in outs]
    moved = sum(v.size * v.dtype.itemsize for v, spec in zip(operands, in_specs) if spec is not ANY)
    moved += sum(v.size * v.dtype.itemsize for v in shapes)
    return pl.pallas_call(
        body,
        out_shape=shapes,
        grid_spec=pltpu.PrefetchScalarGridSpec(
            num_scalar_prefetch=1,
            grid=(steps,),
            in_specs=in_specs,
            out_specs=out_specs,
            scratch_shapes=scratch,
        ),
        compiler_params=pltpu.CompilerParams(vmem_limit_bytes=VMEM_BYTES),
        cost_estimate=pl.CostEstimate(flops=flops, bytes_accessed=moved, transcendentals=0),
        name=name,
    )(meta, *operands)


def on_device(
    block_input, cotangent, lengths, tags, w_qkv, w_o, w_in, w_out, b_qv, b_in, gains, shifts
):
    micro, per, span, width = block_input.shape
    section = lax.axis_index("section")
    rep = lax.axis_index("rep")
    chains = range(micro)
    layers = range(2)

    own_chain = lambda array: lax.dynamic_index_in_dim(array, section, 1, keepdims=False)
    pairs = jnp.stack([own_chain(lengths), own_chain(tags)], axis=1).reshape(-1)
    meta = jnp.concatenate([jnp.stack([section, rep]).astype(jnp.int32), pairs])
    vec_own = jnp.concatenate(
        [gains[0].reshape(2, -1), shifts[0].reshape(2, -1), b_qv[0].reshape(2, -1), b_in[0]], axis=1
    )
    own_q, own_o, own_i, own_d = w_qkv[0], w_o[0], w_in[0], w_out[0]
    vec_got = swap(vec_own, "section")
    got_q, got_o, got_i, got_d = (swap(w, "section") for w in (own_q, own_o, own_i, own_d))
    vecs = [jnp.where(section == layer, vec_own, vec_got) for layer in layers]

    vec_spec = whole((2, PACKED))
    row = whole((span, width))
    row_in = [
        pl.BlockSpec((1, 1, span, width), lambda i, meta, chain=chain: (chain, meta[0], 0, 0))
        for chain in chains
    ]
    qkv_scratch = [
        pltpu.VMEM((3, WIDTH, LOCAL), BF),
        pltpu.VMEM((LOCAL, WIDTH), BF),
        pltpu.SemaphoreType.DMA((2,)),
    ]
    feed_scratch = [
        pltpu.VMEM((WIDTH, HIDDEN), BF),
        pltpu.VMEM((HIDDEN, WIDTH), BF),
        pltpu.SemaphoreType.DMA((2,)),
    ]
    heads = LOCAL // HD
    att_outs = [
        ((span, 3 * LOCAL), BF),
        ((heads, span, span), BF),
        ((span, LOCAL), BF),
        ((span, WIDTH), BF),
    ]
    att_flops = 2 * span * WIDTH * 4 * LOCAL + 4 * span * span * LOCAL
    feed_flops = 4 * span * WIDTH * HIDDEN

    xs = [[block_input] * micro, [None] * micro]
    r1s, r2s, lows, acts, slopes, feeds = ([[None] * micro for _ in layers] for _ in range(6))
    qkvs, probs, atts = ([[None] * micro for _ in layers] for _ in range(3))
    for layer in layers:
        for chain in chains:
            body = functools.partial(attention_kernel, layer, chain)
            weights = [own_q, got_q, own_o, got_o]
            if layer == 0:
                operands = [block_input, vecs[0]] + weights
                specs = [row_in[chain], vec_spec] + [ANY] * 4
                outs = att_outs
            else:
                operands = [*feeds[0][chain], r1s[0][chain], vecs[0], vecs[1]] + weights
                specs = [row, row, row, vec_spec, vec_spec] + [ANY] * 4
                outs = [((span, WIDTH), BF), ((span, WIDTH), F32)] + att_outs
            got = call(
                body, meta, operands, specs, outs, qkv_scratch, f"attention{layer}{chain}", att_flops
            )
            if layer == 1:
                xs[1][chain], r2s[0][chain], *got = got
            qkvs[layer][chain], probs[layer][chain], atts[layer][chain], branch = got
            feeds[layer][chain] = (branch, swap(branch, "mp"))
        for chain in chains:
            body = functools.partial(feed_kernel, layer, chain)
            operands = [xs[layer][chain], *feeds[layer][chain], vecs[layer], own_i, got_i, own_d, got_d]
            specs = [row_in[chain] if layer == 0 else row, row, row, vec_spec] + [ANY] * 4
            outs = [
                ((span, WIDTH), F32),
                ((span, WIDTH), BF),
                ((span, HIDDEN), BF),
                ((span, HIDDEN), BF),
                ((span, WIDTH), BF),
            ]
            r1s[layer][chain], lows[layer][chain], acts[layer][chain], slopes[layer][chain], part = call(
                body, meta, operands, specs, outs, feed_scratch, f"feed{layer}{chain}", feed_flops
            )
            feeds[layer][chain] = (part, swap(part, "mp"))

    lasts, y_grads, vec_grads = [None] * micro, [None] * micro, [[None] * micro for _ in layers]
    dr1s, dxs = [None] * micro, [None] * micro
    ffn_grads, att_grads = [None, None], [None, None]
    for layer in reversed(layers):
        dr2s, dfs, dus, dhs, vec_two = ([None] * micro for _ in range(5))
        for chain in chains:
            body = functools.partial(feed_back_kernel, layer, chain)
            weights = [own_i, got_i, own_d, got_d]
            if layer == 1:
                operands = [*feeds[1][chain], r1s[1][chain], cotangent]
                specs = [row, row, row, row_in[chain]]
            else:
                operands = [*dxs[chain], dr1s[chain], r2s[0][chain]]
                specs = [row, row, row, row]
            outs = [
                ((span, WIDTH), BF),
                ((span, WIDTH), F32),
                ((span, WIDTH), BF),
                ((span, HIDDEN), BF),
                ((span, WIDTH), BF),
                ((1, 3 * WIDTH + HIDDEN), F32),
            ]
            y, dr2s[chain], dfs[chain], dus[chain], dh, vec_two[chain] = call(
                body,
                meta,
                operands + [vecs[layer], slopes[layer][chain]] + weights,
                specs + [vec_spec, whole((span, HIDDEN))] + [ANY] * 4,
                outs,
                feed_scratch,
                f"feed_back{layer}{chain}",
                feed_flops,
            )
            if layer == 1:
                lasts[chain] = y
            else:
                y_grads[chain] = y
            dhs[chain] = (dh, swap(dh, "mp"))
        body = functools.partial(feed_grad_kernel, micro)
        rows = micro * span
        block = 256
        column = pl.BlockSpec((span, block), lambda i, meta: (0, i))
        full = whole((span, HIDDEN))
        grad_out = ((2, WIDTH, HALF), BF)
        grad_spec = pl.BlockSpec((2, block, HALF), lambda i, meta: (0, i, 0))
        ffn_grads[layer] = call(
            body,
            meta,
            dfs + acts[layer] + lows[layer] + dus,
            [column] * micro + [full] * micro + [column] * micro + [full] * micro,
            [grad_out] * 4,
            [pltpu.VMEM((rows, HIDDEN), BF)] * 2,
            f"feed_grad{layer}",
            8 * rows * WIDTH * HIDDEN,
            WIDTH // block,
            [grad_spec] * 4,
        )
        dzs, dqkvs, vec_one = ([None] * micro for _ in range(3))
        for chain in chains:
            body = functools.partial(attention_back_kernel, layer, chain)
            operands = [*dhs[chain], dr2s[chain], r1s[layer][chain], vecs[layer], qkvs[layer][chain]]
            specs = [row, row, row, row, vec_spec, whole((span, 3 * LOCAL))]
            operands += [probs[layer][chain], own_q, got_q, own_o, got_o]
            specs += [whole((heads, span, span))] + [ANY] * 4
            outs = [
                ((span, WIDTH), F32),
                ((span, WIDTH), BF),
                ((span, 3 * LOCAL), BF),
                ((span, WIDTH), BF),
                ((1, 3 * WIDTH + 2 * LOCAL), F32),
            ]
            dr1s[chain], dzs[chain], dqkvs[chain], dx, vec_one[chain] = call(
                body,
                meta,
                operands,
                specs,
                outs,
                qkv_scratch,
                f"attention_back{layer}{chain}",
                att_flops + 4 * span * span * LOCAL,
            )
            dxs[chain] = (dx, swap(dx, "mp"))
        body = functools.partial(attention_grad_kernel, micro)
        if layer == 0:
            x_specs = [
                pl.BlockSpec((1, 1, span, block), lambda i, meta, chain=chain: (chain, meta[0], 0, i))
                for chain in chains
            ]
        else:
            x_specs = [column] * micro
        att_grads[layer] = call(
            body,
            meta,
            dzs + atts[layer] + xs[layer] + dqkvs,
            [column] * micro
            + [whole((span, LOCAL))] * micro
            + x_specs
            + [whole((span, 3 * LOCAL))] * micro,
            [grad_out] * 2,
            [pltpu.VMEM((rows, LOCAL), BF), pltpu.VMEM((rows, 3 * LOCAL), BF)],
            f"attention_grad{layer}",
            8 * rows * WIDTH * HALF,
            WIDTH // block,
            [grad_spec] * 2,
        )
        per_chain = jnp.concatenate(
            [
                jnp.concatenate([one[:, 0:768], two[:, 0:768], one[:, 768:2304], two[:, 768:2304],
                                 one[:, 2304:], two[:, 2304:]], axis=1)
                for one, two in zip(vec_one, vec_two)
            ],
            axis=0,
        )
        own_tags = own_chain(tags)
        by_model = jnp.stack(
            [jnp.sum(jnp.where((own_tags == model)[:, None], per_chain, 0.0), axis=0) for model in range(2)]
        )
        vec_grads[layer] = by_model

    def reduced(keep, send):
        got = swap(send, "section")
        part = keep[1] + got[1]
        half = (keep[0] + got[0]) + swap(part, "rep")
        mine = lax.psum_scatter(half, "dp", scatter_dimension=0, tiled=True)
        other = swap(mine, "rep")
        return jnp.where(rep == 0, jnp.stack([mine, other]), jnp.stack([other, mine]))

    finals = []
    for layer in layers:
        keep_d, send_d, keep_i, send_i = ffn_grads[layer]
        finals.append([reduced(keep_d, send_d), reduced(keep_i, send_i), reduced(*att_grads[layer])])
    owners = []
    for zero, one in zip(*finals):
        mine = jnp.where(section == 0, zero, one)
        other = swap(jnp.where(section == 0, one, zero), "section")
        owners.append(
            jnp.where(section == 0, jnp.stack([mine, other]), jnp.stack([other, mine])).astype(F32)
        )
    down, into, mixed = owners
    shard = down.shape[2]
    grad_out = jnp.swapaxes(down, 2, 3).reshape(2, HIDDEN, shard)
    grad_in = jnp.swapaxes(into, 1, 2).reshape(2, shard, HIDDEN)
    grad_o = jnp.swapaxes(mixed[:, 0, :, 0:LOCAL], 1, 2)
    grad_qkv = jnp.stack(
        [mixed[:, 0, :, LOCAL:], mixed[:, 1, :, 0:LOCAL], mixed[:, 1, :, LOCAL:]], axis=1
    )

    both = jnp.stack(vec_grads)
    both = both + swap(both, "section")
    both = both + swap(both, "rep")
    both = lax.dynamic_index_in_dim(both, section, 0, keepdims=False)
    data = lax.axis_size("dp")
    distance = 1
    while distance < data:
        both = both + lax.ppermute(both, "dp", [(i, i ^ distance) for i in range(data)])
        distance *= 2
    grad_gains = both[:, : SHIFT[0]].reshape(2, 2, WIDTH)
    grad_shifts = both[:, SHIFT[0] : BIAS_Q].reshape(2, 4, WIDTH)
    grad_b_qv = both[:, BIAS_Q:BIAS_IN].reshape(2, 2, LOCAL)
    grad_b_in = both[:, BIAS_IN:]

    def owned(zero, one):
        zero, one = jnp.stack(zero), jnp.stack(one)
        mine = jnp.where(section == 0, zero, one)
        other = swap(jnp.where(section == 0, one, zero), "section")
        return jnp.where(
            section == 0, jnp.stack([mine, other], axis=1), jnp.stack([other, mine], axis=1)
        )[None]

    firsts = [
        ((dx[0].astype(F32) + dx[1].astype(F32)) + dr1).astype(BF) for dx, dr1 in zip(dxs, dr1s)
    ]
    layer_outputs = owned(xs[1], lasts)
    input_grads = owned(firsts, y_grads)
    return (
        layer_outputs,
        input_grads,
        grad_qkv[None],
        grad_o[None],
        grad_in[None],
        grad_out[None],
        grad_b_qv[None],
        grad_b_in[None],
        grad_gains[None],
        grad_shifts[None],
    )


def solution(mesh):
    in_specs = (
        P(None, ("dp", "rep"), None, None),
        P(None, ("dp", "rep"), None, None),
        P(None, ("dp", "rep")),
        P(None, ("dp", "rep")),
        P("section", None, None, None, "mp"),
        P("section", None, "mp", None),
        P("section", None, None, "mp"),
        P("section", None, "mp", None),
        P("section", None, None, "mp"),
        P("section", None, "mp"),
        P("section", None, None, None),
        P("section", None, None, None),
    )
    out_specs = (
        P("section", None, ("dp", "rep"), None, None),
        P("section", None, ("dp", "rep"), None, None),
        P("section", None, None, "dp", "mp"),
        P("section", None, "mp", "dp"),
        P("section", None, "dp", "mp"),
        P("section", None, "mp", "dp"),
        P("section", None, None, "mp"),
        P("section", None, "mp"),
        P("section", None, None, None),
        P("section", None, None, None),
    )
    return jax.shard_map(
        on_device, mesh=mesh, in_specs=in_specs, out_specs=out_specs, check_vma=False
    )
```

```python
import functools

import jax
import jax.numpy as jnp
from jax import lax
from jax.experimental import pallas as pl
from jax.experimental.pallas import tpu as pltpu
from jax.sharding import PartitionSpec as P

HD = 64
EPS = 1e-05
BF = jnp.bfloat16
F32 = jnp.float32

GAIN_ONE, GAIN_TWO = 0, 768
SHIFT = (1536, 2304, 3072, 3840)
BIAS_Q, BIAS_V, BIAS_IN = 4608, 4992, 5376
PACKED = 6912
WIDTH, LOCAL, HIDDEN, HALF = 768, 384, 1536, 768

NN = (((1,), (0,)), ((), ()))
NT = (((1,), (1,)), ((), ()))
TN = (((0,), (0,)), ((), ()))


def mm(left, right, dims=NN):
    return lax.dot_general(left, right, dims, preferred_element_type=F32)


def swap(block, axis):
    return lax.ppermute(block, axis, [(0, 1), (1, 0)])


def after(value, *others):
    return lax.optimization_barrier((value, *others))[0]


class Lazy:
    def __init__(self, source, place, sems, first, parts):
        self.place, self.waited, self.copies = place, set(), []
        extent = place.shape[0] // parts
        for part in range(parts):
            at = pl.ds(part * extent, extent)
            near, away = (place, source) if parts == 1 else (place.at[at], source.at[at])
            self.copies.append(pltpu.make_async_copy(away, near, sems.at[first + part]))

    shape = property(lambda self: self.place.shape)

    def start(self):
        for copy in self.copies:
            copy.start()

    def wait(self, part=None):
        for index in range(len(self.copies)) if part is None else (part,):
            if index not in self.waited:
                self.copies[index].wait()
                self.waited.add(index)

    def __getitem__(self, at):
        self.wait()
        return self.place[at]


class Leaving:
    def __init__(self, place, target, sems, first, pieces):
        self.place, self.started, self.copies = place, set(), []
        for index, at in enumerate(pieces):
            near, away = (place, target) if at is None else (place.at[at], target.at[at])
            self.copies.append(pltpu.make_async_copy(near, away, sems.at[first + index]))

    shape = property(lambda self: self.place.shape)

    def start(self, piece=None):
        for index in range(len(self.copies)) if piece is None else (piece,):
            if index not in self.started:
                self.copies[index].start()
                self.started.add(index)

    def wait(self):
        for copy in self.copies:
            copy.wait()

    def __getitem__(self, at):
        return self.place[at]

    def __setitem__(self, at, value):
        self.place[at] = value
        if at is Ellipsis:
            self.start()


def blocks_of(rows, columns, row_step, column_step):
    return [
        (pl.ds(row, row_step), pl.ds(column, column_step))
        for column in range(0, columns, column_step)
        for row in range(0, rows, row_step)
    ]


class Saved:
    def __init__(self, value, chain=None, parts=1):
        self.value, self.chain, self.parts = value, chain, parts
        self.shape = value.shape if chain is None else value.shape[2:]


class Scalars:
    def __init__(self, lengths, tags, far_tags=None):
        self.section, self.rep = lax.axis_index("section"), lax.axis_index("rep")
        self.lengths, self.tags, self.far_tags = lengths, tags, far_tags

    def length(self, chain):
        return self.lengths[chain, self.section]

    def tag(self, chain):
        return self.tags[chain, self.section]

    def far_tag(self, chain):
        return self.far_tags[chain, self.section]


def layer_norm(resid):
    mean = jnp.mean(resid, -1, keepdims=True)
    centred = resid - mean
    inverse = lax.rsqrt(jnp.mean(centred * centred, -1, keepdims=True) + EPS)
    return centred * inverse, inverse


def layer_norm_back(grad, gain, normed, inverse):
    scaled = grad * gain
    return inverse * (
        scaled
        - jnp.mean(scaled, -1, keepdims=True)
        - normed * jnp.mean(scaled * normed, -1, keepdims=True)
    )


class Weights:
    def __init__(self, own, got, is_own, pieces, place, sems, first=0):
        self.place, self.copies, self.waited = place, {}, set()
        for index, (name, source, target) in enumerate(pieces):
            target = place.at[target] if target is not None else place
            near = pltpu.make_async_copy(own.at[source], target, sems.at[first + index])
            away = pltpu.make_async_copy(got.at[source], target, sems.at[first + index])
            self.copies[name] = near
            pl.when(is_own)(near.start)
            pl.when(jnp.logical_not(is_own))(away.start)

    def __call__(self, name=0):
        self.copies[name].wait()
        return self.place


def in_halves(tag, axis):
    pieces = []
    for half in range(2):
        at = pl.ds(half * HALF, HALF)
        at = (at,) if axis == 0 else (slice(None), at)
        pieces.append((half, (tag, *at), at))
    return pieces


def vec_reader(vecs, is_own, tag):
    own, got = vecs

    def read(at, extent=WIDTH):
        span = slice(at, at + extent) if isinstance(at, int) else pl.ds(at, extent)
        return jnp.where(is_own, own[pl.ds(tag, 1), span], got[pl.ds(tag, 1), span])

    return read


def gelu_and_slope(pre):
    cdf = 0.5 + 0.5 * lax.erf(pre * 0.7071067811865476)
    pdf = jnp.exp(pre * pre * -0.5) * 0.3989422804014327
    return (pre * cdf).astype(BF), (cdf + pre * pdf).astype(BF)


def column_sum(values):
    return jnp.sum(values, axis=0, keepdims=True)


def half_mask(values, which):
    lanes = lax.broadcasted_iota(jnp.int32, values.shape, 1)
    keep = (lanes < HD) if which == 0 else (lanes >= HD)
    return jnp.where(keep, values, jnp.zeros_like(values))


def attend(x, vector, length, wq, out_qkv, out_probs, out_att):
    span = x.shape[0]
    parts = []
    for j in range(3):
        value = mm(x, wq(j)[j])
        if j == 0:
            value = value + vector(BIAS_Q, LOCAL)
        if j == 2:
            value = value + vector(BIAS_V, LOCAL)
        value = value.astype(BF)
        out_qkv[:, j * LOCAL : (j + 1) * LOCAL] = value
        parts.append(value)
    out_qkv.start()
    query, key, value = parts
    keys = lax.broadcasted_iota(jnp.int32, (span, span), 0)
    usable = keys < length
    mixed = []
    for pair in range(LOCAL // 128):
        at = slice(pair * 128, pair * 128 + 128)
        total = None
        for which in range(2):
            scores = mm(half_mask(key[:, at], which), query[:, at], NT) * 0.125
            scores = jnp.where(usable, scores, -1e30)
            raised = jnp.exp(scores - jnp.max(scores, axis=0, keepdims=True))
            probs = (raised * (1.0 / jnp.sum(raised, axis=0, keepdims=True))).astype(BF)
            out_probs[2 * pair + which] = probs
            term = mm(probs, half_mask(value[:, at], which), TN)
            total = term if total is None else total + term
        mixed.append(total.astype(BF))
    out_probs.start()
    att = jnp.concatenate(mixed, axis=1)
    out_att[...] = att
    return att


def attention_kernel(layer, chain, meta, *refs):
    if layer == 0:
        x_ref, *vecs = refs[:3]
        refs = refs[3:]
    else:
        feed_own, feed_got, hidden, *vecs = refs[:5]
        refs = refs[5:]
    own_q, got_q, own_o, got_o, *refs, wq, wo, sems = refs
    if layer == 0:
        out_qkv, out_probs, out_att, out_branch = refs
    else:
        out_x, out_x_saved, out_r2, out_qkv, out_probs, out_att, out_branch = refs
    length, tag = meta.length(chain), meta.tag(chain)
    is_own = meta.section == layer
    vector = vec_reader(vecs, is_own, tag)
    wq = Weights(own_q, got_q, is_own, [(j, (tag, j), j) for j in range(3)], wq, sems)
    wo = Weights(own_o, got_o, is_own, [(0, tag, None)], wo, sems, 3)
    if layer == 0:
        x = x_ref[...]
    else:
        before = vec_reader(vecs, meta.section == 0, tag)
        r2 = hidden[...] + ((feed_own[...].astype(F32) + feed_got[...].astype(F32)) + before(SHIFT[2]))
        out_r2[...] = r2
        normed, _ = layer_norm(r2)
        x = (normed * before(GAIN_TWO) + before(SHIFT[3])).astype(BF)
        out_x[...] = x
        out_x_saved[...] = x
    att = attend(x, vector, length, wq, out_qkv, out_probs, out_att)
    out_branch[...] = mm(att, wo()[...]).astype(BF)


def feed_kernel(layer, chain, meta, x, own, got, *refs):
    *vecs, own_i, got_i, own_d, got_d = refs[:6]
    out_hidden, out_r1, out_slope, out_act, out_low, out_feed, act, wi, wd, sems = refs[6:]
    tag = meta.tag(chain)
    is_own = meta.section == layer
    wi = Weights(own_i, got_i, is_own, in_halves(tag, 1), wi, sems)
    wd = Weights(own_d, got_d, is_own, [(0, tag, None)], wd, sems, 2)
    vector = vec_reader(vecs, is_own, tag)
    branch = (own[...].astype(F32) + got[...].astype(F32)) + vector(SHIFT[0])
    r1 = x[...].astype(F32) + branch
    out_r1[...] = r1
    normed, _ = layer_norm(r1)
    hidden = normed * vector(GAIN_ONE) + vector(SHIFT[1])
    out_hidden[...] = hidden
    low = hidden.astype(BF)
    out_low[...] = low
    for half in range(2):
        at = half * HALF
        pre = mm(low, wi(half)[:, at : at + HALF]) + vector(BIAS_IN + at, HALF)
        act[:, at : at + HALF], out_slope[:, at : at + HALF] = gelu_and_slope(pre)

        @pl.when(meta.rep == half)
        def _():
            out_act[:, :] = act[:, at : at + HALF]

    out_act.start()
    out_slope.start()
    out_feed[...] = mm(act[...], wd()[...]).astype(BF)


def feed_back_kernel(layer, chain, meta, own, got, *refs):
    first, second, *vecs, act_slope, own_i, got_i, own_d, got_d = refs[:9]
    out_y, out_dr2, out_df, out_du, out_dh, out_vec, du_all, wi, wd, sems = refs[9:]
    length, tag = meta.length(chain), meta.tag(chain)
    is_own = meta.section == layer
    wd = Weights(own_d, got_d, is_own, in_halves(tag, 0), wd, sems)
    wi = Weights(own_i, got_i, is_own, [(0, tag, None)], wi, sems, 2)
    vector = vec_reader(vecs, is_own, tag)
    gain = vector(GAIN_TWO)
    both = own[...].astype(F32) + got[...].astype(F32)
    if layer == 1:
        hidden, cotangent = first, second
        normed, inverse = layer_norm(hidden[...] + (both + vector(SHIFT[2])))
        out_y[...] = (normed * gain + vector(SHIFT[3])).astype(BF)
        tokens = lax.broadcasted_iota(jnp.int32, both.shape, 0)
        dy = jnp.where(tokens < length, cotangent[...].astype(F32), 0.0)
    else:
        dr1, r2 = first, second
        low = (both + dr1[...]).astype(BF)
        out_y[...] = low
        dy = low.astype(F32)
        normed, inverse = layer_norm(r2[...])
    dr2 = layer_norm_back(dy, gain, normed, inverse)
    out_dr2[...] = dr2
    df = dr2.astype(BF)
    out_df[...] = df
    out_vec[:, 0:768] = column_sum(dy * normed)
    out_vec[:, 768:1536] = column_sum(dr2)
    out_vec[:, 1536:2304] = column_sum(dy)
    for half in range(2):
        at = half * HALF
        du = mm(df, wd(half)[at : at + HALF, :], NT) * act_slope[:, at : at + HALF].astype(F32)
        out_vec[:, 2304 + at : 2304 + at + HALF] = column_sum(du)
        du_all[:, at : at + HALF] = du.astype(BF)

        @pl.when(meta.rep == half)
        def _():
            out_du[:, :] = du_all[:, at : at + HALF]

    out_du.start()
    out_dh[...] = mm(du_all[...], wi()[...], NT).astype(BF)


def attention_back_kernel(layer, chain, meta, own, got, dr2, r1, *refs):
    *vecs, qkv, probs_ref, own_q, got_q, own_o, got_o = refs[:8]
    out_dr1, out_dz, out_dqkv, out_dx, out_vec, wq, wo, sems = refs[8:]
    tag = meta.tag(chain)
    is_own = meta.section == layer
    wo = Weights(own_o, got_o, is_own, [(0, tag, None)], wo, sems, 3)
    wq = Weights(own_q, got_q, is_own, [(j, (tag, j), j) for j in range(3)], wq, sems)
    vector = vec_reader(vecs, is_own, tag)
    dh = (own[...].astype(F32) + got[...].astype(F32)) + dr2[...]
    normed, inverse = layer_norm(r1[...])
    dr1 = layer_norm_back(dh, vector(GAIN_ONE), normed, inverse)
    out_dr1[...] = dr1
    dz = dr1.astype(BF)
    out_dz[...] = dz
    out_vec[:, 0:768] = column_sum(dh * normed)
    out_vec[:, 768:1536] = column_sum(dr1)
    out_vec[:, 1536:2304] = column_sum(dh)
    datt = mm(dz, wo()[...], NT).astype(BF)
    query, key, value = (qkv[:, j * LOCAL : (j + 1) * LOCAL] for j in range(3))
    for pair in range(LOCAL // 128):
        at = slice(pair * 128, pair * 128 + 128)
        dv = dq = dk = None
        for which in range(2):
            probs = probs_ref[2 * pair + which]
            dv_term = mm(probs, half_mask(datt[:, at], which))
            dprobs = mm(half_mask(value[:, at], which), datt[:, at], NT)
            wide = probs.astype(F32)
            dscores = wide * (dprobs - jnp.sum(wide * dprobs, axis=0, keepdims=True))
            dscores = dscores.astype(BF)
            dk_term = mm(dscores, half_mask(query[:, at], which))
            dq_term = mm(dscores, half_mask(key[:, at], which), TN)
            dv = dv_term if dv is None else dv + dv_term
            dk = dk_term if dk is None else dk + dk_term
            dq = dq_term if dq is None else dq + dq_term
        dq = dq * 0.125
        dk = dk * 0.125
        low = pair * 128
        out_vec[:, 2304 + low : 2304 + low + 128] = column_sum(dq)
        out_vec[:, 2688 + low : 2688 + low + 128] = column_sum(dv)
        out_dqkv[:, low : low + 128] = dq.astype(BF)
        out_dqkv[:, LOCAL + low : LOCAL + low + 128] = dk.astype(BF)
        out_dqkv[:, 2 * LOCAL + low : 2 * LOCAL + low + 128] = dv.astype(BF)
    out_dqkv.start()
    dx = None
    for j in range(3):
        term = mm(out_dqkv[:, j * LOCAL : (j + 1) * LOCAL], wq(j)[j], NT)
        dx = term if dx is None else dx + term
    out_dx[...] = dx.astype(BF)


def token_tags(meta, chains, span, far=False):
    tags = [meta.tag(chain) for chain in range(chains)]
    if far:
        tags += [meta.far_tag(chain) for chain in range(chains)]
    where = lax.broadcasted_iota(jnp.int32, (1, len(tags) * span), 1)
    result = jnp.full((1, len(tags) * span), tags[0], jnp.int32)
    for index, tag in enumerate(tags[1:], 1):
        result = jnp.where(where >= index * span, tag, result)
    return result


def far_kernel(layer, chains, meta, *refs):
    low = refs[:chains]
    *vecs, own_i, got_i, out_act, out_slope, wi, sems = refs[chains:]
    span = low[0].shape[0]
    is_own = meta.section == layer
    half = pl.ds(pl.multiple_of(meta.rep * HALF, HALF), HALF)
    wi = Weights(own_i, got_i, is_own, [(0, (slice(None), slice(None), half), None)], wi, sems)()
    for chain in range(chains):
        tag = meta.far_tag(chain)
        at = slice(chain * span, (chain + 1) * span)
        bias = vec_reader(vecs, is_own, tag)(pl.multiple_of(BIAS_IN + meta.rep * HALF, HALF), HALF)
        pre = mm(low[chain][...], wi[tag]) + bias
        out_act[at, :], out_slope[at, :] = gelu_and_slope(pre)


class Gathered:
    def __init__(self, sources, place, sems, first):
        self.place, self.copies, row = place, [], 0
        for index, source in enumerate(sources):
            extent = source.shape[0]
            at = place.at[pl.ds(row, extent)]
            copy = pltpu.make_async_copy(source, at, sems.at[first + index])
            copy.start()
            self.copies.append(copy)
            row += extent

    def wait(self):
        for copy in self.copies:
            copy.wait()
        return self.place


def feed_grad_kernel(layer, chains, meta, *refs):
    df, act, low, du, far_df, far_low = (refs[i * chains : (i + 1) * chains] for i in range(6))
    far_act, far_slope, own_d, got_d, keep, send, df_all, act_all, low_all, du_all, wd, sems = refs[6 * chains :]
    span = df[0].shape[0]
    rows = chains * span
    half = pl.ds(pl.multiple_of(meta.rep * HALF, HALF), HALF)
    is_own = meta.section == layer
    wd = Weights(own_d, got_d, is_own, [(0, (slice(None), half), None)], wd, sems, 8 * chains)
    df_all = Gathered([*df, *far_df], df_all, sems, 0)
    act_all = Gathered([*act, far_act], act_all, sems, 2 * chains)
    du_all = Gathered(du, du_all, sems, 4 * chains)
    low_all = Gathered([*low, *far_low], low_all, sems, 6 * chains)
    tags = token_tags(meta, chains, span, True)
    mine = tags == meta.section
    theirs = jnp.logical_not(mine)

    def products(left_all, at, right):
        for column in range(0, WIDTH, BLOCK):
            left = left_all[:, column : column + BLOCK].T
            for mask, out in ((theirs, send), (mine, keep)):
                value = mm(jnp.where(mask, left, jnp.zeros_like(left)), right[...])
                out[column : column + BLOCK, at : at + HALF] = value.astype(BF)
            keep.start((at // HALF) * (WIDTH // BLOCK) + column // BLOCK)

    lefts = df_all.wait()
    products(lefts, 0, act_all.wait())
    rights = du_all.wait()
    weights = wd()
    for chain in range(chains):
        at = slice(chain * span, (chain + 1) * span)
        below = slice(rows + chain * span, rows + (chain + 1) * span)
        tag = meta.far_tag(chain)
        value = mm(lefts[below, :], weights[tag], NT) * far_slope[at, :].astype(F32)
        rights[below, :] = value.astype(BF)
    products(low_all.wait(), HALF, rights)


def attention_grad_kernel(layer, chains, meta, *refs):
    dz, att, x, dqkv = (refs[i * chains : (i + 1) * chains] for i in range(4))
    keep, send, dz_all, att_all, x_all, dqkv_all, sems = refs[4 * chains :]
    span = dz[0].shape[0]
    if layer == 0:
        x = [ref.at[chain, meta.section] for chain, ref in enumerate(x)]
    dz_all = Gathered(dz, dz_all, sems, 0)
    att_all = Gathered(att, att_all, sems, chains)
    x_all = Gathered(x, x_all, sems, 2 * chains)
    dqkv_all = Gathered(dqkv, dqkv_all, sems, 3 * chains)
    mine = token_tags(meta, chains, span) == meta.section
    theirs = jnp.logical_not(mine)
    first = jnp.where(meta.rep == 0, 0, 1)
    left_all, right = dz_all.wait(), att_all.wait()
    for column in range(0, WIDTH, BLOCK):
        block = slice(column, column + BLOCK)
        left = left_all[:, block].T
        for mask, out in ((theirs, send), (mine, keep)):
            value = mm(jnp.where(mask, left, jnp.zeros_like(left)), right[...])
            out[first, block, 0:LOCAL] = value.astype(BF)
    left_all, right = x_all.wait(), dqkv_all.wait()
    for column in range(0, WIDTH, BLOCK):
        block = slice(column, column + BLOCK)
        left = left_all[:, block].T
        for mask, out in ((theirs, send), (mine, keep)):
            masked = jnp.where(mask, left, jnp.zeros_like(left))
            out[first, block, LOCAL:HALF] = mm(masked, right[:, 0:LOCAL]).astype(BF)
            out[1 - first, block, :] = mm(masked, right[:, LOCAL : 3 * LOCAL]).astype(BF)


def add_kernel(parts, meta, one, two, out):
    block = one.shape[0] // parts
    for part in range(parts):
        at = slice(part * block, (part + 1) * block)
        one.wait(part)
        two.wait(part)
        out[at, :] = one.place[at, :] + two.place[at, :]
        out.start(part)


def add_halves_kernel(meta, one, two, near, far):
    for half, out in ((1, far), (0, near)):
        one.wait(half)
        two.wait(half)
        out[...] = one.place[half] + two.place[half]


BLOCK = 256
ANY = pl.BlockSpec(memory_space=pl.ANY)


def pack_kernel(gains, shifts, b_qv, b_in, out):
    for model in range(2):
        row = slice(model, model + 1)
        for j in range(2):
            out[row, j * WIDTH : (j + 1) * WIDTH] = gains[0, model, j : j + 1, :]
            out[row, BIAS_Q + j * LOCAL : BIAS_Q + (j + 1) * LOCAL] = b_qv[0, model, j : j + 1, :]
        for j in range(4):
            out[row, SHIFT[j] : SHIFT[j] + WIDTH] = shifts[0, model, j : j + 1, :]
        out[row, BIAS_IN:] = b_in[0, row, :]


def feed_final_kernel(meta, *refs):
    zero, one, got, grad_in, grad_out = refs[:2], refs[2:4], refs[4], refs[5], refs[6]
    for half in range(2):
        local = jnp.where(meta.rep == 0, half, 1 - half)
        mine = jnp.where(meta.section == 0, zero[half][...], one[half][...]).astype(F32)
        columns = pl.ds(pl.multiple_of(local * HALF, HALF), HALF)
        for model, shard in ((meta.section, mine), (1 - meta.section, got[half].astype(F32))):
            grad_out[model, :, columns] = shard[:, 0:HALF]
            grad_in[model, :, columns] = shard[:, HALF:]


def attention_final_kernel(meta, *refs):
    zero, one, got, grad_qkv, grad_o = refs[:2], refs[2:4], refs[4], refs[5], refs[6]
    mine = [jnp.where(meta.section == 0, zero[half][...], one[half][...]).astype(F32) for half in range(2)]
    for model, near, far in (
        (meta.section, *mine),
        (1 - meta.section, got[0].astype(F32), got[1].astype(F32)),
    ):
        low = jnp.where(meta.rep == 0, near, far)
        high = jnp.where(meta.rep == 0, far, near)
        grad_o[model] = low[:, 0:LOCAL]
        grad_qkv[model, 0] = low[:, LOCAL:]
        grad_qkv[model, 1] = high[:, 0:LOCAL]
        grad_qkv[model, 2] = high[:, LOCAL:]


def vector_grad_kernel(chains, meta, *refs):
    out = refs[-1]
    for layer in range(2):
        ones = refs[2 * layer * chains : (2 * layer + 1) * chains]
        twos = refs[(2 * layer + 1) * chains : (2 * layer + 2) * chains]
        rows = [
            jnp.concatenate(
                [one[:, 0:768], two[:, 0:768], one[:, 768:2304], two[:, 768:2304], one[:, 2304:], two[:, 2304:]],
                axis=1,
            )
            for one, two in zip(ones, twos)
        ]
        for model in range(2):
            total = None
            for chain in range(chains):
                row = jnp.where(meta.tag(chain) == model, rows[chain], 0.0)
                total = row if total is None else total + row
            out[layer, model : model + 1, :] = total


STEP = 1.5e9
LONG = 8

VMEM = pl.BlockSpec(memory_space=pltpu.VMEM)
SMEM = pl.BlockSpec(memory_space=pltpu.SMEM)
SAVED = "saved"


def pieces_of(out):
    return out[3] if len(out) > 3 else [None]


def in_hbm(value):
    return pltpu.with_memory_space_constraint(value, pltpu.HBM)


def call(body, scalars, operands, outs, scratch, name, grant, cost):
    saved_in = [value for value in operands if isinstance(value, Saved)]
    saved_out = [out for out in outs if SAVED in out]
    buffers = [pltpu.VMEM(value.shape, value.value.dtype) for value in saved_in]
    buffers += [pltpu.VMEM(out[0], out[1]) for out in saved_out]
    counts = (len(scalars), len(operands), len(outs), len(scratch))

    def kernel(*refs):
        groups = []
        for count in counts:
            groups.append(refs[:count])
            refs = refs[count:]
        numbers, ins, results, own_scratch = groups
        *places, sems = refs
        meta = Scalars(*numbers)
        given, taken, index, sem = [], [], 0, 0
        for value, ref in zip(operands, ins):
            if isinstance(value, Saved):
                source = ref if value.chain is None else ref.at[value.chain, meta.section]
                ref = Lazy(source, places[index], sems, sem, value.parts)
                ref.start()
                sem += value.parts
                index += 1
            given.append(ref)
        for out, ref in zip(outs, results):
            if SAVED in out:
                ref = Leaving(places[index], ref, sems, sem, pieces_of(out))
                sem += len(pieces_of(out))
                index += 1
            taken.append(ref)
        body(meta, *given, *taken, *own_scratch)
        for ref in taken:
            if isinstance(ref, Leaving):
                ref.start()
        for ref in given:
            if isinstance(ref, Lazy):
                ref.wait()
        for ref in taken:
            if isinstance(ref, Leaving):
                ref.wait()

    in_specs = [ANY if isinstance(value, (tuple, Saved)) else VMEM for value in operands]
    values = []
    for value in operands:
        if isinstance(value, Saved):
            value = in_hbm(value.value)
        elif isinstance(value, tuple):
            value = in_hbm(value[0])
        values.append(value)
    shapes = [
        pltpu.HBM(out[0], out[1]) if SAVED in out else jax.ShapeDtypeStruct(out[0], out[1]) for out in outs
    ]
    return pl.pallas_call(
        kernel,
        out_shape=shapes,
        in_specs=[SMEM] * len(scalars) + in_specs,
        out_specs=[ANY if SAVED in out else VMEM for out in outs],
        scratch_shapes=[*scratch, *buffers, pltpu.SemaphoreType.DMA((max(sum(value.parts for value in saved_in) + sum(len(pieces_of(out)) for out in saved_out), 1),))],
        compiler_params=pltpu.CompilerParams(vmem_limit_bytes=grant * 1024 * 1024),
        cost_estimate=pl.CostEstimate(flops=int(cost * STEP), bytes_accessed=1, transcendentals=0),
        name=name,
    )(*scalars, *values)


def on_device(
    block_input, cotangent, lengths, tags, w_qkv, w_o, w_in, w_out, b_qv, b_in, gains, shifts
):
    micro, per, span, width = block_input.shape
    section = lax.axis_index("section")
    rep = lax.axis_index("rep")
    chains = range(micro)
    layers = range(2)

    own_q, own_o, own_i, own_d = w_qkv[0], w_o[0], w_in[0], w_out[0]
    got_q = swap(own_q, "section")
    vec_own = pl.pallas_call(
        pack_kernel, out_shape=jax.ShapeDtypeStruct((2, PACKED), F32), in_specs=[VMEM] * 4, out_specs=VMEM, name="pack"
    )(gains, shifts, b_qv, b_in)
    vecs = [vec_own, swap(vec_own, "section")]
    got_o = swap(own_o, "section")
    later = lax.optimization_barrier((own_i, own_d, got_q, got_o, vecs[1]))
    got_i, got_d = swap(later[0], "section"), swap(later[1], "section")
    far_tags = swap(tags, "rep")

    heads = LOCAL // HD
    row, saved_row = ((span, WIDTH), BF), ((span, WIDTH), BF, SAVED)
    wide, saved_wide = ((span, WIDTH), F32), ((span, WIDTH), F32, SAVED)
    half_row, long_row = ((span, HALF), BF, SAVED), ((span, HIDDEN), BF, SAVED)
    qkv_row = ((span, 3 * LOCAL), BF, SAVED)
    att_outs = [qkv_row, ((heads, span, span), BF, SAVED), ((span, LOCAL), BF, SAVED), row]
    raw = lambda values: [(value,) for value in values]
    w_qo, w_id = raw([own_q, got_q, own_o, got_o]), raw([own_i, got_i, own_d, got_d])
    qo_scratch = [
        pltpu.VMEM((3, WIDTH, LOCAL), BF),
        pltpu.VMEM((LOCAL, WIDTH), BF),
        pltpu.SemaphoreType.DMA((4,)),
    ]
    id_scratch = [
        pltpu.VMEM((span, HIDDEN), BF),
        pltpu.VMEM((WIDTH, HIDDEN), BF),
        pltpu.VMEM((HIDDEN, WIDTH), BF),
        pltpu.SemaphoreType.DMA((3,)),
    ]

    last = [tags]

    def run(body, operands, outs, scratch, name, *waits, far=False, grant=14, cost=1):
        scalars = [lengths, after(tags, last[0], *waits)] + ([far_tags] if far else [])
        results = call(body, scalars, operands, outs, scratch, name, grant, cost)
        last[0] = results[-1]
        return results

    def saved(values):
        return [Saved(value) for value in values]

    def arrived(pair):
        return [pair[0], Saved(pair[1])]

    def owned(zero, one):
        zero, one = jnp.stack(zero), jnp.stack(one)
        mine = jnp.where(section == 0, zero, one)
        other = swap(jnp.where(section == 0, one, zero), "section")
        return jnp.where(
            section == 0, jnp.stack([mine, other], axis=1), jnp.stack([other, mine], axis=1)
        )[None]

    table = lambda: [[None] * micro for _ in layers]
    r1s, r2s, hiddens, acts, slopes, lows, far_lows, feeds, qkvs, probs, atts = (table() for _ in range(11))
    x_now, x_saved = [[Saved(block_input, chain) for chain in chains], [None] * micro], [None] * micro
    for layer in layers:
        for chain in chains:
            body = functools.partial(attention_kernel, layer, chain)
            name = f"attention{layer}{chain}"
            if layer == 0:
                waits = [far_tags] if chain == 1 else []
                got = run(body, [x_now[0][chain], *vecs] + w_qo, att_outs, qo_scratch, name, *waits)
            else:
                operands = [*arrived(feeds[0][chain]), hiddens[0][chain], *vecs] + w_qo
                waits = far_lows[0][:chain]
                x_now[1][chain], x_saved[chain], r2s[0][chain], *got = run(
                    body, operands, [row, saved_row, saved_wide] + att_outs, qo_scratch, name, *waits
                )
            qkvs[layer][chain], probs[layer][chain], atts[layer][chain], branch = got
            feeds[layer][chain] = (branch, swap(branch, "mp"))
        for chain in chains:
            body = functools.partial(feed_kernel, layer, chain)
            waits = far_lows[0][2:] if layer == 1 and chain == 0 else []
            hiddens[layer][chain], r1s[layer][chain], slopes[layer][chain], acts[layer][chain], low, part = run(
                body,
                [x_now[layer][chain], *feeds[layer][chain], *vecs] + w_id,
                [wide, saved_wide, long_row, half_row, saved_row, row],
                id_scratch,
                f"feed{layer}{chain}",
                *waits,
            )
            lows[layer][chain], far_lows[layer][chain] = low, swap(low, "rep") if layer == 0 else None
            feeds[layer][chain] = (part, swap(part, "mp"))
    far_lows[1] = [swap(after(low, part), "rep") for low in lows[1]]

    rows = micro * span
    far_rows = ((rows, HALF), BF, SAVED)
    dr2s, dfs, far_dfs, dus, dhs, vec_one, vec_two, dzs, dqkvs, dr1s, dxs, ys = (table() for _ in range(12))
    far_hidden = [None, None]

    def feed_back(layer, chain, *waits, cost=1):
        if layer == 1:
            operands = [*arrived(feeds[1][chain]), hiddens[1][chain], Saved(cotangent, chain)]
        else:
            operands = [*arrived(dxs[1][chain]), Saved(dr1s[1][chain]), Saved(r2s[0][chain])]
        ys[layer][chain], dr2s[layer][chain], df, dus[layer][chain], dh, vec_two[layer][chain] = run(
            functools.partial(feed_back_kernel, layer, chain),
            operands + [*vecs, Saved(slopes[layer][chain])] + w_id,
            [saved_row, saved_wide, saved_row, half_row, row, ((1, 3 * WIDTH + HIDDEN), F32, SAVED)],
            id_scratch,
            f"feed_back{layer}{chain}",
            *waits,
            cost=cost,
        )
        dfs[layer][chain], far_dfs[layer][chain] = df, swap(df, "rep")
        dhs[layer][chain] = (dh, swap(dh, "mp"))

    def attention_back(layer, chain, *waits, cost=1):
        dr1s[layer][chain], dzs[layer][chain], dqkvs[layer][chain], dx, vec_one[layer][chain] = run(
            functools.partial(attention_back_kernel, layer, chain),
            [*arrived(dhs[layer][chain]), Saved(dr2s[layer][chain]), Saved(r1s[layer][chain]), *vecs]
            + [Saved(qkvs[layer][chain]), Saved(probs[layer][chain])]
            + w_qo,
            [saved_wide, saved_row, qkv_row, row, ((1, 3 * WIDTH + 2 * LOCAL), F32, SAVED)],
            qo_scratch,
            f"attention_back{layer}{chain}",
            *waits,
            cost=cost,
        )
        dxs[layer][chain] = (dx, swap(dx, "mp"))

    def far_part(layer, *waits):
        far_hidden[layer] = run(
            functools.partial(far_kernel, layer, micro),
            saved(far_lows[layer]) + [*vecs] + w_id[:2],
            [far_rows] * 2,
            [pltpu.VMEM((2, WIDTH, HALF), BF), pltpu.SemaphoreType.DMA((1,))],
            f"far{layer}",
            *waits,
            far=True,
            cost=1.5,
        )

    def feed_grad(layer, *waits):
        near = dfs[layer] + acts[layer] + lows[layer] + dus[layer]
        far_act, far_slope = far_hidden[layer]
        stacked = pltpu.VMEM((2 * rows, HALF), BF)
        keep, send = run(
            functools.partial(feed_grad_kernel, layer, micro),
            raw(near + far_dfs[layer] + far_lows[layer] + [far_act]) + [Saved(far_slope)] + w_id[2:],
            [((WIDTH, HIDDEN), BF, SAVED, blocks_of(WIDTH, HIDDEN, BLOCK, HALF)), ((WIDTH, HIDDEN), BF)],
            [stacked] * 4 + [pltpu.VMEM((2, HALF, WIDTH), BF), pltpu.SemaphoreType.DMA((8 * micro + 1,))],
            f"feed_grad{layer}",
            *waits,
            far=True,
            grant=20,
            cost=2,
        )
        return keep, swap(send, "section")

    def feed_grad_sum(layer, parts, *waits):
        (result,) = run(
            functools.partial(add_kernel, WIDTH // BLOCK),
            [Saved(part, parts=WIDTH // BLOCK) for part in parts],
            [((WIDTH, HIDDEN), BF, SAVED, blocks_of(WIDTH, HIDDEN, BLOCK, HIDDEN))],
            [],
            f"feed_grad_sum{layer}",
            *waits,
        )
        return result

    def attention_grad(layer, *waits):
        x_part = raw([block_input] * micro if layer == 0 else x_saved)
        narrow, stacked = pltpu.VMEM((rows, LOCAL), BF), pltpu.VMEM((rows, WIDTH), BF)
        keep, send = run(
            functools.partial(attention_grad_kernel, layer, micro),
            raw(dzs[layer] + atts[layer]) + x_part + raw(dqkvs[layer]),
            [((2, WIDTH, HALF), BF, SAVED, [pl.ds(0, 1), pl.ds(1, 1)]), ((2, WIDTH, HALF), BF)],
            [stacked, narrow, stacked, pltpu.VMEM((rows, 3 * LOCAL), BF), pltpu.SemaphoreType.DMA((4 * micro,))],
            f"attention_grad{layer}",
            *waits,
            cost=2,
        )
        return keep, swap(send, "section")

    def attention_grad_sum(layer, parts, *waits):
        near, far = run(
            add_halves_kernel,
            [Saved(part, parts=2) for part in parts],
            [((WIDTH, HALF), BF, SAVED)] * 2,
            [],
            f"attention_grad_sum{layer}",
            *waits,
        )
        return near, swap(far, "rep")

    def scattered(part):
        return lax.psum_scatter(part, "dp", scatter_dimension=0, tiled=True)

    feed_back(1, 0)
    feed_back(1, 1)
    feed_back(1, 2)
    far_part(1, dhs[1][0][1], far_dfs[1][0])
    parts = feed_grad(1, dhs[1][1][1], far_dfs[1][1])
    attention_back(1, 0, dhs[1][2][1], cost=20)
    feed_one = scattered(feed_grad_sum(1, parts))
    attention_back(1, 1)
    attention_back(1, 2, dxs[1][0][1])
    parts = attention_grad(1, dxs[1][1][1])
    near, far = attention_grad_sum(1, parts)
    feed_back(0, 0)
    feed_back(0, 1, dxs[1][2][1])
    feed_back(0, 2, dhs[0][0][1])
    far_part(0, dhs[0][1][1])
    attention_one = after(near, last[0]) + far
    attention_back(0, 0, attention_one)
    attention_one = scattered(after(attention_one, feed_one))
    parts = feed_grad(0, dhs[0][2][1])
    feed_one = (feed_one, swap(feed_one, "rep"))
    attention_back(0, 1, attention_one, cost=LONG)
    feed_zero = feed_grad_sum(0, parts, feed_one[1])
    feed_zero = scattered(after(feed_zero, attention_one))
    attention_back(0, 2)
    (both,) = run(
        functools.partial(vector_grad_kernel, micro),
        saved(vec_one[0] + vec_two[0] + vec_one[1] + vec_two[1]),
        [((2, 2, PACKED), F32)],
        [],
        "vector_grad",
    )
    attention_one = (attention_one, swap(attention_one, "rep"))
    parts = attention_grad(0)
    both = both + swap(both, "section")
    both = lax.dynamic_index_in_dim(both, section, 0, keepdims=False)
    both = both + swap(both, "rep")
    near, far = attention_grad_sum(0, parts, attention_one[1], both)
    data = lax.axis_size("dp")
    distance = 1
    while distance < data:
        both = both + lax.ppermute(both, "dp", [(i, i ^ distance) for i in range(data)])
        distance *= 2
    grad_gains = both[:, : SHIFT[0]].reshape(2, 2, WIDTH)
    grad_shifts = both[:, SHIFT[0] : BIAS_Q].reshape(2, 4, WIDTH)
    grad_b_qv = both[:, BIAS_Q:BIAS_IN].reshape(2, 2, LOCAL)
    grad_b_in = both[:, BIAS_IN:]
    layer_outputs = owned(after(x_saved, near), ys[1])
    firsts = [
        ((after(dx[0], near).astype(F32) + dx[1].astype(F32)) + dr1).astype(BF) for dx, dr1 in zip(dxs[0], dr1s[0])
    ]
    attention_zero = after(after(near, layer_outputs, firsts) + far, feed_zero)
    done = attention_zero
    feed_zero = (feed_zero, swap(after(feed_zero, done), "rep"))
    attention_zero = scattered(attention_zero)

    def handed(zero, one):
        return swap(jnp.where(section == 0, jnp.stack(one), jnp.stack(zero)), "section")

    shard = feed_zero[0].shape[0]
    grad_in, grad_out = run(
        feed_final_kernel,
        [*feed_zero, *feed_one, handed(feed_zero, feed_one)],
        [((2, shard, HIDDEN), F32)] * 2,
        [],
        "feed_final",
    )
    input_grads = owned(after(firsts, done), ys[0])
    attention_zero = after(attention_zero, grad_in, input_grads, both)
    attention_zero = (attention_zero, swap(attention_zero, "rep"))
    grad_qkv, grad_o = run(
        attention_final_kernel,
        [*attention_zero, *attention_one, handed(attention_zero, attention_one)],
        [((2, 3, shard, LOCAL), F32), ((2, shard, LOCAL), F32)],
        [],
        "attention_final",
    )
    grad_out, grad_o = jnp.swapaxes(grad_out, 1, 2), jnp.swapaxes(grad_o, 1, 2)

    return (
        layer_outputs,
        input_grads,
        grad_qkv[None],
        grad_o[None],
        grad_in[None],
        grad_out[None],
        grad_b_qv[None],
        grad_b_in[None],
        grad_gains[None],
        grad_shifts[None],
    )


def solution(mesh):
    in_specs = (
        P(None, ("dp", "rep"), None, None),
        P(None, ("dp", "rep"), None, None),
        P(None, ("dp", "rep")),
        P(None, ("dp", "rep")),
        P("section", None, None, None, "mp"),
        P("section", None, "mp", None),
        P("section", None, None, "mp"),
        P("section", None, "mp", None),
        P("section", None, None, "mp"),
        P("section", None, "mp"),
        P("section", None, None, None),
        P("section", None, None, None),
    )
    out_specs = (
        P("section", None, ("dp", "rep"), None, None),
        P("section", None, ("dp", "rep"), None, None),
        P("section", None, None, "dp", "mp"),
        P("section", None, "mp", "dp"),
        P("section", None, "dp", "mp"),
        P("section", None, "mp", "dp"),
        P("section", None, None, "mp"),
        P("section", None, "mp"),
        P("section", None, None, None),
        P("section", None, None, None),
    )
    return jax.shard_map(
        on_device, mesh=mesh, in_specs=in_specs, out_specs=out_specs, check_vma=False
    )
```

```python
import functools

import jax
import jax.numpy as jnp
from jax import lax
from jax.experimental import pallas as pl
from jax.experimental.pallas import tpu as pltpu
from jax.sharding import PartitionSpec as P

HD = 64
EPS = 1e-05
BF = jnp.bfloat16
F32 = jnp.float32

GAIN_ONE, GAIN_TWO = 0, 768
SHIFT = (1536, 2304, 3072, 3840)
BIAS_Q, BIAS_V, BIAS_IN = 4608, 4992, 5376
PACKED = 6912
WIDTH, LOCAL, HIDDEN, HALF = 768, 384, 1536, 768

NN = (((1,), (0,)), ((), ()))
NT = (((1,), (1,)), ((), ()))
TN = (((0,), (0,)), ((), ()))


def mm(left, right, dims=NN):
    return lax.dot_general(left, right, dims, preferred_element_type=F32)


def swap(block, axis):
    return lax.ppermute(block, axis, [(0, 1), (1, 0)])


def after(value, *others):
    return lax.optimization_barrier((value, *others))[0]


class Lazy:
    def __init__(self, source, place, sems, first, parts):
        self.place, self.waited, self.copies = place, set(), []
        extent = place.shape[0] // parts
        for part in range(parts):
            at = pl.ds(part * extent, extent)
            near, away = (place, source) if parts == 1 else (place.at[at], source.at[at])
            self.copies.append(pltpu.make_async_copy(away, near, sems.at[first + part]))

    shape = property(lambda self: self.place.shape)

    def start(self):
        for copy in self.copies:
            copy.start()

    def wait(self, part=None):
        for index in range(len(self.copies)) if part is None else (part,):
            if index not in self.waited:
                self.copies[index].wait()
                self.waited.add(index)

    def __getitem__(self, at):
        self.wait()
        return self.place[at]


class Leaving:
    def __init__(self, place, target, sems, first, pieces):
        self.place, self.started, self.copies = place, set(), []
        for index, at in enumerate(pieces):
            near, away = (place, target) if at is None else (place.at[at], target.at[at])
            self.copies.append(pltpu.make_async_copy(near, away, sems.at[first + index]))

    shape = property(lambda self: self.place.shape)

    def start(self, piece=None):
        for index in range(len(self.copies)) if piece is None else (piece,):
            if index not in self.started:
                self.copies[index].start()
                self.started.add(index)

    def wait(self):
        for copy in self.copies:
            copy.wait()

    def __getitem__(self, at):
        return self.place[at]

    def __setitem__(self, at, value):
        self.place[at] = value
        if at is Ellipsis:
            self.start()


def blocks_of(rows, columns, row_step, column_step):
    return [
        (pl.ds(row, row_step), pl.ds(column, column_step))
        for column in range(0, columns, column_step)
        for row in range(0, rows, row_step)
    ]


class Saved:
    def __init__(self, value, chain=None, parts=1):
        self.value, self.chain, self.parts = value, chain, parts
        self.shape = value.shape if chain is None else value.shape[2:]


class Scalars:
    def __init__(self, numbers, far_tags=None):
        self.section, self.rep = lax.axis_index("section"), lax.axis_index("rep")
        self.numbers, self.far_tags = numbers, far_tags

    def length(self, chain):
        return self.numbers[chain, self.section]

    def tag(self, chain):
        return self.numbers[chain, 2 + self.section]

    def far_tag(self, chain):
        return self.far_tags[chain, self.section]


def layer_norm(resid):
    mean = jnp.mean(resid, -1, keepdims=True)
    centred = resid - mean
    inverse = lax.rsqrt(jnp.mean(centred * centred, -1, keepdims=True) + EPS)
    return centred * inverse, inverse


def layer_norm_back(grad, gain, normed, inverse):
    scaled = grad * gain
    return inverse * (
        scaled
        - jnp.mean(scaled, -1, keepdims=True)
        - normed * jnp.mean(scaled * normed, -1, keepdims=True)
    )


class Weights:
    def __init__(self, own, got, is_own, pieces, place, sems, first=0):
        self.place, self.copies, self.waited = place, {}, set()
        for index, (name, source, target) in enumerate(pieces):
            target = place.at[target] if target is not None else place
            near = pltpu.make_async_copy(own.at[source], target, sems.at[first + index])
            away = pltpu.make_async_copy(got.at[source], target, sems.at[first + index])
            self.copies[name] = near
            pl.when(is_own)(near.start)
            pl.when(jnp.logical_not(is_own))(away.start)

    def __call__(self, name=0):
        self.copies[name].wait()
        return self.place


def in_halves(tag, axis):
    pieces = []
    for half in range(2):
        at = pl.ds(half * HALF, HALF)
        at = (at,) if axis == 0 else (slice(None), at)
        pieces.append((half, (tag, *at), at))
    return pieces


def vec_reader(vecs, is_own, tag):
    own, got = vecs

    def read(at, extent=WIDTH):
        span = slice(at, at + extent) if isinstance(at, int) else pl.ds(at, extent)
        return jnp.where(is_own, own[pl.ds(tag, 1), span], got[pl.ds(tag, 1), span])

    return read


def gelu_and_slope(pre):
    cdf = 0.5 + 0.5 * lax.erf(pre * 0.7071067811865476)
    pdf = jnp.exp(pre * pre * -0.5) * 0.3989422804014327
    return (pre * cdf).astype(BF), (cdf + pre * pdf).astype(BF)


def column_sum(values):
    return jnp.sum(values, axis=0, keepdims=True)


def half_mask(values, which):
    lanes = lax.broadcasted_iota(jnp.int32, values.shape, 1)
    keep = (lanes < HD) if which == 0 else (lanes >= HD)
    return jnp.where(keep, values, jnp.zeros_like(values))


def attend(x, vector, length, wq, out_qkv, out_probs, out_att):
    span = x.shape[0]
    parts = []
    for j in range(3):
        value = mm(x, wq(j)[j])
        if j == 0:
            value = value + vector(BIAS_Q, LOCAL)
        if j == 2:
            value = value + vector(BIAS_V, LOCAL)
        value = value.astype(BF)
        out_qkv[:, j * LOCAL : (j + 1) * LOCAL] = value
        parts.append(value)
    out_qkv.start()
    query, key, value = parts
    keys = lax.broadcasted_iota(jnp.int32, (span, span), 0)
    usable = keys < length
    mixed = []
    for pair in range(LOCAL // 128):
        at = slice(pair * 128, pair * 128 + 128)
        total = None
        for which in range(2):
            scores = mm(half_mask(key[:, at], which), query[:, at], NT) * 0.125
            scores = jnp.where(usable, scores, -1e30)
            raised = jnp.exp(scores - jnp.max(scores, axis=0, keepdims=True))
            probs = (raised * (1.0 / jnp.sum(raised, axis=0, keepdims=True))).astype(BF)
            out_probs[2 * pair + which] = probs
            term = mm(probs, half_mask(value[:, at], which), TN)
            total = term if total is None else total + term
        mixed.append(total.astype(BF))
    out_probs.start()
    att = jnp.concatenate(mixed, axis=1)
    out_att[...] = att
    return att


def attention_kernel(layer, chain, meta, *refs):
    if layer == 0:
        x_ref, *vecs = refs[:3]
        refs = refs[3:]
    else:
        feed_own, feed_got, hidden, *vecs = refs[:5]
        refs = refs[5:]
    own_q, got_q, own_o, got_o, *refs, wq, wo, sems = refs
    if layer == 0:
        out_qkv, out_probs, out_att, out_branch = refs
    else:
        out_x, out_x_saved, out_r2, out_qkv, out_probs, out_att, out_branch = refs
    length, tag = meta.length(chain), meta.tag(chain)
    is_own = meta.section == layer
    vector = vec_reader(vecs, is_own, tag)
    wq = Weights(own_q, got_q, is_own, [(j, (tag, j), j) for j in range(3)], wq, sems)
    wo = Weights(own_o, got_o, is_own, [(0, tag, None)], wo, sems, 3)
    if layer == 0:
        x = x_ref[...]
    else:
        before = vec_reader(vecs, meta.section == 0, tag)
        r2 = hidden[...] + ((feed_own[...].astype(F32) + feed_got[...].astype(F32)) + before(SHIFT[2]))
        out_r2[...] = r2
        normed, _ = layer_norm(r2)
        x = (normed * before(GAIN_TWO) + before(SHIFT[3])).astype(BF)
        out_x[...] = x
        out_x_saved[...] = x
    att = attend(x, vector, length, wq, out_qkv, out_probs, out_att)
    out_branch[...] = mm(att, wo()[...]).astype(BF)


def feed_kernel(layer, chain, meta, x, own, got, *refs):
    *vecs, own_i, got_i, own_d, got_d = refs[:6]
    out_hidden, out_r1, out_slope, out_act, out_low, out_feed, act, wi, wd, sems = refs[6:]
    tag = meta.tag(chain)
    is_own = meta.section == layer
    wi = Weights(own_i, got_i, is_own, in_halves(tag, 1), wi, sems)
    wd = Weights(own_d, got_d, is_own, [(0, tag, None)], wd, sems, 2)
    vector = vec_reader(vecs, is_own, tag)
    branch = (own[...].astype(F32) + got[...].astype(F32)) + vector(SHIFT[0])
    r1 = x[...].astype(F32) + branch
    out_r1[...] = r1
    normed, _ = layer_norm(r1)
    hidden = normed * vector(GAIN_ONE) + vector(SHIFT[1])
    out_hidden[...] = hidden
    low = hidden.astype(BF)
    out_low[...] = low
    for half in range(2):
        at = half * HALF
        pre = mm(low, wi(half)[:, at : at + HALF]) + vector(BIAS_IN + at, HALF)
        act[:, at : at + HALF], out_slope[:, at : at + HALF] = gelu_and_slope(pre)

        @pl.when(meta.rep == half)
        def _():
            out_act[:, :] = act[:, at : at + HALF]

    out_act.start()
    out_slope.start()
    out_feed[...] = mm(act[...], wd()[...]).astype(BF)


def feed_back_kernel(layer, chain, meta, own, got, *refs):
    first, second, *vecs, act_slope, own_i, got_i, own_d, got_d = refs[:9]
    out_y, out_dr2, out_df, out_du, out_dh, out_vec, du_all, wi, wd, sems = refs[9:]
    length, tag = meta.length(chain), meta.tag(chain)
    is_own = meta.section == layer
    wd = Weights(own_d, got_d, is_own, in_halves(tag, 0), wd, sems)
    wi = Weights(own_i, got_i, is_own, [(0, tag, None)], wi, sems, 2)
    vector = vec_reader(vecs, is_own, tag)
    gain = vector(GAIN_TWO)
    both = own[...].astype(F32) + got[...].astype(F32)
    if layer == 1:
        hidden, cotangent = first, second
        normed, inverse = layer_norm(hidden[...] + (both + vector(SHIFT[2])))
        out_y[...] = (normed * gain + vector(SHIFT[3])).astype(BF)
        tokens = lax.broadcasted_iota(jnp.int32, both.shape, 0)
        dy = jnp.where(tokens < length, cotangent[...].astype(F32), 0.0)
    else:
        dr1, r2 = first, second
        low = (both + dr1[...]).astype(BF)
        out_y[...] = low
        dy = low.astype(F32)
        normed, inverse = layer_norm(r2[...])
    dr2 = layer_norm_back(dy, gain, normed, inverse)
    out_dr2[...] = dr2
    df = dr2.astype(BF)
    out_df[...] = df
    out_vec[:, 0:768] = column_sum(dy * normed)
    out_vec[:, 768:1536] = column_sum(dr2)
    out_vec[:, 1536:2304] = column_sum(dy)
    for half in range(2):
        at = half * HALF
        du = mm(df, wd(half)[at : at + HALF, :], NT) * act_slope[:, at : at + HALF].astype(F32)
        out_vec[:, 2304 + at : 2304 + at + HALF] = column_sum(du)
        du_all[:, at : at + HALF] = du.astype(BF)

        @pl.when(meta.rep == half)
        def _():
            out_du[:, :] = du_all[:, at : at + HALF]

    out_du.start()
    out_dh[...] = mm(du_all[...], wi()[...], NT).astype(BF)


def attention_back_kernel(layer, chain, meta, own, got, dr2, r1, *refs):
    *vecs, qkv, probs_ref, own_q, got_q, own_o, got_o = refs[:8]
    out_dr1, out_dz, out_dqkv, out_dx, out_vec, wq, wo, sems = refs[8:]
    tag = meta.tag(chain)
    is_own = meta.section == layer
    wo = Weights(own_o, got_o, is_own, [(0, tag, None)], wo, sems, 3)
    wq = Weights(own_q, got_q, is_own, [(j, (tag, j), j) for j in range(3)], wq, sems)
    vector = vec_reader(vecs, is_own, tag)
    dh = (own[...].astype(F32) + got[...].astype(F32)) + dr2[...]
    normed, inverse = layer_norm(r1[...])
    dr1 = layer_norm_back(dh, vector(GAIN_ONE), normed, inverse)
    out_dr1[...] = dr1
    dz = dr1.astype(BF)
    out_dz[...] = dz
    out_vec[:, 0:768] = column_sum(dh * normed)
    out_vec[:, 768:1536] = column_sum(dr1)
    out_vec[:, 1536:2304] = column_sum(dh)
    datt = mm(dz, wo()[...], NT).astype(BF)
    query, key, value = (qkv[:, j * LOCAL : (j + 1) * LOCAL] for j in range(3))
    for pair in range(LOCAL // 128):
        at = slice(pair * 128, pair * 128 + 128)
        dv = dq = dk = None
        for which in range(2):
            probs = probs_ref[2 * pair + which]
            dv_term = mm(probs, half_mask(datt[:, at], which))
            dprobs = mm(half_mask(value[:, at], which), datt[:, at], NT)
            wide = probs.astype(F32)
            dscores = wide * (dprobs - jnp.sum(wide * dprobs, axis=0, keepdims=True))
            dscores = dscores.astype(BF)
            dk_term = mm(dscores, half_mask(query[:, at], which))
            dq_term = mm(dscores, half_mask(key[:, at], which), TN)
            dv = dv_term if dv is None else dv + dv_term
            dk = dk_term if dk is None else dk + dk_term
            dq = dq_term if dq is None else dq + dq_term
        dq = dq * 0.125
        dk = dk * 0.125
        low = pair * 128
        out_vec[:, 2304 + low : 2304 + low + 128] = column_sum(dq)
        out_vec[:, 2688 + low : 2688 + low + 128] = column_sum(dv)
        out_dqkv[:, low : low + 128] = dq.astype(BF)
        out_dqkv[:, LOCAL + low : LOCAL + low + 128] = dk.astype(BF)
        out_dqkv[:, 2 * LOCAL + low : 2 * LOCAL + low + 128] = dv.astype(BF)
    out_dqkv.start()
    dx = None
    for j in range(3):
        term = mm(out_dqkv[:, j * LOCAL : (j + 1) * LOCAL], wq(j)[j], NT)
        dx = term if dx is None else dx + term
    out_dx[...] = dx.astype(BF)


def far_kernel(layer, chains, meta, *refs):
    low = refs[:chains]
    *vecs, own_i, got_i, out_act, out_slope, wi, sems = refs[chains:]
    span = low[0].shape[0]
    is_own = meta.section == layer
    half = pl.ds(pl.multiple_of(meta.rep * HALF, HALF), HALF)
    wi = Weights(own_i, got_i, is_own, [(0, (slice(None), slice(None), half), None)], wi, sems)()
    for chain in range(chains):
        tag = meta.far_tag(chain)
        at = slice(chain * span, (chain + 1) * span)
        bias = vec_reader(vecs, is_own, tag)(pl.multiple_of(BIAS_IN + meta.rep * HALF, HALF), HALF)
        pre = mm(low[chain][...], wi[tag]) + bias
        out_act[at, :], out_slope[at, :] = gelu_and_slope(pre)


def order_of(tags, section):
    mine = [(tag == section).astype(jnp.int32) for tag in tags]
    count = sum(mine)
    places, before = [], 0
    for index, one in enumerate(mine):
        places.append(jnp.where(one == 1, before, count + index - before))
        before = before + one
    return places, count


class Gathered:
    def __init__(self, sources, places, target, sems, first):
        self.place, self.copies = target, []
        for index, (source, place) in enumerate(zip(sources, places)):
            extent = source.shape[0]
            at = pl.ds(pl.multiple_of(place * extent, extent), extent)
            copy = pltpu.make_async_copy(source, target.at[at], sems.at[first + index])
            copy.start()
            self.copies.append(copy)

    def wait(self):
        for copy in self.copies:
            copy.wait()
        return self.place


def both_models(count, chains, span, left, rights, stores):
    def branch(number):
        def products():
            cut = number * span
            for right, store in zip(rights, stores):
                columns = right.shape[1]
                for keeping, rows in ((False, slice(cut, chains * span)), (True, slice(0, cut))):
                    if rows.start == rows.stop:
                        store(keeping, jnp.zeros((left.shape[0], columns), BF))
                    else:
                        store(keeping, mm(left[:, rows], right[rows, :]).astype(BF))

        return products

    for number in range(chains + 1):
        pl.when(count == number)(branch(number))


def feed_grad_kernel(layer, chains, meta, *refs):
    df, act, low, du, far_df, far_low = (refs[i * chains : (i + 1) * chains] for i in range(6))
    far_act, far_slope, own_d, got_d, keep, send, df_all, act_all, low_all, du_all, wd, sems = refs[6 * chains :]
    span = df[0].shape[0]
    half = pl.ds(pl.multiple_of(meta.rep * HALF, HALF), HALF)
    is_own = meta.section == layer
    tags = [meta.tag(chain) for chain in range(chains)] + [meta.far_tag(chain) for chain in range(chains)]
    places, count = order_of(tags, meta.section)
    far_acts = [far_act.at[pl.ds(chain * span, span)] for chain in range(chains)]
    wd = Weights(own_d, got_d, is_own, [(0, (slice(None), half), None)], wd, sems, 8 * chains)
    df_all = Gathered([*df, *far_df], places, df_all, sems, 0)
    act_all = Gathered([*act, *far_acts], places, act_all, sems, 2 * chains)
    du_all = Gathered(du, places, du_all, sems, 4 * chains)
    low_all = Gathered([*low, *far_low], places, low_all, sems, 6 * chains)

    def products(left_all, at, right):
        def column_block(index, carry):
            rows = pl.ds(pl.multiple_of(index * BLOCK, BLOCK), BLOCK)
            left = left_all[:, rows].T

            def store(keeping, value):
                out = keep.place if keeping else send
                out[rows, at : at + HALF] = value

            both_models(count, 2 * chains, span, left, [right], [store])
            return carry

        lax.fori_loop(0, WIDTH // BLOCK, column_block, 0)
        keep.start(at // HALF)

    lefts = df_all.wait()
    products(lefts, 0, act_all.wait())
    rights = du_all.wait()
    weights = wd()
    for chain in range(chains):
        at = slice(chain * span, (chain + 1) * span)
        there = pl.ds(pl.multiple_of(places[chains + chain] * span, span), span)
        value = mm(lefts[there, :], weights[meta.far_tag(chain)], NT) * far_slope[at, :].astype(F32)
        rights[there, :] = value.astype(BF)
    products(low_all.wait(), HALF, rights)


def attention_grad_kernel(layer, chains, meta, *refs):
    dz, att, x, dqkv = (refs[i * chains : (i + 1) * chains] for i in range(4))
    keep, send, dz_all, att_all, x_all, dqkv_all, sems = refs[4 * chains :]
    span = dz[0].shape[0]
    if layer == 0:
        x = [ref.at[chain, meta.section] for chain, ref in enumerate(x)]
    places, count = order_of([meta.tag(chain) for chain in range(chains)], meta.section)
    dz_all = Gathered(dz, places, dz_all, sems, 0)
    att_all = Gathered(att, places, att_all, sems, chains)
    x_all = Gathered(x, places, x_all, sems, 2 * chains)
    dqkv_all = Gathered(dqkv, places, dqkv_all, sems, 3 * chains)
    first = jnp.where(meta.rep == 0, 0, 1)

    def products(left_all, rights, targets):
        def column_block(index, carry):
            rows = pl.ds(pl.multiple_of(index * BLOCK, BLOCK), BLOCK)
            left = left_all[:, rows].T

            def store_at(slot, columns):
                def store(keeping, value):
                    out = keep.place if keeping else send
                    out[slot, rows, columns] = value

                return store

            both_models(count, chains, span, left, rights, [store_at(*target) for target in targets])
            return carry

        lax.fori_loop(0, WIDTH // BLOCK, column_block, 0)

    left_all, right = dz_all.wait(), att_all.wait()
    products(left_all, [right], [(first, slice(0, LOCAL))])
    left_all, right = x_all.wait(), dqkv_all.wait()
    rights = [right.at[:, pl.ds(0, LOCAL)], right.at[:, pl.ds(LOCAL, 2 * LOCAL)]]
    products(left_all, rights, [(first, slice(LOCAL, HALF)), (1 - first, slice(0, HALF))])


def add_kernel(parts, meta, one, two, out):
    block = one.shape[0] // parts
    for part in range(parts):
        at = slice(part * block, (part + 1) * block)
        one.wait(part)
        out[at, :] = one.place[at, :] + two[at, :]
        out.start(part)


def add_halves_kernel(meta, one, two, near, far):
    for half, out in ((1, far), (0, near)):
        one.wait(half)
        out[...] = one.place[half] + two[half]


BLOCK = 256
ANY = pl.BlockSpec(memory_space=pl.ANY)


def pack_kernel(gains, shifts, b_qv, b_in, out):
    for model in range(2):
        row = slice(model, model + 1)
        for j in range(2):
            out[row, j * WIDTH : (j + 1) * WIDTH] = gains[0, model, j : j + 1, :]
            out[row, BIAS_Q + j * LOCAL : BIAS_Q + (j + 1) * LOCAL] = b_qv[0, model, j : j + 1, :]
        for j in range(4):
            out[row, SHIFT[j] : SHIFT[j] + WIDTH] = shifts[0, model, j : j + 1, :]
        out[row, BIAS_IN:] = b_in[0, row, :]


def feed_final_kernel(meta, *refs):
    zero, one, got, grad_in, grad_out = refs[:2], refs[2:4], refs[4], refs[5], refs[6]
    for half in range(2):
        local = jnp.where(meta.rep == 0, half, 1 - half)
        mine = jnp.where(meta.section == 0, zero[half][...], one[half][...]).astype(F32)
        columns = pl.ds(pl.multiple_of(local * HALF, HALF), HALF)
        for model, shard in ((meta.section, mine), (1 - meta.section, got[half].astype(F32))):
            grad_out[model, :, columns] = shard[:, 0:HALF]
            grad_in[model, :, columns] = shard[:, HALF:]


def attention_final_kernel(meta, *refs):
    zero, one, got, grad_qkv, grad_o = refs[:2], refs[2:4], refs[4], refs[5], refs[6]
    mine = [jnp.where(meta.section == 0, zero[half][...], one[half][...]).astype(F32) for half in range(2)]
    for model, near, far in (
        (meta.section, *mine),
        (1 - meta.section, got[0].astype(F32), got[1].astype(F32)),
    ):
        low = jnp.where(meta.rep == 0, near, far)
        high = jnp.where(meta.rep == 0, far, near)
        grad_o[model] = low[:, 0:LOCAL]
        grad_qkv[model, 0] = low[:, LOCAL:]
        grad_qkv[model, 1] = high[:, 0:LOCAL]
        grad_qkv[model, 2] = high[:, LOCAL:]


def vector_grad_kernel(chains, meta, *refs):
    out = refs[-1]
    for layer in range(2):
        ones = refs[2 * layer * chains : (2 * layer + 1) * chains]
        twos = refs[(2 * layer + 1) * chains : (2 * layer + 2) * chains]
        rows = [
            jnp.concatenate(
                [one[:, 0:768], two[:, 0:768], one[:, 768:2304], two[:, 768:2304], one[:, 2304:], two[:, 2304:]],
                axis=1,
            )
            for one, two in zip(ones, twos)
        ]
        for model in range(2):
            total = None
            for chain in range(chains):
                row = jnp.where(meta.tag(chain) == model, rows[chain], 0.0)
                total = row if total is None else total + row
            out[layer, model : model + 1, :] = total


STEP = 1.5e9
LONG = 8

VMEM = pl.BlockSpec(memory_space=pltpu.VMEM)
SMEM = pl.BlockSpec(memory_space=pltpu.SMEM)
SAVED = "saved"


def pieces_of(out):
    return out[3] if len(out) > 3 else [None]


def in_hbm(value):
    return pltpu.with_memory_space_constraint(value, pltpu.HBM)


def call(body, scalars, operands, outs, scratch, name, grant, cost):
    saved_in = [value for value in operands if isinstance(value, Saved)]
    saved_out = [out for out in outs if SAVED in out]
    buffers = [pltpu.VMEM(value.shape, value.value.dtype) for value in saved_in]
    buffers += [pltpu.VMEM(out[0], out[1]) for out in saved_out]
    counts = (len(scalars), len(operands), len(outs), len(scratch))

    def kernel(*refs):
        groups = []
        for count in counts:
            groups.append(refs[:count])
            refs = refs[count:]
        numbers, ins, results, own_scratch = groups
        *places, sems = refs
        meta = Scalars(*numbers)
        given, taken, index, sem = [], [], 0, 0
        for value, ref in zip(operands, ins):
            if isinstance(value, Saved):
                source = ref if value.chain is None else ref.at[value.chain, meta.section]
                ref = Lazy(source, places[index], sems, sem, value.parts)
                ref.start()
                sem += value.parts
                index += 1
            given.append(ref)
        for out, ref in zip(outs, results):
            if SAVED in out:
                ref = Leaving(places[index], ref, sems, sem, pieces_of(out))
                sem += len(pieces_of(out))
                index += 1
            taken.append(ref)
        body(meta, *given, *taken, *own_scratch)
        for ref in taken:
            if isinstance(ref, Leaving):
                ref.start()
        for ref in given:
            if isinstance(ref, Lazy):
                ref.wait()
        for ref in taken:
            if isinstance(ref, Leaving):
                ref.wait()

    in_specs = [ANY if isinstance(value, (tuple, Saved)) else VMEM for value in operands]
    values = []
    for value in operands:
        if isinstance(value, Saved):
            value = in_hbm(value.value)
        elif isinstance(value, tuple):
            value = in_hbm(value[0])
        values.append(value)
    shapes = [
        pltpu.HBM(out[0], out[1]) if SAVED in out else jax.ShapeDtypeStruct(out[0], out[1]) for out in outs
    ]
    return pl.pallas_call(
        kernel,
        out_shape=shapes,
        in_specs=[SMEM] * len(scalars) + in_specs,
        out_specs=[ANY if SAVED in out else VMEM for out in outs],
        scratch_shapes=[*scratch, *buffers, pltpu.SemaphoreType.DMA((max(sum(value.parts for value in saved_in) + sum(len(pieces_of(out)) for out in saved_out), 1),))],
        compiler_params=pltpu.CompilerParams(vmem_limit_bytes=grant * 1024 * 1024),
        cost_estimate=pl.CostEstimate(flops=int(cost * STEP), bytes_accessed=1, transcendentals=0),
        name=name,
    )(*scalars, *values)


def on_device(
    block_input, cotangent, lengths, tags, w_qkv, w_o, w_in, w_out, b_qv, b_in, gains, shifts
):
    micro, per, span, width = block_input.shape
    section = lax.axis_index("section")
    rep = lax.axis_index("rep")
    chains = range(micro)
    layers = range(2)

    own_q, own_o, own_i, own_d = w_qkv[0], w_o[0], w_in[0], w_out[0]
    got_q = swap(own_q, "section")
    vec_own = pl.pallas_call(
        pack_kernel, out_shape=jax.ShapeDtypeStruct((2, PACKED), F32), in_specs=[VMEM] * 4, out_specs=VMEM, name="pack"
    )(gains, shifts, b_qv, b_in)
    numbers = jnp.concatenate([lengths, tags], axis=1)
    vec_own = after(vec_own, numbers)
    vecs = [vec_own, swap(vec_own, "section")]
    got_o = swap(own_o, "section")
    later = lax.optimization_barrier((own_i, own_d, got_q, got_o, vecs[1]))
    got_i, got_d = swap(later[0], "section"), swap(later[1], "section")

    heads = LOCAL // HD
    row, saved_row = ((span, WIDTH), BF), ((span, WIDTH), BF, SAVED)
    wide, saved_wide = ((span, WIDTH), F32), ((span, WIDTH), F32, SAVED)
    half_row, long_row = ((span, HALF), BF, SAVED), ((span, HIDDEN), BF, SAVED)
    qkv_row = ((span, 3 * LOCAL), BF, SAVED)
    att_outs = [qkv_row, ((heads, span, span), BF, SAVED), ((span, LOCAL), BF, SAVED), row]
    raw = lambda values: [(value,) for value in values]
    w_qo, w_id = raw([own_q, got_q, own_o, got_o]), raw([own_i, got_i, own_d, got_d])
    qo_scratch = [
        pltpu.VMEM((3, WIDTH, LOCAL), BF),
        pltpu.VMEM((LOCAL, WIDTH), BF),
        pltpu.SemaphoreType.DMA((4,)),
    ]
    id_scratch = [
        pltpu.VMEM((span, HIDDEN), BF),
        pltpu.VMEM((WIDTH, HIDDEN), BF),
        pltpu.VMEM((HIDDEN, WIDTH), BF),
        pltpu.SemaphoreType.DMA((3,)),
    ]

    last = [numbers]

    def run(body, operands, outs, scratch, name, *waits, far=False, grant=14, cost=1):
        scalars = [after(numbers, last[0], *waits)] + ([far_tags] if far else [])
        results = call(body, scalars, operands, outs, scratch, name, grant, cost)
        last[0] = results[-1]
        return results

    def saved(values):
        return [Saved(value) for value in values]

    def arrived(pair):
        return [pair[0], Saved(pair[1])]

    def owned(zero, one):
        zero, one = jnp.stack(zero), jnp.stack(one)
        mine = jnp.where(section == 0, zero, one)
        other = swap(jnp.where(section == 0, one, zero), "section")
        core = lax.broadcasted_iota(jnp.int32, (micro, per, span, width), 1)
        return jnp.where(core == section, mine[:, None], other[:, None])[None]

    table = lambda: [[None] * micro for _ in layers]
    r1s, r2s, hiddens, acts, slopes, lows, far_lows, feeds, qkvs, probs, atts = (table() for _ in range(11))
    x_now, x_saved = [[Saved(block_input, chain) for chain in chains], [None] * micro], [None] * micro
    for layer in layers:
        for chain in chains:
            body = functools.partial(attention_kernel, layer, chain)
            name = f"attention{layer}{chain}"
            if layer == 0:
                got = run(body, [x_now[0][chain], *vecs] + w_qo, att_outs, qo_scratch, name)
            else:
                operands = [*arrived(feeds[0][chain]), hiddens[0][chain], *vecs] + w_qo
                waits = far_lows[0][:chain]
                x_now[1][chain], x_saved[chain], r2s[0][chain], *got = run(
                    body, operands, [row, saved_row, saved_wide] + att_outs, qo_scratch, name, *waits
                )
            qkvs[layer][chain], probs[layer][chain], atts[layer][chain], branch = got
            feeds[layer][chain] = (branch, swap(branch, "mp"))
        if layer == 0:
            far_tags = swap(after(tags, last[0]), "rep")
        for chain in chains:
            body = functools.partial(feed_kernel, layer, chain)
            waits = (far_lows[0][2:] if layer == 1 else []) + ([far_tags] if layer == 0 and chain == 2 else [])
            waits = waits if layer == 0 or chain == 0 else []
            hiddens[layer][chain], r1s[layer][chain], slopes[layer][chain], acts[layer][chain], low, part = run(
                body,
                [x_now[layer][chain], *feeds[layer][chain], *vecs] + w_id,
                [wide, saved_wide, long_row, half_row, saved_row, row],
                id_scratch,
                f"feed{layer}{chain}",
                *waits,
            )
            lows[layer][chain], far_lows[layer][chain] = low, swap(low, "rep") if layer == 0 or chain == 0 else None
            feeds[layer][chain] = (part, swap(part, "mp"))
    far_lows[1][1:] = [swap(after(low, part), "rep") for low in lows[1][1:]]

    rows = micro * span
    far_rows = ((rows, HALF), BF, SAVED)
    dr2s, dfs, far_dfs, dus, dhs, vec_one, vec_two, dzs, dqkvs, dr1s, dxs, ys = (table() for _ in range(12))
    far_hidden = [None, None]

    def feed_back(layer, chain, *waits, cost=1):
        if layer == 1:
            operands = [*arrived(feeds[1][chain]), hiddens[1][chain], Saved(cotangent, chain)]
        else:
            operands = [*arrived(dxs[1][chain]), Saved(dr1s[1][chain]), Saved(r2s[0][chain])]
        ys[layer][chain], dr2s[layer][chain], df, dus[layer][chain], dh, vec_two[layer][chain] = run(
            functools.partial(feed_back_kernel, layer, chain),
            operands + [*vecs, Saved(slopes[layer][chain])] + w_id,
            [saved_row, saved_wide, saved_row, half_row, row, ((1, 3 * WIDTH + HIDDEN), F32, SAVED)],
            id_scratch,
            f"feed_back{layer}{chain}",
            *waits,
            cost=cost,
        )
        dfs[layer][chain], far_dfs[layer][chain] = df, swap(df, "rep")
        dhs[layer][chain] = (dh, swap(dh, "mp"))

    def attention_back(layer, chain, *waits, cost=1):
        dr1s[layer][chain], dzs[layer][chain], dqkvs[layer][chain], dx, vec_one[layer][chain] = run(
            functools.partial(attention_back_kernel, layer, chain),
            [*arrived(dhs[layer][chain]), Saved(dr2s[layer][chain]), Saved(r1s[layer][chain]), *vecs]
            + [Saved(qkvs[layer][chain]), Saved(probs[layer][chain])]
            + w_qo,
            [saved_wide, saved_row, qkv_row, row, ((1, 3 * WIDTH + 2 * LOCAL), F32, SAVED)],
            qo_scratch,
            f"attention_back{layer}{chain}",
            *waits,
            cost=cost,
        )
        dxs[layer][chain] = (dx, swap(dx, "mp"))

    def far_part(layer, *waits):
        far_hidden[layer] = run(
            functools.partial(far_kernel, layer, micro),
            saved(far_lows[layer]) + [*vecs] + w_id[:2],
            [far_rows] * 2,
            [pltpu.VMEM((2, WIDTH, HALF), BF), pltpu.SemaphoreType.DMA((1,))],
            f"far{layer}",
            *waits,
            far=True,
            cost=1.5,
        )

    def feed_grad(layer, *waits, cost=2):
        near = dfs[layer] + acts[layer] + lows[layer] + dus[layer]
        far_act, far_slope = far_hidden[layer]
        stacked = pltpu.VMEM((2 * rows, HALF), BF)
        keep, send = run(
            functools.partial(feed_grad_kernel, layer, micro),
            raw(near + far_dfs[layer] + far_lows[layer] + [far_act]) + [Saved(far_slope)] + w_id[2:],
            [((WIDTH, HIDDEN), BF, SAVED, blocks_of(WIDTH, HIDDEN, WIDTH, HALF)), ((WIDTH, HIDDEN), BF)],
            [stacked] * 4 + [pltpu.VMEM((2, HALF, WIDTH), BF), pltpu.SemaphoreType.DMA((8 * micro + 1,))],
            f"feed_grad{layer}",
            *waits,
            far=True,
            grant=20,
            cost=cost,
        )
        return keep, swap(send, "section")

    def feed_grad_sum(layer, parts, *waits):
        (result,) = run(
            functools.partial(add_kernel, WIDTH // BLOCK),
            [Saved(parts[0], parts=WIDTH // BLOCK), parts[1]],
            [((WIDTH, HIDDEN), BF, SAVED, blocks_of(WIDTH, HIDDEN, BLOCK, HIDDEN))],
            [],
            f"feed_grad_sum{layer}",
            *waits,
        )
        return result

    def attention_grad(layer, *waits):
        x_part = raw([block_input] * micro if layer == 0 else x_saved)
        narrow, stacked = pltpu.VMEM((rows, LOCAL), BF), pltpu.VMEM((rows, WIDTH), BF)
        keep, send = run(
            functools.partial(attention_grad_kernel, layer, micro),
            raw(dzs[layer] + atts[layer]) + x_part + raw(dqkvs[layer]),
            [((2, WIDTH, HALF), BF, SAVED, [pl.ds(0, 1), pl.ds(1, 1)]), ((2, WIDTH, HALF), BF)],
            [stacked, narrow, stacked, pltpu.VMEM((rows, 3 * LOCAL), BF), pltpu.SemaphoreType.DMA((4 * micro,))],
            f"attention_grad{layer}",
            *waits,
            cost=2,
        )
        return keep, swap(send, "section")

    def attention_grad_sum(layer, parts, *waits):
        near, far = run(
            add_halves_kernel,
            [Saved(parts[0], parts=2), parts[1]],
            [((WIDTH, HALF), BF, SAVED)] * 2,
            [],
            f"attention_grad_sum{layer}",
            *waits,
        )
        return near, swap(far, "rep")

    def scattered(part):
        return lax.psum_scatter(part, "dp", scatter_dimension=0, tiled=True)

    feed_back(1, 0, feeds[1][1][1], far_lows[1][0])
    feed_back(1, 1, feeds[1][2][1])
    feed_back(1, 2)
    far_part(1, dhs[1][0][1], far_dfs[1][0])
    parts = feed_grad(1, dhs[1][1][1], far_dfs[1][1])
    attention_back(1, 0, dhs[1][2][1], cost=20)
    feed_one = scattered(feed_grad_sum(1, parts))
    attention_back(1, 1)
    attention_back(1, 2, dxs[1][0][1])
    parts = attention_grad(1, dxs[1][1][1])
    near, far = attention_grad_sum(1, parts)
    feed_back(0, 0)
    feed_back(0, 1, dxs[1][2][1])
    feed_back(0, 2, dhs[0][0][1])
    far_part(0, dhs[0][1][1])
    attention_one = after(near, last[0]) + far
    layer_outputs = owned(after(x_saved, last[0]), ys[1])
    attention_back(0, 0, attention_one, layer_outputs)
    attention_one = scattered(after(attention_one, feed_one))
    feed_one = (feed_one, swap(feed_one, "rep"))
    parts = feed_grad(0, dhs[0][2][1], cost=4)
    attention_back(0, 1, attention_one, feed_one[1], cost=30)
    feed_zero = feed_grad_sum(0, parts)
    feed_zero = scattered(after(feed_zero, attention_one))
    attention_back(0, 2)
    (both,) = run(
        functools.partial(vector_grad_kernel, micro),
        saved(vec_one[0] + vec_two[0] + vec_one[1] + vec_two[1]),
        [((2, 2, PACKED), F32)],
        [],
        "vector_grad",
    )
    both = both + swap(both, "section")
    both = lax.dynamic_index_in_dim(both, section, 0, keepdims=False)
    parts = attention_grad(0, both)
    both = both + swap(both, "rep")
    near, far = attention_grad_sum(0, parts, both)
    both = after(both, near)
    data = lax.axis_size("dp")
    distance = 1
    while distance < data:
        both = both + lax.ppermute(both, "dp", [(i, i ^ distance) for i in range(data)])
        distance *= 2
    firsts = [
        ((after(dx[0], near, feed_zero, both).astype(F32) + dx[1].astype(F32)) + dr1).astype(BF) for dx, dr1 in zip(dxs[0], dr1s[0])
    ]
    attention_zero = after(after(near, firsts) + far, feed_zero)
    done = attention_zero
    feed_zero = (feed_zero, swap(after(feed_zero, done), "rep"))
    attention_one = (attention_one, swap(after(attention_one, both), "rep"))
    grad_gains = both[:, : SHIFT[0]].reshape(2, 2, WIDTH)
    grad_shifts = both[:, SHIFT[0] : BIAS_Q].reshape(2, 4, WIDTH)
    grad_b_qv = both[:, BIAS_Q:BIAS_IN].reshape(2, 2, LOCAL)
    grad_b_in = both[:, BIAS_IN:]
    attention_zero = scattered(attention_zero)

    def handed(zero, one):
        return swap(jnp.where(section == 0, jnp.stack(one), jnp.stack(zero)), "section")

    shard = feed_zero[0].shape[0]
    grad_in, grad_out = run(
        feed_final_kernel,
        [*feed_zero, *feed_one, handed(feed_zero, feed_one)],
        [((2, shard, HIDDEN), F32)] * 2,
        [],
        "feed_final",
    )
    input_grads = owned(after(firsts, done), ys[0])
    attention_zero = after(attention_zero, input_grads, attention_one[1])
    vectors = grad_b_qv[None], grad_b_in[None], grad_gains[None], grad_shifts[None]
    far, vectors, _ = lax.optimization_barrier((swap(attention_zero, "rep"), vectors, grad_in))
    attention_zero = (attention_zero, far)
    grad_qkv, grad_o = run(
        attention_final_kernel,
        [*attention_zero, *attention_one, handed(attention_zero, attention_one)],
        [((2, 3, shard, LOCAL), F32), ((2, shard, LOCAL), F32)],
        [],
        "attention_final",
    )
    grad_out, grad_o = jnp.swapaxes(grad_out, 1, 2), jnp.swapaxes(grad_o, 1, 2)

    return (
        layer_outputs,
        input_grads,
        grad_qkv[None],
        grad_o[None],
        grad_in[None],
        grad_out[None],
        *vectors,
    )


def solution(mesh):
    in_specs = (
        P(None, ("dp", "rep"), None, None),
        P(None, ("dp", "rep"), None, None),
        P(None, ("dp", "rep")),
        P(None, ("dp", "rep")),
        P("section", None, None, None, "mp"),
        P("section", None, "mp", None),
        P("section", None, None, "mp"),
        P("section", None, "mp", None),
        P("section", None, None, "mp"),
        P("section", None, "mp"),
        P("section", None, None, None),
        P("section", None, None, None),
    )
    out_specs = (
        P("section", None, ("dp", "rep"), None, None),
        P("section", None, ("dp", "rep"), None, None),
        P("section", None, None, "dp", "mp"),
        P("section", None, "mp", "dp"),
        P("section", None, "dp", "mp"),
        P("section", None, "mp", "dp"),
        P("section", None, None, "mp"),
        P("section", None, "mp"),
        P("section", None, None, None),
        P("section", None, None, None),
    )
    return jax.shard_map(
        on_device, mesh=mesh, in_specs=in_specs, out_specs=out_specs, check_vma=False
    )
```

```python
import functools

import jax
import jax.numpy as jnp
from jax import lax
from jax.experimental import pallas as pl
from jax.experimental.pallas import tpu as pltpu
from jax.sharding import PartitionSpec as P

HD = 64
EPS = 1e-05
BF = jnp.bfloat16
F32 = jnp.float32

GAIN_ONE, GAIN_TWO = 0, 768
SHIFT = (1536, 2304, 3072, 3840)
BIAS_Q, BIAS_V, BIAS_IN = 4608, 4992, 5376
PACKED = 6912
WIDTH, LOCAL, HIDDEN, HALF = 768, 384, 1536, 768

NN = (((1,), (0,)), ((), ()))
NT = (((1,), (1,)), ((), ()))
TN = (((0,), (0,)), ((), ()))


def mm(left, right, dims=NN):
    return lax.dot_general(left, right, dims, preferred_element_type=F32)


def swap(block, axis):
    return lax.ppermute(block, axis, [(0, 1), (1, 0)])


def after(value, *others):
    return lax.optimization_barrier((value, *others))[0]


class Lazy:
    def __init__(self, source, place, sems, first, parts):
        self.place, self.waited, self.copies = place, set(), []
        extent = place.shape[0] // parts
        for part in range(parts):
            at = pl.ds(part * extent, extent)
            near, away = (place, source) if parts == 1 else (place.at[at], source.at[at])
            self.copies.append(pltpu.make_async_copy(away, near, sems.at[first + part]))

    shape = property(lambda self: self.place.shape)

    def start(self):
        for copy in self.copies:
            copy.start()

    def wait(self, part=None):
        for index in range(len(self.copies)) if part is None else (part,):
            if index not in self.waited:
                self.copies[index].wait()
                self.waited.add(index)

    def __getitem__(self, at):
        self.wait()
        return self.place[at]


class Leaving:
    def __init__(self, place, target, sems, first, pieces):
        self.place, self.started, self.copies = place, set(), []
        for index, at in enumerate(pieces):
            near, away = (place, target) if at is None else (place.at[at], target.at[at])
            self.copies.append(pltpu.make_async_copy(near, away, sems.at[first + index]))

    shape = property(lambda self: self.place.shape)

    def start(self, piece=None):
        for index in range(len(self.copies)) if piece is None else (piece,):
            if index not in self.started:
                self.copies[index].start()
                self.started.add(index)

    def wait(self):
        for copy in self.copies:
            copy.wait()

    def __getitem__(self, at):
        return self.place[at]

    def __setitem__(self, at, value):
        self.place[at] = value
        if at is Ellipsis:
            self.start()


def blocks_of(rows, columns, row_step, column_step):
    return [
        (pl.ds(row, row_step), pl.ds(column, column_step))
        for column in range(0, columns, column_step)
        for row in range(0, rows, row_step)
    ]


class Saved:
    def __init__(self, value, chain=None, parts=1):
        self.value, self.chain, self.parts = value, chain, parts
        self.shape = value.shape if chain is None else value.shape[2:]


class Scalars:
    def __init__(self, numbers, far_tags=None):
        self.section, self.rep = lax.axis_index("section"), lax.axis_index("rep")
        self.numbers, self.far_tags = numbers, far_tags

    def length(self, chain):
        return self.numbers[chain, self.section]

    def tag(self, chain):
        return self.numbers[chain, 2 + self.section]

    def far_tag(self, chain):
        return self.far_tags[chain, self.section]


def layer_norm(resid):
    mean = jnp.mean(resid, -1, keepdims=True)
    centred = resid - mean
    inverse = lax.rsqrt(jnp.mean(centred * centred, -1, keepdims=True) + EPS)
    return centred * inverse, inverse


def layer_norm_back(grad, gain, normed, inverse):
    scaled = grad * gain
    return inverse * (
        scaled
        - jnp.mean(scaled, -1, keepdims=True)
        - normed * jnp.mean(scaled * normed, -1, keepdims=True)
    )


class Weights:
    def __init__(self, own, got, is_own, pieces, place, sems, first=0):
        self.place, self.copies, self.waited = place, {}, set()
        for index, (name, source, target) in enumerate(pieces):
            target = place.at[target] if target is not None else place
            near = pltpu.make_async_copy(own.at[source], target, sems.at[first + index])
            away = pltpu.make_async_copy(got.at[source], target, sems.at[first + index])
            self.copies[name] = near
            pl.when(is_own)(near.start)
            pl.when(jnp.logical_not(is_own))(away.start)

    def __call__(self, name=0):
        self.copies[name].wait()
        return self.place


def in_halves(tag, axis):
    pieces = []
    for half in range(2):
        at = pl.ds(half * HALF, HALF)
        at = (at,) if axis == 0 else (slice(None), at)
        pieces.append((half, (tag, *at), at))
    return pieces


def vec_reader(vecs, is_own, tag):
    own, got = vecs

    def read(at, extent=WIDTH):
        span = slice(at, at + extent) if isinstance(at, int) else pl.ds(at, extent)
        return jnp.where(is_own, own[pl.ds(tag, 1), span], got[pl.ds(tag, 1), span])

    return read


def gelu_and_slope(pre):
    cdf = 0.5 + 0.5 * lax.erf(pre * 0.7071067811865476)
    pdf = jnp.exp(pre * pre * -0.5) * 0.3989422804014327
    return (pre * cdf).astype(BF), (cdf + pre * pdf).astype(BF)


def column_sum(values):
    return jnp.sum(values, axis=0, keepdims=True)


def half_mask(values, which):
    lanes = lax.broadcasted_iota(jnp.int32, values.shape, 1)
    keep = (lanes < HD) if which == 0 else (lanes >= HD)
    return jnp.where(keep, values, jnp.zeros_like(values))


def attend(x, vector, length, wq, out_qkv, out_probs, out_att):
    span = x.shape[0]
    parts = []
    for j in range(3):
        value = mm(x, wq(j)[j])
        if j == 0:
            value = value + vector(BIAS_Q, LOCAL)
        if j == 2:
            value = value + vector(BIAS_V, LOCAL)
        value = value.astype(BF)
        out_qkv[:, j * LOCAL : (j + 1) * LOCAL] = value
        parts.append(value)
    out_qkv.start()
    query, key, value = parts
    keys = lax.broadcasted_iota(jnp.int32, (span, span), 0)
    usable = keys < length
    mixed = []
    for pair in range(LOCAL // 128):
        at = slice(pair * 128, pair * 128 + 128)
        total = None
        for which in range(2):
            scores = mm(half_mask(key[:, at], which), query[:, at], NT) * 0.125
            scores = jnp.where(usable, scores, -1e30)
            raised = jnp.exp(scores - jnp.max(scores, axis=0, keepdims=True))
            probs = (raised * (1.0 / jnp.sum(raised, axis=0, keepdims=True))).astype(BF)
            out_probs[2 * pair + which] = probs
            term = mm(probs, half_mask(value[:, at], which), TN)
            total = term if total is None else total + term
        mixed.append(total.astype(BF))
    out_probs.start()
    att = jnp.concatenate(mixed, axis=1)
    out_att[...] = att
    return att


def attention_kernel(layer, chain, meta, *refs):
    if layer == 0:
        x_ref, *vecs = refs[:3]
        refs = refs[3:]
    else:
        feed_own, feed_got, hidden, *vecs = refs[:5]
        refs = refs[5:]
    own_q, got_q, own_o, got_o, *refs, wq, wo, sems = refs
    if layer == 0:
        out_qkv, out_probs, out_att, out_branch = refs
    else:
        out_x, out_x_saved, out_r2, out_qkv, out_probs, out_att, out_branch = refs
    length, tag = meta.length(chain), meta.tag(chain)
    is_own = meta.section == layer
    vector = vec_reader(vecs, is_own, tag)
    wq = Weights(own_q, got_q, is_own, [(j, (tag, j), j) for j in range(3)], wq, sems)
    wo = Weights(own_o, got_o, is_own, [(0, tag, None)], wo, sems, 3)
    if layer == 0:
        x = x_ref[...]
    else:
        before = vec_reader(vecs, meta.section == 0, tag)
        r2 = hidden[...] + ((feed_own[...].astype(F32) + feed_got[...].astype(F32)) + before(SHIFT[2]))
        out_r2[...] = r2
        normed, _ = layer_norm(r2)
        x = (normed * before(GAIN_TWO) + before(SHIFT[3])).astype(BF)
        out_x[...] = x
        out_x_saved[...] = x
    att = attend(x, vector, length, wq, out_qkv, out_probs, out_att)
    out_branch[...] = mm(att, wo()[...]).astype(BF)


def feed_kernel(layer, chain, meta, x, own, got, *refs):
    *vecs, own_i, got_i, own_d, got_d = refs[:6]
    *_, out_hidden, out_r1, out_slope, out_act, out_low, out_feed, act, wi, wd, low_rows, sems = refs[6:]
    span = x.shape[0]
    tag = meta.tag(chain)
    is_own = meta.section == layer
    wi = Weights(own_i, got_i, is_own, in_halves(tag, 1), wi, sems)
    wd = Weights(own_d, got_d, is_own, [(0, tag, None)], wd, sems, 2)
    vector = vec_reader(vecs, is_own, tag)
    branch = (own[...].astype(F32) + got[...].astype(F32)) + vector(SHIFT[0])
    r1 = x[...].astype(F32) + branch
    out_r1[...] = r1
    normed, _ = layer_norm(r1)
    hidden = normed * vector(GAIN_ONE) + vector(SHIFT[1])
    out_hidden[...] = hidden
    low = hidden.astype(BF)
    low_rows[...] = low
    low_copy = pltpu.make_async_copy(low_rows, out_low.at[pl.ds(chain * span, span)], sems.at[3])
    low_copy.start()
    for half in range(2):
        at = half * HALF
        pre = mm(low, wi(half)[:, at : at + HALF]) + vector(BIAS_IN + at, HALF)
        act[:, at : at + HALF], out_slope[:, at : at + HALF] = gelu_and_slope(pre)

        @pl.when(meta.rep == half)
        def _():
            out_act[:, :] = act[:, at : at + HALF]

    out_act.start()
    out_slope.start()
    out_feed[...] = mm(act[...], wd()[...]).astype(BF)
    low_copy.wait()


def feed_back_kernel(layer, chain, meta, own, got, *refs):
    first, second, *vecs, act_slope, own_i, got_i, own_d, got_d = refs[:9]
    out_y, out_dr2, out_df, out_du, out_dh, out_vec, du_all, wi, wd, sems = refs[9:]
    length, tag = meta.length(chain), meta.tag(chain)
    is_own = meta.section == layer
    wd = Weights(own_d, got_d, is_own, in_halves(tag, 0), wd, sems)
    wi = Weights(own_i, got_i, is_own, [(0, tag, None)], wi, sems, 2)
    vector = vec_reader(vecs, is_own, tag)
    gain = vector(GAIN_TWO)
    both = own[...].astype(F32) + got[...].astype(F32)
    if layer == 1:
        hidden, cotangent = first, second
        normed, inverse = layer_norm(hidden[...] + (both + vector(SHIFT[2])))
        out_y[...] = (normed * gain + vector(SHIFT[3])).astype(BF)
        tokens = lax.broadcasted_iota(jnp.int32, both.shape, 0)
        dy = jnp.where(tokens < length, cotangent[...].astype(F32), 0.0)
    else:
        dr1, r2 = first, second
        low = (both + dr1[...]).astype(BF)
        out_y[...] = low
        dy = low.astype(F32)
        normed, inverse = layer_norm(r2[...])
    dr2 = layer_norm_back(dy, gain, normed, inverse)
    out_dr2[...] = dr2
    df = dr2.astype(BF)
    out_df[...] = df
    out_vec[:, 0:768] = column_sum(dy * normed)
    out_vec[:, 768:1536] = column_sum(dr2)
    out_vec[:, 1536:2304] = column_sum(dy)
    for half in range(2):
        at = half * HALF
        du = mm(df, wd(half)[at : at + HALF, :], NT) * act_slope[:, at : at + HALF].astype(F32)
        out_vec[:, 2304 + at : 2304 + at + HALF] = column_sum(du)
        du_all[:, at : at + HALF] = du.astype(BF)

        @pl.when(meta.rep == half)
        def _():
            out_du[:, :] = du_all[:, at : at + HALF]

    out_du.start()
    out_dh[...] = mm(du_all[...], wi()[...], NT).astype(BF)


def attention_back_kernel(layer, chain, meta, own, got, dr2, r1, *refs):
    *vecs, qkv, probs_ref, own_q, got_q, own_o, got_o = refs[:8]
    out_dr1, out_dz, out_dqkv, out_dx, out_vec, wq, wo, sems = refs[8:]
    tag = meta.tag(chain)
    is_own = meta.section == layer
    wo = Weights(own_o, got_o, is_own, [(0, tag, None)], wo, sems, 3)
    wq = Weights(own_q, got_q, is_own, [(j, (tag, j), j) for j in range(3)], wq, sems)
    vector = vec_reader(vecs, is_own, tag)
    dh = (own[...].astype(F32) + got[...].astype(F32)) + dr2[...]
    normed, inverse = layer_norm(r1[...])
    dr1 = layer_norm_back(dh, vector(GAIN_ONE), normed, inverse)
    out_dr1[...] = dr1
    dz = dr1.astype(BF)
    out_dz[...] = dz
    out_vec[:, 0:768] = column_sum(dh * normed)
    out_vec[:, 768:1536] = column_sum(dr1)
    out_vec[:, 1536:2304] = column_sum(dh)
    datt = mm(dz, wo()[...], NT).astype(BF)
    query, key, value = (qkv[:, j * LOCAL : (j + 1) * LOCAL] for j in range(3))
    for pair in range(LOCAL // 128):
        at = slice(pair * 128, pair * 128 + 128)
        dv = dq = dk = None
        for which in range(2):
            probs = probs_ref[2 * pair + which]
            dv_term = mm(probs, half_mask(datt[:, at], which))
            dprobs = mm(half_mask(value[:, at], which), datt[:, at], NT)
            wide = probs.astype(F32)
            dscores = wide * (dprobs - jnp.sum(wide * dprobs, axis=0, keepdims=True))
            dscores = dscores.astype(BF)
            dk_term = mm(dscores, half_mask(query[:, at], which))
            dq_term = mm(dscores, half_mask(key[:, at], which), TN)
            dv = dv_term if dv is None else dv + dv_term
            dk = dk_term if dk is None else dk + dk_term
            dq = dq_term if dq is None else dq + dq_term
        dq = dq * 0.125
        dk = dk * 0.125
        low = pair * 128
        out_vec[:, 2304 + low : 2304 + low + 128] = column_sum(dq)
        out_vec[:, 2688 + low : 2688 + low + 128] = column_sum(dv)
        out_dqkv[:, low : low + 128] = dq.astype(BF)
        out_dqkv[:, LOCAL + low : LOCAL + low + 128] = dk.astype(BF)
        out_dqkv[:, 2 * LOCAL + low : 2 * LOCAL + low + 128] = dv.astype(BF)
    out_dqkv.start()
    dx = None
    for j in range(3):
        term = mm(out_dqkv[:, j * LOCAL : (j + 1) * LOCAL], wq(j)[j], NT)
        dx = term if dx is None else dx + term
    out_dx[...] = dx.astype(BF)


def far_kernel(layer, chains, meta, *refs):
    low, *vecs, own_i, got_i, out_act, out_slope, wi, sems = refs
    span = low.shape[0] // chains
    is_own = meta.section == layer
    half = pl.ds(pl.multiple_of(meta.rep * HALF, HALF), HALF)
    wi = Weights(own_i, got_i, is_own, [(0, (slice(None), slice(None), half), None)], wi, sems)()
    for chain in range(chains):
        tag = meta.far_tag(chain)
        at = slice(chain * span, (chain + 1) * span)
        bias = vec_reader(vecs, is_own, tag)(pl.multiple_of(BIAS_IN + meta.rep * HALF, HALF), HALF)
        pre = mm(low[at, :], wi[tag]) + bias
        out_act[at, :], out_slope[at, :] = gelu_and_slope(pre)


def order_of(tags, section):
    mine = [(tag == section).astype(jnp.int32) for tag in tags]
    count = sum(mine)
    places, before = [], 0
    for index, one in enumerate(mine):
        places.append(jnp.where(one == 1, before, count + index - before))
        before = before + one
    return places, count


class Gathered:
    def __init__(self, sources, places, target, sems, first):
        self.place, self.copies = target, []
        for index, (source, place) in enumerate(zip(sources, places)):
            extent = source.shape[0]
            at = pl.ds(pl.multiple_of(place * extent, extent), extent)
            copy = pltpu.make_async_copy(source, target.at[at], sems.at[first + index])
            copy.start()
            self.copies.append(copy)

    def wait(self):
        for copy in self.copies:
            copy.wait()
        return self.place


def both_models(count, chains, span, left, rights, stores):
    def branch(number):
        def products():
            cut = number * span
            for right, store in zip(rights, stores):
                columns = right.shape[1]
                for keeping, rows in ((False, slice(cut, chains * span)), (True, slice(0, cut))):
                    if rows.start == rows.stop:
                        store(keeping, jnp.zeros((left.shape[0], columns), BF))
                    else:
                        store(keeping, mm(left[:, rows], right[rows, :]).astype(BF))

        return products

    for number in range(chains + 1):
        pl.when(count == number)(branch(number))


def feed_grad_kernel(layer, chains, meta, *refs):
    df, act, du, far_df = (refs[i * chains : (i + 1) * chains] for i in range(4))
    low, far_low, far_act, slope_from, own_d, got_d, *refs = refs[4 * chains :]
    keep, send, df_all, act_all, low_all, du_all, far_slope, wd, sems = refs
    span = df[0].shape[0]
    half = pl.ds(pl.multiple_of(meta.rep * HALF, HALF), HALF)
    is_own = meta.section == layer
    tags = [meta.tag(chain) for chain in range(chains)] + [meta.far_tag(chain) for chain in range(chains)]
    places, count = order_of(tags, meta.section)
    split = lambda rows: [rows.at[pl.ds(chain * span, span)] for chain in range(chains)]
    df_all = Gathered([*df, *far_df], places, df_all, sems, 0)
    act_all = Gathered([*act, *split(far_act)], places, act_all, sems, 2 * chains)
    wd = Weights(own_d, got_d, is_own, [(0, (slice(None), half), None)], wd, sems, 8 * chains)
    far_slope = Lazy(slope_from, far_slope, sems, 8 * chains + 1, 1)
    far_slope.start()
    du_all = Gathered(du, places, du_all, sems, 4 * chains)
    low_all = Gathered([*split(low), *split(far_low)], places, low_all, sems, 6 * chains)

    def products(left_all, at, right):
        def column_block(index, carry):
            rows = pl.ds(pl.multiple_of(index * BLOCK, BLOCK), BLOCK)
            left = left_all[:, rows].T

            def store(keeping, value):
                out = keep.place if keeping else send
                out[rows, at : at + HALF] = value

            both_models(count, 2 * chains, span, left, [right], [store])
            return carry

        lax.fori_loop(0, WIDTH // BLOCK, column_block, 0)
        keep.start(at // HALF)

    lefts = df_all.wait()
    products(lefts, 0, act_all.wait())
    rights = du_all.wait()
    weights = wd()
    for chain in range(chains):
        at = slice(chain * span, (chain + 1) * span)
        there = pl.ds(pl.multiple_of(places[chains + chain] * span, span), span)
        value = mm(lefts[there, :], weights[meta.far_tag(chain)], NT) * far_slope[at, :].astype(F32)
        rights[there, :] = value.astype(BF)
    products(low_all.wait(), HALF, rights)


def attention_grad_kernel(layer, chains, meta, *refs):
    dz, att, x, dqkv = (refs[i * chains : (i + 1) * chains] for i in range(4))
    keep, send, dz_all, att_all, x_all, dqkv_all, sems = refs[4 * chains :]
    span = dz[0].shape[0]
    if layer == 0:
        x = [ref.at[chain, meta.section] for chain, ref in enumerate(x)]
    places, count = order_of([meta.tag(chain) for chain in range(chains)], meta.section)
    dz_all = Gathered(dz, places, dz_all, sems, 0)
    att_all = Gathered(att, places, att_all, sems, chains)
    x_all = Gathered(x, places, x_all, sems, 2 * chains)
    dqkv_all = Gathered(dqkv, places, dqkv_all, sems, 3 * chains)
    first = jnp.where(meta.rep == 0, 0, 1)

    def products(left_all, rights, targets):
        def column_block(index, carry):
            rows = pl.ds(pl.multiple_of(index * BLOCK, BLOCK), BLOCK)
            left = left_all[:, rows].T

            def store_at(slot, columns):
                def store(keeping, value):
                    out = keep.place if keeping else send
                    out[slot, rows, columns] = value

                return store

            both_models(count, chains, span, left, rights, [store_at(*target) for target in targets])
            return carry

        lax.fori_loop(0, WIDTH // BLOCK, column_block, 0)

    left_all, right = dz_all.wait(), att_all.wait()
    products(left_all, [right], [(first, slice(0, LOCAL))])
    left_all, right = x_all.wait(), dqkv_all.wait()
    rights = [right.at[:, pl.ds(0, LOCAL)], right.at[:, pl.ds(LOCAL, 2 * LOCAL)]]
    products(left_all, rights, [(first, slice(LOCAL, HALF)), (1 - first, slice(0, HALF))])


def add_kernel(parts, meta, one, two, out):
    block = one.shape[0] // parts
    for part in range(parts):
        at = slice(part * block, (part + 1) * block)
        one.wait(part)
        out[at, :] = one.place[at, :] + two[at, :]
        out.start(part)


def add_halves_kernel(meta, one, two, near, far):
    for half, out in ((1, far), (0, near)):
        one.wait(half)
        out[...] = one.place[half] + two[half]


BLOCK = 256
ANY = pl.BlockSpec(memory_space=pl.ANY)


def pack_kernel(gains, shifts, b_qv, b_in, out):
    for model in range(2):
        row = slice(model, model + 1)
        for j in range(2):
            out[row, j * WIDTH : (j + 1) * WIDTH] = gains[0, model, j : j + 1, :]
            out[row, BIAS_Q + j * LOCAL : BIAS_Q + (j + 1) * LOCAL] = b_qv[0, model, j : j + 1, :]
        for j in range(4):
            out[row, SHIFT[j] : SHIFT[j] + WIDTH] = shifts[0, model, j : j + 1, :]
        out[row, BIAS_IN:] = b_in[0, row, :]


def feed_final_kernel(meta, *refs):
    zero, one, got, grad_in, grad_out = refs[:2], refs[2:4], refs[4], refs[5], refs[6]
    for half in range(2):
        local = jnp.where(meta.rep == 0, half, 1 - half)
        mine = jnp.where(meta.section == 0, zero[half][...], one[half][...]).astype(F32)
        columns = pl.ds(pl.multiple_of(local * HALF, HALF), HALF)
        for model, shard in ((meta.section, mine), (1 - meta.section, got[half].astype(F32))):
            grad_out[model, :, columns] = shard[:, 0:HALF]
            grad_in[model, :, columns] = shard[:, HALF:]


def attention_final_kernel(meta, *refs):
    zero, one, got_zero, got_one, (grad_qkv, grad_o) = refs[:2], refs[2:4], refs[4:6], refs[6:8], refs[8:]
    for model, zeros, ones in ((meta.section, zero, one), (1 - meta.section, got_zero, got_one)):
        near, far = [jnp.where(meta.section == 0, zeros[half][...], ones[half][...]).astype(F32) for half in range(2)]
        low = jnp.where(meta.rep == 0, near, far)
        high = jnp.where(meta.rep == 0, far, near)
        grad_o[model] = low[:, 0:LOCAL]
        grad_qkv[model, 0] = low[:, LOCAL:]
        grad_qkv[model, 1] = high[:, 0:LOCAL]
        grad_qkv[model, 2] = high[:, LOCAL:]


def vector_grad_kernel(chains, meta, *refs):
    out = refs[-1]
    for layer in range(2):
        ones = refs[2 * layer * chains : (2 * layer + 1) * chains]
        twos = refs[(2 * layer + 1) * chains : (2 * layer + 2) * chains]
        rows = [
            jnp.concatenate(
                [one[:, 0:768], two[:, 0:768], one[:, 768:2304], two[:, 768:2304], one[:, 2304:], two[:, 2304:]],
                axis=1,
            )
            for one, two in zip(ones, twos)
        ]
        for model in range(2):
            total = None
            for chain in range(chains):
                row = jnp.where(meta.tag(chain) == model, rows[chain], 0.0)
                total = row if total is None else total + row
            out[layer, model : model + 1, :] = total


STEP = 1.5e9
LONG = 8

VMEM = pl.BlockSpec(memory_space=pltpu.VMEM)
SMEM = pl.BlockSpec(memory_space=pltpu.SMEM)
SAVED, PARTLY = "saved", "partly"


def pieces_of(out):
    return out[3] if len(out) > 3 else [None]


def in_hbm(value):
    return pltpu.with_memory_space_constraint(value, pltpu.HBM)


def call(body, scalars, operands, outs, scratch, name, grant, cost):
    saved_in = [value for value in operands if isinstance(value, Saved)]
    saved_out = [out for out in outs if SAVED in out]
    buffers = [pltpu.VMEM(value.shape, value.value.dtype) for value in saved_in]
    buffers += [pltpu.VMEM(out[0], out[1]) for out in saved_out]
    counts = (len(scalars), len(operands), len(outs), len(scratch))

    def kernel(*refs):
        groups = []
        for count in counts:
            groups.append(refs[:count])
            refs = refs[count:]
        numbers, ins, results, own_scratch = groups
        *places, sems = refs
        meta = Scalars(*numbers)
        given, taken, index, sem = [], [], 0, 0
        for value, ref in zip(operands, ins):
            if isinstance(value, Saved):
                source = ref if value.chain is None else ref.at[value.chain, meta.section]
                ref = Lazy(source, places[index], sems, sem, value.parts)
                ref.start()
                sem += value.parts
                index += 1
            given.append(ref)
        for out, ref in zip(outs, results):
            if SAVED in out:
                ref = Leaving(places[index], ref, sems, sem, pieces_of(out))
                sem += len(pieces_of(out))
                index += 1
            taken.append(ref)
        body(meta, *given, *taken, *own_scratch)
        for ref in taken:
            if isinstance(ref, Leaving):
                ref.start()
        for ref in given:
            if isinstance(ref, Lazy):
                ref.wait()
        for ref in taken:
            if isinstance(ref, Leaving):
                ref.wait()

    in_specs = [ANY if isinstance(value, (tuple, Saved)) else VMEM for value in operands]
    values = []
    for value in operands:
        if isinstance(value, Saved):
            value = in_hbm(value.value)
        elif isinstance(value, tuple):
            value = in_hbm(value[0])
        values.append(value)
    shapes = [
        pltpu.HBM(*out[:2]) if SAVED in out or PARTLY in out else jax.ShapeDtypeStruct(*out[:2]) for out in outs
    ]
    return pl.pallas_call(
        kernel,
        out_shape=shapes,
        in_specs=[SMEM] * len(scalars) + in_specs,
        out_specs=[ANY if SAVED in out or PARTLY in out else VMEM for out in outs],
        input_output_aliases={
            len(scalars) + out[3]: index for index, out in enumerate(outs) if PARTLY in out and len(out) > 3
        },
        scratch_shapes=[*scratch, *buffers, pltpu.SemaphoreType.DMA((max(sum(value.parts for value in saved_in) + sum(len(pieces_of(out)) for out in saved_out), 1),))],
        compiler_params=pltpu.CompilerParams(vmem_limit_bytes=grant * 1024 * 1024),
        cost_estimate=pl.CostEstimate(flops=int(cost * STEP), bytes_accessed=1, transcendentals=0),
        name=name,
    )(*scalars, *values)


def on_device(
    block_input, cotangent, lengths, tags, w_qkv, w_o, w_in, w_out, b_qv, b_in, gains, shifts
):
    micro, per, span, width = block_input.shape
    section = lax.axis_index("section")
    rep = lax.axis_index("rep")
    chains = range(micro)
    layers = range(2)

    own_q, own_o, own_i, own_d = w_qkv[0], w_o[0], w_in[0], w_out[0]
    got_q = swap(own_q, "section")
    vec_own = pl.pallas_call(
        pack_kernel, out_shape=jax.ShapeDtypeStruct((2, PACKED), F32), in_specs=[VMEM] * 4, out_specs=VMEM, name="pack"
    )(gains, shifts, b_qv, b_in)
    numbers = jnp.concatenate([lengths, tags], axis=1)
    vec_own = after(vec_own, numbers)
    vecs = [vec_own, swap(vec_own, "section")]
    got_o = swap(own_o, "section")
    later = lax.optimization_barrier((own_i, own_d, got_q, got_o, vecs[1]))
    got_i, got_d = swap(later[0], "section"), swap(later[1], "section")

    heads = LOCAL // HD
    row, saved_row = ((span, WIDTH), BF), ((span, WIDTH), BF, SAVED)
    wide, saved_wide = ((span, WIDTH), F32), ((span, WIDTH), F32, SAVED)
    half_row, long_row = ((span, HALF), BF, SAVED), ((span, HIDDEN), BF, SAVED)
    qkv_row = ((span, 3 * LOCAL), BF, SAVED)
    att_outs = [qkv_row, ((heads, span, span), BF, SAVED), ((span, LOCAL), BF, SAVED), row]
    raw = lambda values: [(value,) for value in values]
    w_qo, w_id = raw([own_q, got_q, own_o, got_o]), raw([own_i, got_i, own_d, got_d])
    qo_scratch = [
        pltpu.VMEM((3, WIDTH, LOCAL), BF),
        pltpu.VMEM((LOCAL, WIDTH), BF),
        pltpu.SemaphoreType.DMA((4,)),
    ]
    id_scratch = [
        pltpu.VMEM((span, HIDDEN), BF),
        pltpu.VMEM((WIDTH, HIDDEN), BF),
        pltpu.VMEM((HIDDEN, WIDTH), BF),
        pltpu.SemaphoreType.DMA((3,)),
    ]
    feed_scratch = id_scratch[:3] + [pltpu.VMEM((span, WIDTH), BF), pltpu.SemaphoreType.DMA((4,))]

    last = [numbers]

    def run(body, operands, outs, scratch, name, *waits, far=False, grant=14, cost=1):
        scalars = [after(numbers, last[0], *waits)] + ([far_tags] if far else [])
        results = call(body, scalars, operands, outs, scratch, name, grant, cost)
        last[0] = results[-1]
        return results

    def saved(values):
        return [Saved(value) for value in values]

    def arrived(pair):
        return [pair[0], Saved(pair[1])]

    def owned(zero, one):
        zero, one = jnp.stack(zero), jnp.stack(one)
        mine = jnp.where(section == 0, zero, one)
        other = swap(jnp.where(section == 0, one, zero), "section")
        core = lax.broadcasted_iota(jnp.int32, (micro, per, span, width), 1)
        return jnp.where(core == section, mine[:, None], other[:, None])[None]

    table = lambda: [[None] * micro for _ in layers]
    r1s, r2s, hiddens, acts, slopes, feeds, qkvs, probs, atts = (table() for _ in range(9))
    lows, far_lows = [None, None], [None, None]
    x_now, x_saved = [[Saved(block_input, chain) for chain in chains], [None] * micro], [None] * micro
    for layer in layers:
        for chain in chains:
            body = functools.partial(attention_kernel, layer, chain)
            name = f"attention{layer}{chain}"
            if layer == 0:
                got = run(body, [x_now[0][chain], *vecs] + w_qo, att_outs, qo_scratch, name)
            else:
                operands = [*arrived(feeds[0][chain]), hiddens[0][chain], *vecs] + w_qo
                waits = []
                x_now[1][chain], x_saved[chain], r2s[0][chain], *got = run(
                    body, operands, [row, saved_row, saved_wide] + att_outs, qo_scratch, name, *waits
                )
            qkvs[layer][chain], probs[layer][chain], atts[layer][chain], branch = got
            feeds[layer][chain] = (branch, swap(branch, "mp"))
        if layer == 0:
            far_tags = swap(after(tags, last[0]), "rep")
        for chain in chains:
            body = functools.partial(feed_kernel, layer, chain)
            waits = [far_tags] if layer == 0 and chain == 2 else []
            operands = [x_now[layer][chain], *feeds[layer][chain], *vecs] + w_id
            rows_out = ((micro * span, WIDTH), BF, PARTLY)
            if chain:
                rows_out += (len(operands),)
                operands.append((lows[layer],))
            hiddens[layer][chain], r1s[layer][chain], slopes[layer][chain], acts[layer][chain], lows[layer], part = run(
                body,
                operands,
                [wide, saved_wide, long_row, half_row, rows_out, row],
                feed_scratch,
                f"feed{layer}{chain}",
                *waits,
            )
            feeds[layer][chain] = (part, swap(part, "mp"))
        far_lows[layer] = swap(lows[layer], "rep")

    rows = micro * span
    far_rows = ((rows, HALF), BF, SAVED)
    dr2s, dfs, far_dfs, dus, dhs, vec_one, vec_two, dzs, dqkvs, dr1s, dxs, ys = (table() for _ in range(12))
    far_hidden = [None, None]

    def feed_back(layer, chain, *waits, cost=1):
        if layer == 1:
            operands = [*arrived(feeds[1][chain]), hiddens[1][chain], Saved(cotangent, chain)]
        else:
            operands = [*arrived(dxs[1][chain]), Saved(dr1s[1][chain]), Saved(r2s[0][chain])]
        ys[layer][chain], dr2s[layer][chain], df, dus[layer][chain], dh, vec_two[layer][chain] = run(
            functools.partial(feed_back_kernel, layer, chain),
            operands + [*vecs, Saved(slopes[layer][chain])] + w_id,
            [saved_row, saved_wide, saved_row, half_row, row, ((1, 3 * WIDTH + HIDDEN), F32, SAVED)],
            id_scratch,
            f"feed_back{layer}{chain}",
            *waits,
            cost=cost,
        )
        dfs[layer][chain], far_dfs[layer][chain] = df, swap(df, "rep")
        dhs[layer][chain] = (dh, swap(dh, "mp"))

    def attention_back(layer, chain, *waits, cost=1):
        dr1s[layer][chain], dzs[layer][chain], dqkvs[layer][chain], dx, vec_one[layer][chain] = run(
            functools.partial(attention_back_kernel, layer, chain),
            [*arrived(dhs[layer][chain]), Saved(dr2s[layer][chain]), Saved(r1s[layer][chain]), *vecs]
            + [Saved(qkvs[layer][chain]), Saved(probs[layer][chain])]
            + w_qo,
            [saved_wide, saved_row, qkv_row, row, ((1, 3 * WIDTH + 2 * LOCAL), F32, SAVED)],
            qo_scratch,
            f"attention_back{layer}{chain}",
            *waits,
            cost=cost,
        )
        dxs[layer][chain] = (dx, swap(dx, "mp"))

    def far_part(layer, *waits):
        far_hidden[layer] = run(
            functools.partial(far_kernel, layer, micro),
            [Saved(far_lows[layer]), *vecs] + w_id[:2],
            [far_rows] * 2,
            [pltpu.VMEM((2, WIDTH, HALF), BF), pltpu.SemaphoreType.DMA((1,))],
            f"far{layer}",
            *waits,
            far=True,
            cost=1.5,
        )

    def feed_grad(layer, *waits, cost=2):
        near = dfs[layer] + acts[layer] + dus[layer] + far_dfs[layer]
        far_act, far_slope = far_hidden[layer]
        stacked = pltpu.VMEM((2 * rows, HALF), BF)
        keep, send = run(
            functools.partial(feed_grad_kernel, layer, micro),
            raw(near + [lows[layer], far_lows[layer], far_act, far_slope]) + w_id[2:],
            [((WIDTH, HIDDEN), BF, SAVED, blocks_of(WIDTH, HIDDEN, WIDTH, HALF)), ((WIDTH, HIDDEN), BF)],
            [stacked] * 4
            + [pltpu.VMEM((rows, HALF), BF), pltpu.VMEM((2, HALF, WIDTH), BF), pltpu.SemaphoreType.DMA((8 * micro + 2,))],
            f"feed_grad{layer}",
            *waits,
            far=True,
            grant=20,
            cost=cost,
        )
        return keep, swap(send, "section")

    def feed_grad_sum(layer, parts, *waits):
        (result,) = run(
            functools.partial(add_kernel, WIDTH // BLOCK),
            [Saved(parts[0], parts=WIDTH // BLOCK), parts[1]],
            [((WIDTH, HIDDEN), BF, SAVED, blocks_of(WIDTH, HIDDEN, BLOCK, HIDDEN))],
            [],
            f"feed_grad_sum{layer}",
            *waits,
        )
        return result

    def attention_grad(layer, *waits):
        x_part = raw([block_input] * micro if layer == 0 else x_saved)
        narrow, stacked = pltpu.VMEM((rows, LOCAL), BF), pltpu.VMEM((rows, WIDTH), BF)
        keep, send = run(
            functools.partial(attention_grad_kernel, layer, micro),
            raw(dzs[layer] + atts[layer]) + x_part + raw(dqkvs[layer]),
            [((2, WIDTH, HALF), BF, SAVED, [pl.ds(0, 1), pl.ds(1, 1)]), ((2, WIDTH, HALF), BF)],
            [stacked, narrow, stacked, pltpu.VMEM((rows, 3 * LOCAL), BF), pltpu.SemaphoreType.DMA((4 * micro,))],
            f"attention_grad{layer}",
            *waits,
            cost=2,
        )
        return keep, swap(send, "section")

    def attention_grad_sum(layer, parts, *waits):
        near, far = run(
            add_halves_kernel,
            [Saved(parts[0], parts=2), parts[1]],
            [((WIDTH, HALF), BF, SAVED)] * 2,
            [],
            f"attention_grad_sum{layer}",
            *waits,
        )
        return near, swap(far, "rep")

    def scattered(part):
        return lax.psum_scatter(part, "dp", scatter_dimension=0, tiled=True)

    feed_back(1, 0, far_lows[0])
    feed_back(1, 1)
    feed_back(1, 2, cost=3)
    far_part(1, dhs[1][0][1], far_dfs[1][0])
    parts = feed_grad(1, dhs[1][1][1], far_dfs[1][1])
    attention_back(1, 0, dhs[1][2][1], cost=20)
    feed_one = scattered(feed_grad_sum(1, parts))
    attention_back(1, 1)
    attention_back(1, 2, dxs[1][0][1])
    parts = attention_grad(1, dxs[1][1][1])
    far_part(0)
    near, far = attention_grad_sum(1, parts)
    feed_back(0, 0)
    feed_back(0, 1, dxs[1][2][1], cost=0.1)
    feed_back(0, 2, dhs[0][0][1], cost=0.1)
    attention_one = after(near, last[0]) + far
    layer_outputs = owned(after(x_saved, last[0]), ys[1])
    attention_back(0, 0, attention_one, layer_outputs)
    attention_one = scattered(after(attention_one, feed_one))
    feed_one = (feed_one, swap(feed_one, "rep"))
    parts = feed_grad(0, dhs[0][2][1], cost=14.5)
    attention_back(0, 1, attention_one, feed_one[1], cost=30)
    feed_zero = feed_grad_sum(0, parts)
    feed_zero = scattered(after(feed_zero, attention_one))
    attention_back(0, 2)
    (both,) = run(
        functools.partial(vector_grad_kernel, micro),
        saved(vec_one[0] + vec_two[0] + vec_one[1] + vec_two[1]),
        [((2, 2, PACKED), F32)],
        [],
        "vector_grad",
    )
    both = both + swap(both, "section")
    both = lax.dynamic_index_in_dim(both, section, 0, keepdims=False)
    parts = attention_grad(0, both)
    both = both + swap(both, "rep")
    near, far = attention_grad_sum(0, parts, both)
    both = after(both, near)
    data = lax.axis_size("dp")
    distance = 1
    while distance < data:
        both = both + lax.ppermute(both, "dp", [(i, i ^ distance) for i in range(data)])
        distance *= 2
    firsts = [
        ((after(dx[0], near, feed_zero, both).astype(F32) + dx[1].astype(F32)) + dr1).astype(BF) for dx, dr1 in zip(dxs[0], dr1s[0])
    ]
    attention_zero = after(after(near, firsts) + far, feed_zero)
    done = attention_zero
    feed_zero = (feed_zero, swap(after(feed_zero, done), "rep"))
    attention_one = (attention_one, swap(after(attention_one, both), "rep"))
    grad_gains = both[:, : SHIFT[0]].reshape(2, 2, WIDTH)
    grad_shifts = both[:, SHIFT[0] : BIAS_Q].reshape(2, 4, WIDTH)
    grad_b_qv = both[:, BIAS_Q:BIAS_IN].reshape(2, 2, LOCAL)
    grad_b_in = both[:, BIAS_IN:]
    attention_zero = scattered(attention_zero)

    def handed(zero, one):
        return swap(jnp.where(section == 0, jnp.stack(one), jnp.stack(zero)), "section")

    shard = feed_zero[0].shape[0]
    grad_in, grad_out = run(
        feed_final_kernel,
        [*feed_zero, *feed_one, handed(feed_zero, feed_one)],
        [((2, shard, HIDDEN), F32)] * 2,
        [],
        "feed_final",
    )
    input_grads = owned(after(firsts, done), ys[0])
    got_one = [swap(part, "section") for part in attention_one]
    attention_zero = after(attention_zero, input_grads, got_one)
    vectors = grad_b_qv[None], grad_b_in[None], grad_gains[None], grad_shifts[None]
    far, vectors, _ = lax.optimization_barrier((swap(attention_zero, "rep"), vectors, grad_in))
    got_zero = swap(attention_zero, "section"), swap(far, "section")
    attention_zero = (attention_zero, far)
    grad_qkv, grad_o = run(
        attention_final_kernel,
        [*attention_zero, *attention_one, *got_zero, *got_one],
        [((2, 3, shard, LOCAL), F32), ((2, shard, LOCAL), F32)],
        [],
        "attention_final",
    )
    grad_out, grad_o = jnp.swapaxes(grad_out, 1, 2), jnp.swapaxes(grad_o, 1, 2)

    return (
        layer_outputs,
        input_grads,
        grad_qkv[None],
        grad_o[None],
        grad_in[None],
        grad_out[None],
        *vectors,
    )


def solution(mesh):
    in_specs = (
        P(None, ("dp", "rep"), None, None),
        P(None, ("dp", "rep"), None, None),
        P(None, ("dp", "rep")),
        P(None, ("dp", "rep")),
        P("section", None, None, None, "mp"),
        P("section", None, "mp", None),
        P("section", None, None, "mp"),
        P("section", None, "mp", None),
        P("section", None, None, "mp"),
        P("section", None, "mp"),
        P("section", None, None, None),
        P("section", None, None, None),
    )
    out_specs = (
        P("section", None, ("dp", "rep"), None, None),
        P("section", None, ("dp", "rep"), None, None),
        P("section", None, None, "dp", "mp"),
        P("section", None, "mp", "dp"),
        P("section", None, "dp", "mp"),
        P("section", None, "mp", "dp"),
        P("section", None, None, "mp"),
        P("section", None, "mp"),
        P("section", None, None, None),
        P("section", None, None, None),
    )
    return jax.shard_map(
        on_device, mesh=mesh, in_specs=in_specs, out_specs=out_specs, check_vma=False
    )
```

```python
import functools

import jax
import jax.numpy as jnp
from jax import lax
from jax.experimental import pallas as pl
from jax.experimental.pallas import tpu as pltpu
from jax.sharding import PartitionSpec as P

HD = 64
EPS = 1e-05
BF = jnp.bfloat16
F32 = jnp.float32

GAIN_ONE, GAIN_TWO = 0, 768
SHIFT = (1536, 2304, 3072, 3840)
BIAS_Q, BIAS_V, BIAS_IN = 4608, 4992, 5376
PACKED = 6912
WIDTH, LOCAL, HIDDEN, HALF = 768, 384, 1536, 768

NN = (((1,), (0,)), ((), ()))
NT = (((1,), (1,)), ((), ()))
TN = (((0,), (0,)), ((), ()))


def mm(left, right, dims=NN):
    return lax.dot_general(left, right, dims, preferred_element_type=F32)


def swap(block, axis):
    return lax.ppermute(block, axis, [(0, 1), (1, 0)])


def after(value, *others):
    return lax.optimization_barrier((value, *others))[0]


class Lazy:
    def __init__(self, source, place, sems, first, parts):
        self.place, self.waited, self.copies = place, set(), []
        extent = place.shape[0] // parts
        for part in range(parts):
            at = pl.ds(part * extent, extent)
            near, away = (place, source) if parts == 1 else (place.at[at], source.at[at])
            self.copies.append(pltpu.make_async_copy(away, near, sems.at[first + part]))

    shape = property(lambda self: self.place.shape)

    def start(self):
        for copy in self.copies:
            copy.start()

    def wait(self, part=None):
        for index in range(len(self.copies)) if part is None else (part,):
            if index not in self.waited:
                self.copies[index].wait()
                self.waited.add(index)

    def __getitem__(self, at):
        self.wait()
        return self.place[at]


class Leaving:
    def __init__(self, place, target, sems, first, pieces):
        self.place, self.started, self.copies = place, set(), []
        for index, at in enumerate(pieces):
            near, away = (place, target) if at is None else (place.at[at], target.at[at])
            self.copies.append(pltpu.make_async_copy(near, away, sems.at[first + index]))

    shape = property(lambda self: self.place.shape)

    def start(self, piece=None):
        for index in range(len(self.copies)) if piece is None else (piece,):
            if index not in self.started:
                self.copies[index].start()
                self.started.add(index)

    def wait(self):
        for copy in self.copies:
            copy.wait()

    def __getitem__(self, at):
        return self.place[at]

    def __setitem__(self, at, value):
        self.place[at] = value
        if at is Ellipsis:
            self.start()


def blocks_of(rows, columns, row_step, column_step):
    return [
        (pl.ds(row, row_step), pl.ds(column, column_step))
        for column in range(0, columns, column_step)
        for row in range(0, rows, row_step)
    ]


class Saved:
    def __init__(self, value, chain=None, parts=1):
        self.value, self.chain, self.parts = value, chain, parts
        self.shape = value.shape if chain is None else value.shape[2:]


class Scalars:
    def __init__(self, numbers, far_tags=None):
        self.section, self.rep = lax.axis_index("section"), lax.axis_index("rep")
        self.numbers, self.far_tags = numbers, far_tags

    def length(self, chain):
        return self.numbers[chain, self.section]

    def tag(self, chain):
        return self.numbers[chain, 2 + self.section]

    def far_tag(self, chain):
        return self.far_tags[chain, self.section]


def layer_norm(resid):
    mean = jnp.mean(resid, -1, keepdims=True)
    centred = resid - mean
    inverse = lax.rsqrt(jnp.mean(centred * centred, -1, keepdims=True) + EPS)
    return centred * inverse, inverse


def layer_norm_back(grad, gain, normed, inverse):
    scaled = grad * gain
    return inverse * (
        scaled
        - jnp.mean(scaled, -1, keepdims=True)
        - normed * jnp.mean(scaled * normed, -1, keepdims=True)
    )


class Weights:
    def __init__(self, own, got, is_own, pieces, place, sems, first=0):
        self.place, self.copies, self.waited = place, {}, set()
        for index, (name, source, target) in enumerate(pieces):
            target = place.at[target] if target is not None else place
            near = pltpu.make_async_copy(own.at[source], target, sems.at[first + index])
            away = pltpu.make_async_copy(got.at[source], target, sems.at[first + index])
            self.copies[name] = near
            pl.when(is_own)(near.start)
            pl.when(jnp.logical_not(is_own))(away.start)

    def __call__(self, name=0):
        self.copies[name].wait()
        return self.place


def in_halves(tag, axis):
    pieces = []
    for half in range(2):
        at = pl.ds(half * HALF, HALF)
        at = (at,) if axis == 0 else (slice(None), at)
        pieces.append((half, (tag, *at), at))
    return pieces


def vec_reader(vecs, is_own, tag):
    own, got = vecs

    def read(at, extent=WIDTH):
        span = slice(at, at + extent) if isinstance(at, int) else pl.ds(at, extent)
        return jnp.where(is_own, own[pl.ds(tag, 1), span], got[pl.ds(tag, 1), span])

    return read


def gelu_and_slope(pre):
    cdf = 0.5 + 0.5 * lax.erf(pre * 0.7071067811865476)
    pdf = jnp.exp(pre * pre * -0.5) * 0.3989422804014327
    return (pre * cdf).astype(BF), (cdf + pre * pdf).astype(BF)


def column_sum(values):
    return jnp.sum(values, axis=0, keepdims=True)


def half_mask(values, which):
    lanes = lax.broadcasted_iota(jnp.int32, values.shape, 1)
    keep = (lanes < HD) if which == 0 else (lanes >= HD)
    return jnp.where(keep, values, jnp.zeros_like(values))


def attend(x, vector, length, wq, out_qkv, out_probs, out_att):
    span = x.shape[0]
    parts = []
    for j in range(3):
        value = mm(x, wq(j)[j])
        if j == 0:
            value = value + vector(BIAS_Q, LOCAL)
        if j == 2:
            value = value + vector(BIAS_V, LOCAL)
        value = value.astype(BF)
        out_qkv[:, j * LOCAL : (j + 1) * LOCAL] = value
        parts.append(value)
    out_qkv.start()
    query, key, value = parts
    keys = lax.broadcasted_iota(jnp.int32, (span, span), 0)
    usable = keys < length
    mixed = []
    for pair in range(LOCAL // 128):
        at = slice(pair * 128, pair * 128 + 128)
        total = None
        for which in range(2):
            scores = mm(half_mask(key[:, at], which), query[:, at], NT) * 0.125
            scores = jnp.where(usable, scores, -1e30)
            raised = jnp.exp(scores - jnp.max(scores, axis=0, keepdims=True))
            probs = (raised * (1.0 / jnp.sum(raised, axis=0, keepdims=True))).astype(BF)
            out_probs[2 * pair + which] = probs
            term = mm(probs, half_mask(value[:, at], which), TN)
            total = term if total is None else total + term
        mixed.append(total.astype(BF))
    out_probs.start()
    att = jnp.concatenate(mixed, axis=1)
    out_att[...] = att
    return att


def attention_kernel(layer, chain, meta, *refs):
    if layer == 0:
        x_ref, *vecs = refs[:3]
        refs = refs[3:]
    else:
        feed_own, feed_got, hidden, *vecs = refs[:5]
        refs = refs[5:]
    own_q, got_q, own_o, got_o, *refs, wq, wo, sems = refs
    if layer == 0:
        out_qkv, out_probs, out_att, out_branch = refs
    else:
        out_x, out_x_saved, out_r2, out_qkv, out_probs, out_att, out_branch = refs
    length, tag = meta.length(chain), meta.tag(chain)
    is_own = meta.section == layer
    vector = vec_reader(vecs, is_own, tag)
    wq = Weights(own_q, got_q, is_own, [(j, (tag, j), j) for j in range(3)], wq, sems)
    wo = Weights(own_o, got_o, is_own, [(0, tag, None)], wo, sems, 3)
    if layer == 0:
        x = x_ref[...]
    else:
        before = vec_reader(vecs, meta.section == 0, tag)
        r2 = hidden[...] + ((feed_own[...].astype(F32) + feed_got[...].astype(F32)) + before(SHIFT[2]))
        out_r2[...] = r2
        normed, _ = layer_norm(r2)
        x = (normed * before(GAIN_TWO) + before(SHIFT[3])).astype(BF)
        out_x[...] = x
        out_x_saved[...] = x
    att = attend(x, vector, length, wq, out_qkv, out_probs, out_att)
    out_branch[...] = mm(att, wo()[...]).astype(BF)


def feed_kernel(layer, chain, meta, x, own, got, *refs):
    *vecs, own_i, got_i, own_d, got_d = refs[:6]
    *_, out_hidden, out_r1, out_slope, out_act, out_low, out_feed, act, wi, wd, low_rows, sems = refs[6:]
    span = x.shape[0]
    tag = meta.tag(chain)
    is_own = meta.section == layer
    wi = Weights(own_i, got_i, is_own, in_halves(tag, 1), wi, sems)
    wd = Weights(own_d, got_d, is_own, [(0, tag, None)], wd, sems, 2)
    vector = vec_reader(vecs, is_own, tag)
    branch = (own[...].astype(F32) + got[...].astype(F32)) + vector(SHIFT[0])
    r1 = x[...].astype(F32) + branch
    out_r1[...] = r1
    normed, _ = layer_norm(r1)
    hidden = normed * vector(GAIN_ONE) + vector(SHIFT[1])
    out_hidden[...] = hidden
    low = hidden.astype(BF)
    low_rows[...] = low
    low_copy = pltpu.make_async_copy(low_rows, out_low.at[pl.ds(chain * span, span)], sems.at[3])
    low_copy.start()
    for half in range(2):
        at = half * HALF
        pre = mm(low, wi(half)[:, at : at + HALF]) + vector(BIAS_IN + at, HALF)
        act[:, at : at + HALF], out_slope[:, at : at + HALF] = gelu_and_slope(pre)

        @pl.when(meta.rep == half)
        def _():
            out_act[:, :] = act[:, at : at + HALF]

    out_act.start()
    out_slope.start()
    out_feed[...] = mm(act[...], wd()[...]).astype(BF)
    low_copy.wait()


def feed_back_kernel(layer, chain, meta, own, got, *refs):
    first, second, *vecs, act_slope, own_i, got_i, own_d, got_d = refs[:9]
    out_y, out_dr2, out_df, out_du, out_dh, out_vec, du_all, wi, wd, sems = refs[9:]
    length, tag = meta.length(chain), meta.tag(chain)
    is_own = meta.section == layer
    wd = Weights(own_d, got_d, is_own, in_halves(tag, 0), wd, sems)
    wi = Weights(own_i, got_i, is_own, [(0, tag, None)], wi, sems, 2)
    vector = vec_reader(vecs, is_own, tag)
    gain = vector(GAIN_TWO)
    both = own[...].astype(F32) + got[...].astype(F32)
    if layer == 1:
        hidden, cotangent = first, second
        normed, inverse = layer_norm(hidden[...] + (both + vector(SHIFT[2])))
        out_y[...] = (normed * gain + vector(SHIFT[3])).astype(BF)
        tokens = lax.broadcasted_iota(jnp.int32, both.shape, 0)
        dy = jnp.where(tokens < length, cotangent[...].astype(F32), 0.0)
    else:
        dr1, r2 = first, second
        low = (both + dr1[...]).astype(BF)
        out_y[...] = low
        dy = low.astype(F32)
        normed, inverse = layer_norm(r2[...])
    dr2 = layer_norm_back(dy, gain, normed, inverse)
    out_dr2[...] = dr2
    df = dr2.astype(BF)
    out_df[...] = df
    out_vec[:, 0:768] = column_sum(dy * normed)
    out_vec[:, 768:1536] = column_sum(dr2)
    out_vec[:, 1536:2304] = column_sum(dy)
    for half in range(2):
        at = half * HALF
        du = mm(df, wd(half)[at : at + HALF, :], NT) * act_slope[:, at : at + HALF].astype(F32)
        out_vec[:, 2304 + at : 2304 + at + HALF] = column_sum(du)
        du_all[:, at : at + HALF] = du.astype(BF)

        @pl.when(meta.rep == half)
        def _():
            out_du[:, :] = du_all[:, at : at + HALF]

    out_du.start()
    out_dh[...] = mm(du_all[...], wi()[...], NT).astype(BF)


def attention_back_kernel(layer, chain, meta, own, got, dr2, r1, *refs):
    *vecs, qkv, probs_ref, own_q, got_q, own_o, got_o = refs[:8]
    out_dr1, out_dz, out_dqkv, out_dx, out_vec, wq, wo, sems = refs[8:]
    tag = meta.tag(chain)
    is_own = meta.section == layer
    wo = Weights(own_o, got_o, is_own, [(0, tag, None)], wo, sems, 3)
    wq = Weights(own_q, got_q, is_own, [(j, (tag, j), j) for j in range(3)], wq, sems)
    vector = vec_reader(vecs, is_own, tag)
    dh = (own[...].astype(F32) + got[...].astype(F32)) + dr2[...]
    normed, inverse = layer_norm(r1[...])
    dr1 = layer_norm_back(dh, vector(GAIN_ONE), normed, inverse)
    out_dr1[...] = dr1
    dz = dr1.astype(BF)
    out_dz[...] = dz
    out_vec[:, 0:768] = column_sum(dh * normed)
    out_vec[:, 768:1536] = column_sum(dr1)
    out_vec[:, 1536:2304] = column_sum(dh)
    datt = mm(dz, wo()[...], NT).astype(BF)
    query, key, value = (qkv[:, j * LOCAL : (j + 1) * LOCAL] for j in range(3))
    for pair in range(LOCAL // 128):
        at = slice(pair * 128, pair * 128 + 128)
        dv = dq = dk = None
        for which in range(2):
            probs = probs_ref[2 * pair + which]
            dv_term = mm(probs, half_mask(datt[:, at], which))
            dprobs = mm(half_mask(value[:, at], which), datt[:, at], NT)
            wide = probs.astype(F32)
            dscores = wide * (dprobs - jnp.sum(wide * dprobs, axis=0, keepdims=True))
            dscores = dscores.astype(BF)
            dk_term = mm(dscores, half_mask(query[:, at], which))
            dq_term = mm(dscores, half_mask(key[:, at], which), TN)
            dv = dv_term if dv is None else dv + dv_term
            dk = dk_term if dk is None else dk + dk_term
            dq = dq_term if dq is None else dq + dq_term
        dq = dq * 0.125
        dk = dk * 0.125
        low = pair * 128
        out_vec[:, 2304 + low : 2304 + low + 128] = column_sum(dq)
        out_vec[:, 2688 + low : 2688 + low + 128] = column_sum(dv)
        out_dqkv[:, low : low + 128] = dq.astype(BF)
        out_dqkv[:, LOCAL + low : LOCAL + low + 128] = dk.astype(BF)
        out_dqkv[:, 2 * LOCAL + low : 2 * LOCAL + low + 128] = dv.astype(BF)
    out_dqkv.start()
    dx = None
    for j in range(3):
        term = mm(out_dqkv[:, j * LOCAL : (j + 1) * LOCAL], wq(j)[j], NT)
        dx = term if dx is None else dx + term
    out_dx[...] = dx.astype(BF)


def far_kernel(layer, chains, meta, *refs):
    low, *vecs, own_i, got_i, out_act, out_slope, wi, sems = refs
    span = low.shape[0] // chains
    is_own = meta.section == layer
    half = pl.ds(pl.multiple_of(meta.rep * HALF, HALF), HALF)
    wi = Weights(own_i, got_i, is_own, [(0, (slice(None), slice(None), half), None)], wi, sems)()
    for chain in range(chains):
        tag = meta.far_tag(chain)
        at = slice(chain * span, (chain + 1) * span)
        bias = vec_reader(vecs, is_own, tag)(pl.multiple_of(BIAS_IN + meta.rep * HALF, HALF), HALF)
        pre = mm(low[at, :], wi[tag]) + bias
        out_act[at, :], out_slope[at, :] = gelu_and_slope(pre)


def order_of(tags, section):
    mine = [(tag == section).astype(jnp.int32) for tag in tags]
    count = sum(mine)
    places, before = [], 0
    for index, one in enumerate(mine):
        places.append(jnp.where(one == 1, before, count + index - before))
        before = before + one
    return places, count


class Gathered:
    def __init__(self, sources, places, target, sems, first):
        self.place, self.copies = target, []
        for index, (source, place) in enumerate(zip(sources, places)):
            extent = source.shape[0]
            at = pl.ds(pl.multiple_of(place * extent, extent), extent)
            copy = pltpu.make_async_copy(source, target.at[at], sems.at[first + index])
            copy.start()
            self.copies.append(copy)

    def wait(self):
        for copy in self.copies:
            copy.wait()
        return self.place


def both_models(count, chains, span, left, rights, stores):
    def branch(number):
        def products():
            cut = number * span
            for right, store in zip(rights, stores):
                columns = right.shape[1]
                for keeping, rows in ((False, slice(cut, chains * span)), (True, slice(0, cut))):
                    if rows.start == rows.stop:
                        store(keeping, jnp.zeros((left.shape[0], columns), BF))
                    else:
                        store(keeping, mm(left[:, rows], right[rows, :]).astype(BF))

        return products

    for number in range(chains + 1):
        pl.when(count == number)(branch(number))


def feed_grad_kernel(layer, chains, meta, *refs):
    df, act, du, far_df = (refs[i * chains : (i + 1) * chains] for i in range(4))
    low, far_low, far_act, slope_from, own_d, got_d, *refs = refs[4 * chains :]
    keep, send, df_all, act_all, low_all, du_all, far_slope, wd, sems = refs
    span = df[0].shape[0]
    half = pl.ds(pl.multiple_of(meta.rep * HALF, HALF), HALF)
    is_own = meta.section == layer
    tags = [meta.tag(chain) for chain in range(chains)] + [meta.far_tag(chain) for chain in range(chains)]
    places, count = order_of(tags, meta.section)
    split = lambda rows: [rows.at[pl.ds(chain * span, span)] for chain in range(chains)]
    df_all = Gathered([*df, *far_df], places, df_all, sems, 0)
    act_all = Gathered([*act, *split(far_act)], places, act_all, sems, 2 * chains)
    wd = Weights(own_d, got_d, is_own, [(0, (slice(None), half), None)], wd, sems, 8 * chains)
    far_slope = Lazy(slope_from, far_slope, sems, 8 * chains + 1, 1)
    far_slope.start()
    du_all = Gathered(du, places, du_all, sems, 4 * chains)
    low_all = Gathered([*split(low), *split(far_low)], places, low_all, sems, 6 * chains)

    def products(left_all, at, right):
        def column_block(index, carry):
            rows = pl.ds(pl.multiple_of(index * BLOCK, BLOCK), BLOCK)
            left = left_all[:, rows].T

            def store(keeping, value):
                out = keep.place if keeping else send
                out[rows, at : at + HALF] = value

            both_models(count, 2 * chains, span, left, [right], [store])
            return carry

        lax.fori_loop(0, WIDTH // BLOCK, column_block, 0)
        keep.start(at // HALF)

    lefts = df_all.wait()
    products(lefts, 0, act_all.wait())
    rights = du_all.wait()
    weights = wd()
    for chain in range(chains):
        at = slice(chain * span, (chain + 1) * span)
        there = pl.ds(pl.multiple_of(places[chains + chain] * span, span), span)
        value = mm(lefts[there, :], weights[meta.far_tag(chain)], NT) * far_slope[at, :].astype(F32)
        rights[there, :] = value.astype(BF)
    products(low_all.wait(), HALF, rights)


def attention_grad_kernel(layer, chains, meta, *refs):
    dz, att, x, dqkv = (refs[i * chains : (i + 1) * chains] for i in range(4))
    keep, send, dz_all, att_all, x_all, dqkv_all, sems = refs[4 * chains :]
    span = dz[0].shape[0]
    if layer == 0:
        x = [ref.at[chain, meta.section] for chain, ref in enumerate(x)]
    places, count = order_of([meta.tag(chain) for chain in range(chains)], meta.section)
    dz_all = Gathered(dz, places, dz_all, sems, 0)
    att_all = Gathered(att, places, att_all, sems, chains)
    x_all = Gathered(x, places, x_all, sems, 2 * chains)
    dqkv_all = Gathered(dqkv, places, dqkv_all, sems, 3 * chains)

    def products(left_all, rights, targets):
        def column_block(index, carry):
            rows = pl.ds(pl.multiple_of(index * BLOCK, BLOCK), BLOCK)
            left = left_all[:, rows].T

            def store_at(slot, columns):
                def store(keeping, value):
                    out = keep.place if keeping else send
                    if layer == 1:
                        out[rows, columns.start + slot * HALF : columns.stop + slot * HALF] = value
                    else:
                        out[jnp.where(meta.rep == 0, slot, 1 - slot), rows, columns] = value

                return store

            both_models(count, chains, span, left, rights, [store_at(*target) for target in targets])
            return carry

        lax.fori_loop(0, WIDTH // BLOCK, column_block, 0)

    left_all, right = dz_all.wait(), att_all.wait()
    products(left_all, [right], [(0, slice(0, LOCAL))])
    left_all, right = x_all.wait(), dqkv_all.wait()
    rights = [right.at[:, pl.ds(0, LOCAL)], right.at[:, pl.ds(LOCAL, 2 * LOCAL)]]
    products(left_all, rights, [(0, slice(LOCAL, HALF)), (1, slice(0, HALF))])


def add_kernel(parts, meta, one, two, out):
    block = one.shape[0] // parts
    for part in range(parts):
        at = slice(part * block, (part + 1) * block)
        one.wait(part)
        out[at, :] = one.place[at, :] + two[at, :]
        out.start(part)


def add_halves_kernel(meta, one, two, near, far):
    for half, out in ((1, far), (0, near)):
        one.wait(half)
        out[...] = one.place[half] + two[half]


BLOCK = 256
ANY = pl.BlockSpec(memory_space=pl.ANY)


def pack_kernel(gains, shifts, b_qv, b_in, out):
    for model in range(2):
        row = slice(model, model + 1)
        for j in range(2):
            out[row, j * WIDTH : (j + 1) * WIDTH] = gains[0, model, j : j + 1, :]
            out[row, BIAS_Q + j * LOCAL : BIAS_Q + (j + 1) * LOCAL] = b_qv[0, model, j : j + 1, :]
        for j in range(4):
            out[row, SHIFT[j] : SHIFT[j] + WIDTH] = shifts[0, model, j : j + 1, :]
        out[row, BIAS_IN:] = b_in[0, row, :]


def feed_final_kernel(meta, *refs):
    zero, one, got, grad_in, grad_out = refs[:2], refs[2:4], refs[4], refs[5], refs[6]
    for half in range(2):
        local = jnp.where(meta.rep == 0, half, 1 - half)
        mine = jnp.where(meta.section == 0, zero[half][...], one[half][...]).astype(F32)
        columns = pl.ds(pl.multiple_of(local * HALF, HALF), HALF)
        for model, shard in ((meta.section, mine), (1 - meta.section, got[half].astype(F32))):
            grad_out[model, :, columns] = shard[:, 0:HALF]
            grad_in[model, :, columns] = shard[:, HALF:]


def attention_final_kernel(meta, *refs):
    zero, got_zero, (one, got_one, grad_qkv, grad_o) = refs[:2], refs[2:4], refs[4:]
    for model, halves, whole in ((meta.section, zero, one), (1 - meta.section, got_zero, got_one)):
        near, far = halves[0][...], halves[1][...]
        low = jnp.where(meta.rep == 0, near, far)
        high = jnp.where(meta.rep == 0, far, near)
        low = jnp.where(meta.section == 0, low, whole[:, 0:HALF]).astype(F32)
        high = jnp.where(meta.section == 0, high, whole[:, HALF:]).astype(F32)
        grad_o[model] = low[:, 0:LOCAL]
        grad_qkv[model, 0] = low[:, LOCAL:]
        grad_qkv[model, 1] = high[:, 0:LOCAL]
        grad_qkv[model, 2] = high[:, LOCAL:]


def vector_grad_kernel(chains, meta, *refs):
    out = refs[-1]
    for layer in range(2):
        ones = refs[2 * layer * chains : (2 * layer + 1) * chains]
        twos = refs[(2 * layer + 1) * chains : (2 * layer + 2) * chains]
        rows = [
            jnp.concatenate(
                [one[:, 0:768], two[:, 0:768], one[:, 768:2304], two[:, 768:2304], one[:, 2304:], two[:, 2304:]],
                axis=1,
            )
            for one, two in zip(ones, twos)
        ]
        for model in range(2):
            total = None
            for chain in range(chains):
                row = jnp.where(meta.tag(chain) == model, rows[chain], 0.0)
                total = row if total is None else total + row
            out[layer, model : model + 1, :] = total


STEP = 1.5e9
LONG = 8

VMEM = pl.BlockSpec(memory_space=pltpu.VMEM)
SMEM = pl.BlockSpec(memory_space=pltpu.SMEM)
SAVED, PARTLY = "saved", "partly"


def pieces_of(out):
    return out[3] if len(out) > 3 else [None]


def in_hbm(value):
    return pltpu.with_memory_space_constraint(value, pltpu.HBM)


def call(body, scalars, operands, outs, scratch, name, grant, cost):
    saved_in = [value for value in operands if isinstance(value, Saved)]
    saved_out = [out for out in outs if SAVED in out]
    buffers = [pltpu.VMEM(value.shape, value.value.dtype) for value in saved_in]
    buffers += [pltpu.VMEM(out[0], out[1]) for out in saved_out]
    counts = (len(scalars), len(operands), len(outs), len(scratch))

    def kernel(*refs):
        groups = []
        for count in counts:
            groups.append(refs[:count])
            refs = refs[count:]
        numbers, ins, results, own_scratch = groups
        *places, sems = refs
        meta = Scalars(*numbers)
        given, taken, index, sem = [], [], 0, 0
        for value, ref in zip(operands, ins):
            if isinstance(value, Saved):
                source = ref if value.chain is None else ref.at[value.chain, meta.section]
                ref = Lazy(source, places[index], sems, sem, value.parts)
                ref.start()
                sem += value.parts
                index += 1
            given.append(ref)
        for out, ref in zip(outs, results):
            if SAVED in out:
                ref = Leaving(places[index], ref, sems, sem, pieces_of(out))
                sem += len(pieces_of(out))
                index += 1
            taken.append(ref)
        body(meta, *given, *taken, *own_scratch)
        for ref in taken:
            if isinstance(ref, Leaving):
                ref.start()
        for ref in given:
            if isinstance(ref, Lazy):
                ref.wait()
        for ref in taken:
            if isinstance(ref, Leaving):
                ref.wait()

    in_specs = [ANY if isinstance(value, (tuple, Saved)) else VMEM for value in operands]
    values = []
    for value in operands:
        if isinstance(value, Saved):
            value = in_hbm(value.value)
        elif isinstance(value, tuple):
            value = in_hbm(value[0])
        values.append(value)
    shapes = [
        pltpu.HBM(*out[:2]) if SAVED in out or PARTLY in out else jax.ShapeDtypeStruct(*out[:2]) for out in outs
    ]
    return pl.pallas_call(
        kernel,
        out_shape=shapes,
        in_specs=[SMEM] * len(scalars) + in_specs,
        out_specs=[ANY if SAVED in out or PARTLY in out else VMEM for out in outs],
        input_output_aliases={
            len(scalars) + out[3]: index for index, out in enumerate(outs) if PARTLY in out and len(out) > 3
        },
        scratch_shapes=[*scratch, *buffers, pltpu.SemaphoreType.DMA((max(sum(value.parts for value in saved_in) + sum(len(pieces_of(out)) for out in saved_out), 1),))],
        compiler_params=pltpu.CompilerParams(vmem_limit_bytes=grant * 1024 * 1024),
        cost_estimate=pl.CostEstimate(flops=int(cost * STEP), bytes_accessed=1, transcendentals=0),
        name=name,
    )(*scalars, *values)


def on_device(
    block_input, cotangent, lengths, tags, w_qkv, w_o, w_in, w_out, b_qv, b_in, gains, shifts
):
    micro, per, span, width = block_input.shape
    section = lax.axis_index("section")
    rep = lax.axis_index("rep")
    chains = range(micro)
    layers = range(2)

    own_q, own_o, own_i, own_d = w_qkv[0], w_o[0], w_in[0], w_out[0]
    got_q = swap(own_q, "section")
    vec_own = pl.pallas_call(
        pack_kernel, out_shape=jax.ShapeDtypeStruct((2, PACKED), F32), in_specs=[VMEM] * 4, out_specs=VMEM, name="pack"
    )(gains, shifts, b_qv, b_in)
    numbers = jnp.concatenate([lengths, tags], axis=1)
    vec_own = after(vec_own, numbers)
    vecs = [vec_own, swap(vec_own, "section")]
    got_o = swap(own_o, "section")
    later = lax.optimization_barrier((own_i, own_d, got_q, got_o, vecs[1]))
    got_i, got_d = swap(later[0], "section"), swap(later[1], "section")

    heads = LOCAL // HD
    row, saved_row = ((span, WIDTH), BF), ((span, WIDTH), BF, SAVED)
    wide, saved_wide = ((span, WIDTH), F32), ((span, WIDTH), F32, SAVED)
    half_row, long_row = ((span, HALF), BF, SAVED), ((span, HIDDEN), BF, SAVED)
    qkv_row = ((span, 3 * LOCAL), BF, SAVED)
    att_outs = [qkv_row, ((heads, span, span), BF, SAVED), ((span, LOCAL), BF, SAVED), row]
    raw = lambda values: [(value,) for value in values]
    w_qo, w_id = raw([own_q, got_q, own_o, got_o]), raw([own_i, got_i, own_d, got_d])
    qo_scratch = [
        pltpu.VMEM((3, WIDTH, LOCAL), BF),
        pltpu.VMEM((LOCAL, WIDTH), BF),
        pltpu.SemaphoreType.DMA((4,)),
    ]
    id_scratch = [
        pltpu.VMEM((span, HIDDEN), BF),
        pltpu.VMEM((WIDTH, HIDDEN), BF),
        pltpu.VMEM((HIDDEN, WIDTH), BF),
        pltpu.SemaphoreType.DMA((3,)),
    ]
    feed_scratch = id_scratch[:3] + [pltpu.VMEM((span, WIDTH), BF), pltpu.SemaphoreType.DMA((4,))]

    last = [numbers]

    def run(body, operands, outs, scratch, name, *waits, far=False, grant=14, cost=1):
        scalars = [after(numbers, last[0], *waits)] + ([far_tags] if far else [])
        results = call(body, scalars, operands, outs, scratch, name, grant, cost)
        last[0] = results[-1]
        return results

    def saved(values):
        return [Saved(value) for value in values]

    def arrived(pair):
        return [pair[0], Saved(pair[1])]

    def owned(zero, one):
        zero, one = jnp.stack(zero), jnp.stack(one)
        mine = jnp.where(section == 0, zero, one)
        other = swap(jnp.where(section == 0, one, zero), "section")
        core = lax.broadcasted_iota(jnp.int32, (micro, per, span, width), 1)
        return jnp.where(core == section, mine[:, None], other[:, None])[None]

    table = lambda: [[None] * micro for _ in layers]
    r1s, r2s, hiddens, acts, slopes, feeds, qkvs, probs, atts = (table() for _ in range(9))
    lows, far_lows = [None, None], [None, None]
    x_now, x_saved = [[Saved(block_input, chain) for chain in chains], [None] * micro], [None] * micro
    for layer in layers:
        for chain in chains:
            body = functools.partial(attention_kernel, layer, chain)
            name = f"attention{layer}{chain}"
            if layer == 0:
                got = run(body, [x_now[0][chain], *vecs] + w_qo, att_outs, qo_scratch, name)
            else:
                operands = [*arrived(feeds[0][chain]), hiddens[0][chain], *vecs] + w_qo
                waits = []
                x_now[1][chain], x_saved[chain], r2s[0][chain], *got = run(
                    body, operands, [row, saved_row, saved_wide] + att_outs, qo_scratch, name, *waits
                )
            qkvs[layer][chain], probs[layer][chain], atts[layer][chain], branch = got
            feeds[layer][chain] = (branch, swap(branch, "mp"))
        if layer == 0:
            far_tags = swap(after(tags, last[0]), "rep")
        for chain in chains:
            body = functools.partial(feed_kernel, layer, chain)
            waits = [far_tags] if layer == 0 and chain == 2 else []
            operands = [x_now[layer][chain], *feeds[layer][chain], *vecs] + w_id
            rows_out = ((micro * span, WIDTH), BF, PARTLY)
            if chain:
                rows_out += (len(operands),)
                operands.append((lows[layer],))
            hiddens[layer][chain], r1s[layer][chain], slopes[layer][chain], acts[layer][chain], lows[layer], part = run(
                body,
                operands,
                [wide, saved_wide, long_row, half_row, rows_out, row],
                feed_scratch,
                f"feed{layer}{chain}",
                *waits,
            )
            feeds[layer][chain] = (part, swap(part, "mp"))
        far_lows[layer] = swap(lows[layer], "rep")

    rows = micro * span
    far_rows = ((rows, HALF), BF, SAVED)
    dr2s, dfs, far_dfs, dus, dhs, vec_one, vec_two, dzs, dqkvs, dr1s, dxs, ys = (table() for _ in range(12))
    far_hidden = [None, None]

    def feed_back(layer, chain, *waits, cost=1):
        if layer == 1:
            operands = [*arrived(feeds[1][chain]), hiddens[1][chain], Saved(cotangent, chain)]
        else:
            operands = [*arrived(dxs[1][chain]), Saved(dr1s[1][chain]), Saved(r2s[0][chain])]
        ys[layer][chain], dr2s[layer][chain], df, dus[layer][chain], dh, vec_two[layer][chain] = run(
            functools.partial(feed_back_kernel, layer, chain),
            operands + [*vecs, Saved(slopes[layer][chain])] + w_id,
            [saved_row, saved_wide, saved_row, half_row, row, ((1, 3 * WIDTH + HIDDEN), F32, SAVED)],
            id_scratch,
            f"feed_back{layer}{chain}",
            *waits,
            cost=cost,
        )
        dfs[layer][chain], far_dfs[layer][chain] = df, swap(df, "rep")
        dhs[layer][chain] = (dh, swap(dh, "mp"))

    def attention_back(layer, chain, *waits, cost=1):
        dr1s[layer][chain], dzs[layer][chain], dqkvs[layer][chain], dx, vec_one[layer][chain] = run(
            functools.partial(attention_back_kernel, layer, chain),
            [*arrived(dhs[layer][chain]), Saved(dr2s[layer][chain]), Saved(r1s[layer][chain]), *vecs]
            + [Saved(qkvs[layer][chain]), Saved(probs[layer][chain])]
            + w_qo,
            [saved_wide, saved_row, qkv_row, row, ((1, 3 * WIDTH + 2 * LOCAL), F32, SAVED)],
            qo_scratch,
            f"attention_back{layer}{chain}",
            *waits,
            cost=cost,
        )
        dxs[layer][chain] = (dx, swap(dx, "mp"))

    def far_part(layer, *waits):
        far_hidden[layer] = run(
            functools.partial(far_kernel, layer, micro),
            [Saved(far_lows[layer]), *vecs] + w_id[:2],
            [far_rows] * 2,
            [pltpu.VMEM((2, WIDTH, HALF), BF), pltpu.SemaphoreType.DMA((1,))],
            f"far{layer}",
            *waits,
            far=True,
            cost=1.5,
        )

    def feed_grad(layer, *waits, cost=2):
        near = dfs[layer] + acts[layer] + dus[layer] + far_dfs[layer]
        far_act, far_slope = far_hidden[layer]
        stacked = pltpu.VMEM((2 * rows, HALF), BF)
        keep, send = run(
            functools.partial(feed_grad_kernel, layer, micro),
            raw(near + [lows[layer], far_lows[layer], far_act, far_slope]) + w_id[2:],
            [((WIDTH, HIDDEN), BF, SAVED, blocks_of(WIDTH, HIDDEN, WIDTH, HALF)), ((WIDTH, HIDDEN), BF)],
            [stacked] * 4
            + [pltpu.VMEM((rows, HALF), BF), pltpu.VMEM((2, HALF, WIDTH), BF), pltpu.SemaphoreType.DMA((8 * micro + 2,))],
            f"feed_grad{layer}",
            *waits,
            far=True,
            grant=20,
            cost=cost,
        )
        return keep, swap(send, "section")

    def whole_sum(name, parts, *waits):
        (result,) = run(
            functools.partial(add_kernel, WIDTH // BLOCK),
            [Saved(parts[0], parts=WIDTH // BLOCK), parts[1]],
            [((WIDTH, HIDDEN), BF, SAVED, blocks_of(WIDTH, HIDDEN, BLOCK, HIDDEN))],
            [],
            name,
            *waits,
        )
        return result

    def attention_grad(layer, *waits):
        x_part = raw([block_input] * micro if layer == 0 else x_saved)
        narrow, stacked = pltpu.VMEM((rows, LOCAL), BF), pltpu.VMEM((rows, WIDTH), BF)
        shape = (WIDTH, HIDDEN) if layer == 1 else (2, WIDTH, HALF)
        pieces = [None] if layer == 1 else [pl.ds(0, 1), pl.ds(1, 1)]
        keep, send = run(
            functools.partial(attention_grad_kernel, layer, micro),
            raw(dzs[layer] + atts[layer]) + x_part + raw(dqkvs[layer]),
            [(shape, BF, SAVED, pieces), (shape, BF)],
            [stacked, narrow, stacked, pltpu.VMEM((rows, 3 * LOCAL), BF), pltpu.SemaphoreType.DMA((4 * micro,))],
            f"attention_grad{layer}",
            *waits,
            cost=2,
        )
        return keep, swap(send, "section")

    def attention_grad_sum(layer, parts, *waits):
        near, far = run(
            add_halves_kernel,
            [Saved(parts[0], parts=2), parts[1]],
            [((WIDTH, HALF), BF, SAVED)] * 2,
            [],
            f"attention_grad_sum{layer}",
            *waits,
        )
        return near, swap(far, "rep")

    def scattered(part):
        return lax.psum_scatter(part, "dp", scatter_dimension=0, tiled=True)

    feed_back(1, 0, far_lows[0])
    feed_back(1, 1)
    feed_back(1, 2, cost=3)
    far_part(1, dhs[1][0][1], far_dfs[1][0])
    parts = feed_grad(1, dhs[1][1][1], far_dfs[1][1])
    attention_back(1, 0, dhs[1][2][1], cost=20)
    feed_one = scattered(whole_sum("feed_grad_sum1", parts))
    attention_back(1, 1)
    attention_back(1, 2, dxs[1][0][1])
    parts = attention_grad(1, dxs[1][1][1])
    far_part(0)
    attention_one = whole_sum("attention_grad_sum1", parts)
    feed_back(0, 0)
    feed_back(0, 1, dxs[1][2][1])
    attention_one = scattered(after(attention_one, feed_one, last[0]))
    feed_back(0, 2)
    attention_back(0, 0, feed_one, far_dfs[0][0], far_dfs[0][1])
    feed_one = (feed_one, swap(feed_one, "rep"))
    parts = feed_grad(0, dhs[0][2][1], dhs[0][1][1])
    attention_back(0, 1, cost=LONG)
    summed = whole_sum("feed_grad_sum0", parts)
    attention_one = after(attention_one, summed)
    feed_zero = scattered(after(summed, attention_one))
    attention_back(0, 2, attention_one, cost=2.75)
    attention_one = (attention_one, swap(after(attention_one, summed), "rep"))
    parts = attention_grad(0, feed_one[1])
    (both,) = run(
        functools.partial(vector_grad_kernel, micro),
        saved(vec_one[0] + vec_two[0] + vec_one[1] + vec_two[1]),
        [((2, 2, PACKED), F32)],
        [],
        "vector_grad",
        attention_one[1],
        *[dx[1] for dx in dxs[0][:2]],
        cost=20,
    )
    near, far = attention_grad_sum(0, parts)
    both = after(both, near)
    both = both + swap(both, "section")
    both = lax.dynamic_index_in_dim(both, section, 0, keepdims=False)
    data = lax.axis_size("dp")
    distance = 1
    while distance < data:
        both = both + lax.ppermute(both, "dp", [(i, i ^ distance) for i in range(data)])
        distance *= 2
    def first_grad(chain, *others):
        (own, got), dr1 = dxs[0][chain], dr1s[0][chain]
        return ((after(own, *others).astype(F32) + got.astype(F32)) + dr1).astype(BF)

    firsts = [first_grad(chain, near, both) for chain in chains[:-1]]
    firsts.append(first_grad(micro - 1, *firsts))
    attention_zero = after(after(near, firsts) + far, feed_zero)
    done = attention_zero
    both = both + swap(after(both, done), "rep")
    feed_zero = (feed_zero, swap(after(feed_zero, done), "rep"))
    attention_one = (after(attention_one[0], done).astype(F32) + attention_one[1].astype(F32)).astype(BF)
    feed_zero = (feed_zero[0], after(feed_zero[1], attention_one))
    layer_outputs = owned(after(x_saved, done), ys[1])
    grad_gains = both[:, : SHIFT[0]].reshape(2, 2, WIDTH)
    grad_shifts = both[:, SHIFT[0] : BIAS_Q].reshape(2, 4, WIDTH)
    grad_b_qv = both[:, BIAS_Q:BIAS_IN].reshape(2, 2, LOCAL)
    grad_b_in = both[:, BIAS_IN:]
    attention_zero = scattered(attention_zero)

    def handed(zero, one):
        return swap(jnp.where(section == 0, jnp.stack(one), jnp.stack(zero)), "section")

    shard = feed_zero[0].shape[0]
    grad_in, grad_out = run(
        feed_final_kernel,
        [*feed_zero, *feed_one, handed(feed_zero, feed_one)],
        [((2, shard, HIDDEN), F32)] * 2,
        [],
        "feed_final",
    )
    input_grads = owned(after(firsts, done), ys[0])
    got_one = swap(attention_one, "section")
    attention_zero = after(attention_zero, input_grads, layer_outputs, got_one)
    vectors = grad_b_qv[None], grad_b_in[None], grad_gains[None], grad_shifts[None]
    far, vectors, _ = lax.optimization_barrier((swap(attention_zero, "rep"), vectors, grad_in))
    got_zero = swap(attention_zero, "section"), swap(far, "section")
    attention_zero = (attention_zero, far)
    grad_qkv, grad_o = run(
        attention_final_kernel,
        [*attention_zero, *got_zero, attention_one, got_one],
        [((2, 3, shard, LOCAL), F32), ((2, shard, LOCAL), F32)],
        [],
        "attention_final",
    )
    grad_out, grad_o = jnp.swapaxes(grad_out, 1, 2), jnp.swapaxes(grad_o, 1, 2)

    return (
        layer_outputs,
        input_grads,
        grad_qkv[None],
        grad_o[None],
        grad_in[None],
        grad_out[None],
        *vectors,
    )


def solution(mesh):
    in_specs = (
        P(None, ("dp", "rep"), None, None),
        P(None, ("dp", "rep"), None, None),
        P(None, ("dp", "rep")),
        P(None, ("dp", "rep")),
        P("section", None, None, None, "mp"),
        P("section", None, "mp", None),
        P("section", None, None, "mp"),
        P("section", None, "mp", None),
        P("section", None, None, "mp"),
        P("section", None, "mp"),
        P("section", None, None, None),
        P("section", None, None, None),
    )
    out_specs = (
        P("section", None, ("dp", "rep"), None, None),
        P("section", None, ("dp", "rep"), None, None),
        P("section", None, None, "dp", "mp"),
        P("section", None, "mp", "dp"),
        P("section", None, "dp", "mp"),
        P("section", None, "mp", "dp"),
        P("section", None, None, "mp"),
        P("section", None, "mp"),
        P("section", None, None, None),
        P("section", None, None, None),
    )
    return jax.shard_map(
        on_device, mesh=mesh, in_specs=in_specs, out_specs=out_specs, check_vma=False
    )
```

```python
import functools

import jax
import jax.numpy as jnp
from jax import lax
from jax.experimental import pallas as pl
from jax.experimental.pallas import tpu as pltpu
from jax.sharding import PartitionSpec as P

HD = 64
EPS = 1e-05
BF = jnp.bfloat16
F32 = jnp.float32

GAIN_ONE, GAIN_TWO = 0, 768
SHIFT = (1536, 2304, 3072, 3840)
BIAS_Q, BIAS_V, BIAS_IN = 4608, 4992, 5376
PACKED = 6912
WIDTH, LOCAL, HIDDEN, HALF = 768, 384, 1536, 768

NN = (((1,), (0,)), ((), ()))
NT = (((1,), (1,)), ((), ()))
TN = (((0,), (0,)), ((), ()))


def mm(left, right, dims=NN):
    return lax.dot_general(left, right, dims, preferred_element_type=F32)


def swap(block, axis):
    return lax.ppermute(block, axis, [(0, 1), (1, 0)])


def after(value, *others):
    return lax.optimization_barrier((value, *others))[0]


class Lazy:
    def __init__(self, source, place, sems, first, parts):
        self.place, self.waited, self.copies = place, set(), []
        extent = place.shape[0] // parts
        for part in range(parts):
            at = pl.ds(part * extent, extent)
            near, away = (place, source) if parts == 1 else (place.at[at], source.at[at])
            self.copies.append(pltpu.make_async_copy(away, near, sems.at[first + part]))

    shape = property(lambda self: self.place.shape)

    def start(self):
        for copy in self.copies:
            copy.start()

    def wait(self, part=None):
        for index in range(len(self.copies)) if part is None else (part,):
            if index not in self.waited:
                self.copies[index].wait()
                self.waited.add(index)

    def __getitem__(self, at):
        self.wait()
        return self.place[at]


class Leaving:
    def __init__(self, place, target, sems, first, pieces):
        self.place, self.started, self.copies = place, set(), []
        for index, at in enumerate(pieces):
            near, away = (place, target) if at is None else (place.at[at], target.at[at])
            self.copies.append(pltpu.make_async_copy(near, away, sems.at[first + index]))

    shape = property(lambda self: self.place.shape)

    def start(self, piece=None):
        for index in range(len(self.copies)) if piece is None else (piece,):
            if index not in self.started:
                self.copies[index].start()
                self.started.add(index)

    def wait(self):
        for copy in self.copies:
            copy.wait()

    def __getitem__(self, at):
        return self.place[at]

    def __setitem__(self, at, value):
        self.place[at] = value
        if at is Ellipsis:
            self.start()


def blocks_of(rows, columns, row_step, column_step):
    return [
        (pl.ds(row, row_step), pl.ds(column, column_step))
        for column in range(0, columns, column_step)
        for row in range(0, rows, row_step)
    ]


class Saved:
    def __init__(self, value, chain=None, parts=1):
        self.value, self.chain, self.parts = value, chain, parts
        self.shape = value.shape if chain is None else value.shape[2:]


class Scalars:
    def __init__(self, numbers, far_tags=None):
        self.section, self.rep = lax.axis_index("section"), lax.axis_index("rep")
        self.numbers, self.far_tags = numbers, far_tags

    def length(self, chain):
        return self.numbers[chain, self.section]

    def tag(self, chain):
        return self.numbers[chain, 2 + self.section]

    def far_tag(self, chain):
        return self.far_tags[chain, self.section]


def layer_norm(resid):
    mean = jnp.mean(resid, -1, keepdims=True)
    centred = resid - mean
    inverse = lax.rsqrt(jnp.mean(centred * centred, -1, keepdims=True) + EPS)
    return centred * inverse, inverse


def layer_norm_back(grad, gain, normed, inverse):
    scaled = grad * gain
    return inverse * (
        scaled
        - jnp.mean(scaled, -1, keepdims=True)
        - normed * jnp.mean(scaled * normed, -1, keepdims=True)
    )


class Weights:
    def __init__(self, own, got, is_own, pieces, place, sems, first=0):
        self.place, self.copies, self.waited = place, {}, set()
        for index, (name, source, target) in enumerate(pieces):
            target = place.at[target] if target is not None else place
            near = pltpu.make_async_copy(own.at[source], target, sems.at[first + index])
            away = pltpu.make_async_copy(got.at[source], target, sems.at[first + index])
            self.copies[name] = near
            pl.when(is_own)(near.start)
            pl.when(jnp.logical_not(is_own))(away.start)

    def __call__(self, name=0):
        self.copies[name].wait()
        return self.place


def in_halves(tag, axis):
    pieces = []
    for half in range(2):
        at = pl.ds(half * HALF, HALF)
        at = (at,) if axis == 0 else (slice(None), at)
        pieces.append((half, (tag, *at), at))
    return pieces


def vec_reader(vecs, is_own, tag):
    own, got = vecs

    def read(at, extent=WIDTH):
        span = slice(at, at + extent) if isinstance(at, int) else pl.ds(at, extent)
        return jnp.where(is_own, own[pl.ds(tag, 1), span], got[pl.ds(tag, 1), span])

    return read


def gelu_and_slope(pre):
    cdf = 0.5 + 0.5 * lax.erf(pre * 0.7071067811865476)
    pdf = jnp.exp(pre * pre * -0.5) * 0.3989422804014327
    return (pre * cdf).astype(BF), (cdf + pre * pdf).astype(BF)


def column_sum(values):
    return jnp.sum(values, axis=0, keepdims=True)


def half_mask(values, which):
    lanes = lax.broadcasted_iota(jnp.int32, values.shape, 1)
    keep = (lanes < HD) if which == 0 else (lanes >= HD)
    return jnp.where(keep, values, jnp.zeros_like(values))


def attend(x, vector, length, wq, out_qkv, out_probs, out_att):
    span = x.shape[0]
    parts = []
    for j in range(3):
        value = mm(x, wq(j)[j])
        if j == 0:
            value = value + vector(BIAS_Q, LOCAL)
        if j == 2:
            value = value + vector(BIAS_V, LOCAL)
        value = value.astype(BF)
        out_qkv[:, j * LOCAL : (j + 1) * LOCAL] = value
        parts.append(value)
    out_qkv.start()
    query, key, value = parts
    keys = lax.broadcasted_iota(jnp.int32, (span, span), 0)
    usable = keys < length
    mixed = []
    for pair in range(LOCAL // 128):
        at = slice(pair * 128, pair * 128 + 128)
        total = None
        for which in range(2):
            scores = mm(half_mask(key[:, at], which), query[:, at], NT) * 0.125
            scores = jnp.where(usable, scores, -1e30)
            raised = jnp.exp(scores - jnp.max(scores, axis=0, keepdims=True))
            probs = (raised * (1.0 / jnp.sum(raised, axis=0, keepdims=True))).astype(BF)
            out_probs[2 * pair + which] = probs
            term = mm(probs, half_mask(value[:, at], which), TN)
            total = term if total is None else total + term
        mixed.append(total.astype(BF))
    out_probs.start()
    att = jnp.concatenate(mixed, axis=1)
    out_att[...] = att
    return att


def attention_kernel(layer, chain, meta, *refs):
    if layer == 0:
        x_ref, *vecs = refs[:3]
        refs = refs[3:]
    else:
        feed_own, feed_got, hidden, *vecs = refs[:5]
        refs = refs[5:]
    own_q, got_q, own_o, got_o, *refs, wq, wo, sems = refs
    if layer == 0:
        out_qkv, out_probs, out_att, out_branch = refs
    else:
        out_x, out_x_saved, out_r2, out_qkv, out_probs, out_att, out_branch = refs
    length, tag = meta.length(chain), meta.tag(chain)
    is_own = meta.section == layer
    vector = vec_reader(vecs, is_own, tag)
    wq = Weights(own_q, got_q, is_own, [(j, (tag, j), j) for j in range(3)], wq, sems)
    wo = Weights(own_o, got_o, is_own, [(0, tag, None)], wo, sems, 3)
    if layer == 0:
        x = x_ref[...]
    else:
        before = vec_reader(vecs, meta.section == 0, tag)
        r2 = hidden[...] + ((feed_own[...].astype(F32) + feed_got[...].astype(F32)) + before(SHIFT[2]))
        out_r2[...] = r2
        normed, _ = layer_norm(r2)
        x = (normed * before(GAIN_TWO) + before(SHIFT[3])).astype(BF)
        out_x[...] = x
        out_x_saved[...] = x
    att = attend(x, vector, length, wq, out_qkv, out_probs, out_att)
    out_branch[...] = mm(att, wo()[...]).astype(BF)


def feed_kernel(layer, chain, meta, x, own, got, *refs):
    *vecs, own_i, got_i, own_d, got_d = refs[:6]
    *_, out_hidden, out_r1, out_slope, out_act, out_low, out_feed, act, wi, wd, low_rows, sems = refs[6:]
    span = x.shape[0]
    tag = meta.tag(chain)
    is_own = meta.section == layer
    wi = Weights(own_i, got_i, is_own, in_halves(tag, 1), wi, sems)
    wd = Weights(own_d, got_d, is_own, [(0, tag, None)], wd, sems, 2)
    vector = vec_reader(vecs, is_own, tag)
    branch = (own[...].astype(F32) + got[...].astype(F32)) + vector(SHIFT[0])
    r1 = x[...].astype(F32) + branch
    out_r1[...] = r1
    normed, _ = layer_norm(r1)
    hidden = normed * vector(GAIN_ONE) + vector(SHIFT[1])
    out_hidden[...] = hidden
    low = hidden.astype(BF)
    low_rows[...] = low
    low_copy = pltpu.make_async_copy(low_rows, out_low.at[pl.ds(chain * span, span)], sems.at[3])
    low_copy.start()
    for half in range(2):
        at = half * HALF
        pre = mm(low, wi(half)[:, at : at + HALF]) + vector(BIAS_IN + at, HALF)
        act[:, at : at + HALF], out_slope[:, at : at + HALF] = gelu_and_slope(pre)

        @pl.when(meta.rep == half)
        def _():
            out_act[:, :] = act[:, at : at + HALF]

    out_act.start()
    out_slope.start()
    out_feed[...] = mm(act[...], wd()[...]).astype(BF)
    low_copy.wait()


def feed_back_kernel(layer, chain, meta, own, got, *refs):
    first, second, *vecs, act_slope, own_i, got_i, own_d, got_d = refs[:9]
    out_y, out_dr2, out_df, out_du, out_dh, out_vec, du_all, wi, wd, sems = refs[9:]
    length, tag = meta.length(chain), meta.tag(chain)
    is_own = meta.section == layer
    wd = Weights(own_d, got_d, is_own, in_halves(tag, 0), wd, sems)
    wi = Weights(own_i, got_i, is_own, [(0, tag, None)], wi, sems, 2)
    vector = vec_reader(vecs, is_own, tag)
    gain = vector(GAIN_TWO)
    both = own[...].astype(F32) + got[...].astype(F32)
    if layer == 1:
        hidden, cotangent = first, second
        normed, inverse = layer_norm(hidden[...] + (both + vector(SHIFT[2])))
        out_y[...] = (normed * gain + vector(SHIFT[3])).astype(BF)
        tokens = lax.broadcasted_iota(jnp.int32, both.shape, 0)
        dy = jnp.where(tokens < length, cotangent[...].astype(F32), 0.0)
    else:
        dr1, r2 = first, second
        low = (both + dr1[...]).astype(BF)
        out_y[...] = low
        dy = low.astype(F32)
        normed, inverse = layer_norm(r2[...])
    dr2 = layer_norm_back(dy, gain, normed, inverse)
    out_dr2[...] = dr2
    df = dr2.astype(BF)
    out_df[...] = df
    out_vec[:, 0:768] = column_sum(dy * normed)
    out_vec[:, 768:1536] = column_sum(dr2)
    out_vec[:, 1536:2304] = column_sum(dy)
    for half in range(2):
        at = half * HALF
        du = mm(df, wd(half)[at : at + HALF, :], NT) * act_slope[:, at : at + HALF].astype(F32)
        out_vec[:, 2304 + at : 2304 + at + HALF] = column_sum(du)
        du_all[:, at : at + HALF] = du.astype(BF)

        @pl.when(meta.rep == half)
        def _():
            out_du[:, :] = du_all[:, at : at + HALF]

    out_du.start()
    out_dh[...] = mm(du_all[...], wi()[...], NT).astype(BF)


def attention_back_kernel(layer, chain, meta, own, got, dr2, r1, *refs):
    *vecs, qkv, probs_ref, own_q, got_q, own_o, got_o = refs[:8]
    out_dr1, out_dz, out_dqkv, out_dx, out_vec, wq, wo, sems = refs[8:]
    tag = meta.tag(chain)
    is_own = meta.section == layer
    wo = Weights(own_o, got_o, is_own, [(0, tag, None)], wo, sems, 3)
    wq = Weights(own_q, got_q, is_own, [(j, (tag, j), j) for j in range(3)], wq, sems)
    vector = vec_reader(vecs, is_own, tag)
    dh = (own[...].astype(F32) + got[...].astype(F32)) + dr2[...]
    normed, inverse = layer_norm(r1[...])
    dr1 = layer_norm_back(dh, vector(GAIN_ONE), normed, inverse)
    out_dr1[...] = dr1
    dz = dr1.astype(BF)
    out_dz[...] = dz
    out_vec[:, 0:768] = column_sum(dh * normed)
    out_vec[:, 768:1536] = column_sum(dr1)
    out_vec[:, 1536:2304] = column_sum(dh)
    datt = mm(dz, wo()[...], NT).astype(BF)
    query, key, value = (qkv[:, j * LOCAL : (j + 1) * LOCAL] for j in range(3))
    for pair in range(LOCAL // 128):
        at = slice(pair * 128, pair * 128 + 128)
        dv = dq = dk = None
        for which in range(2):
            probs = probs_ref[2 * pair + which]
            dv_term = mm(probs, half_mask(datt[:, at], which))
            dprobs = mm(half_mask(value[:, at], which), datt[:, at], NT)
            wide = probs.astype(F32)
            dscores = wide * (dprobs - jnp.sum(wide * dprobs, axis=0, keepdims=True))
            dscores = dscores.astype(BF)
            dk_term = mm(dscores, half_mask(query[:, at], which))
            dq_term = mm(dscores, half_mask(key[:, at], which), TN)
            dv = dv_term if dv is None else dv + dv_term
            dk = dk_term if dk is None else dk + dk_term
            dq = dq_term if dq is None else dq + dq_term
        dq = dq * 0.125
        dk = dk * 0.125
        low = pair * 128
        out_vec[:, 2304 + low : 2304 + low + 128] = column_sum(dq)
        out_vec[:, 2688 + low : 2688 + low + 128] = column_sum(dv)
        out_dqkv[:, low : low + 128] = dq.astype(BF)
        out_dqkv[:, LOCAL + low : LOCAL + low + 128] = dk.astype(BF)
        out_dqkv[:, 2 * LOCAL + low : 2 * LOCAL + low + 128] = dv.astype(BF)
    out_dqkv.start()
    dx = None
    for j in range(3):
        term = mm(out_dqkv[:, j * LOCAL : (j + 1) * LOCAL], wq(j)[j], NT)
        dx = term if dx is None else dx + term
    out_dx[...] = dx.astype(BF)


def far_kernel(layer, chains, meta, *refs):
    low, *vecs, own_i, got_i, out_act, out_slope, wi, sems = refs
    span = low.shape[0] // chains
    is_own = meta.section == layer
    half = pl.ds(pl.multiple_of(meta.rep * HALF, HALF), HALF)
    wi = Weights(own_i, got_i, is_own, [(0, (slice(None), slice(None), half), None)], wi, sems)()
    for chain in range(chains):
        tag = meta.far_tag(chain)
        at = slice(chain * span, (chain + 1) * span)
        bias = vec_reader(vecs, is_own, tag)(pl.multiple_of(BIAS_IN + meta.rep * HALF, HALF), HALF)
        pre = mm(low[at, :], wi[tag]) + bias
        out_act[at, :], out_slope[at, :] = gelu_and_slope(pre)


def order_of(tags, section):
    mine = [(tag == section).astype(jnp.int32) for tag in tags]
    count = sum(mine)
    places, before = [], 0
    for index, one in enumerate(mine):
        places.append(jnp.where(one == 1, before, count + index - before))
        before = before + one
    return places, count


class Gathered:
    def __init__(self, sources, places, target, sems, first):
        self.place, self.copies = target, []
        for index, (source, place) in enumerate(zip(sources, places)):
            extent = source.shape[0]
            at = pl.ds(pl.multiple_of(place * extent, extent), extent)
            copy = pltpu.make_async_copy(source, target.at[at], sems.at[first + index])
            copy.start()
            self.copies.append(copy)

    def wait(self):
        for copy in self.copies:
            copy.wait()
        return self.place


def both_models(count, chains, span, left, rights, stores):
    def branch(number):
        def products():
            cut = number * span
            for right, store in zip(rights, stores):
                columns = right.shape[1]
                for keeping, rows in ((False, slice(cut, chains * span)), (True, slice(0, cut))):
                    if rows.start == rows.stop:
                        store(keeping, jnp.zeros((left.shape[0], columns), BF))
                    else:
                        store(keeping, mm(left[:, rows], right[rows, :]).astype(BF))

        return products

    for number in range(chains + 1):
        pl.when(count == number)(branch(number))


def feed_grad_kernel(layer, chains, meta, *refs):
    df, act, du, far_df = (refs[i * chains : (i + 1) * chains] for i in range(4))
    low, far_low, far_act, slope_from, own_d, got_d, *refs = refs[4 * chains :]
    keep, send, df_all, act_all, low_all, du_all, far_slope, wd, sems = refs
    span = df[0].shape[0]
    half = pl.ds(pl.multiple_of(meta.rep * HALF, HALF), HALF)
    is_own = meta.section == layer
    tags = [meta.tag(chain) for chain in range(chains)] + [meta.far_tag(chain) for chain in range(chains)]
    places, count = order_of(tags, meta.section)
    split = lambda rows: [rows.at[pl.ds(chain * span, span)] for chain in range(chains)]
    df_all = Gathered([*df, *far_df], places, df_all, sems, 0)
    act_all = Gathered([*act, *split(far_act)], places, act_all, sems, 2 * chains)
    wd = Weights(own_d, got_d, is_own, [(0, (slice(None), half), None)], wd, sems, 8 * chains)
    far_slope = Lazy(slope_from, far_slope, sems, 8 * chains + 1, 1)
    far_slope.start()
    du_all = Gathered(du, places, du_all, sems, 4 * chains)
    low_all = Gathered([*split(low), *split(far_low)], places, low_all, sems, 6 * chains)

    def products(left_all, at, right):
        def column_block(index, carry):
            rows = pl.ds(pl.multiple_of(index * BLOCK, BLOCK), BLOCK)
            left = left_all[:, rows].T

            def store(keeping, value):
                out = keep.place if keeping else send
                out[rows, at : at + HALF] = value

            both_models(count, 2 * chains, span, left, [right], [store])
            return carry

        lax.fori_loop(0, WIDTH // BLOCK, column_block, 0)
        keep.start(at // HALF)

    lefts = df_all.wait()
    products(lefts, 0, act_all.wait())
    rights = du_all.wait()
    weights = wd()
    for chain in range(chains):
        at = slice(chain * span, (chain + 1) * span)
        there = pl.ds(pl.multiple_of(places[chains + chain] * span, span), span)
        value = mm(lefts[there, :], weights[meta.far_tag(chain)], NT) * far_slope[at, :].astype(F32)
        rights[there, :] = value.astype(BF)
    products(low_all.wait(), HALF, rights)


def attention_grad_kernel(layer, chains, meta, *refs):
    dz, att, x, dqkv = (refs[i * chains : (i + 1) * chains] for i in range(4))
    keep, send, dz_all, att_all, x_all, dqkv_all, sems = refs[4 * chains :]
    span = dz[0].shape[0]
    if layer == 0:
        x = [ref.at[chain, meta.section] for chain, ref in enumerate(x)]
    places, count = order_of([meta.tag(chain) for chain in range(chains)], meta.section)
    dz_all = Gathered(dz, places, dz_all, sems, 0)
    att_all = Gathered(att, places, att_all, sems, chains)
    x_all = Gathered(x, places, x_all, sems, 2 * chains)
    dqkv_all = Gathered(dqkv, places, dqkv_all, sems, 3 * chains)

    def products(left_all, rights, targets):
        def column_block(index, carry):
            rows = pl.ds(pl.multiple_of(index * BLOCK, BLOCK), BLOCK)
            left = left_all[:, rows].T

            def store_at(slot, columns):
                def store(keeping, value):
                    out = keep.place if keeping else send
                    if layer == 1:
                        out[rows, columns.start + slot * HALF : columns.stop + slot * HALF] = value
                    else:
                        out[jnp.where(meta.rep == 0, slot, 1 - slot), rows, columns] = value

                return store

            both_models(count, chains, span, left, rights, [store_at(*target) for target in targets])
            return carry

        lax.fori_loop(0, WIDTH // BLOCK, column_block, 0)

    left_all, right = dz_all.wait(), att_all.wait()
    products(left_all, [right], [(0, slice(0, LOCAL))])
    left_all, right = x_all.wait(), dqkv_all.wait()
    rights = [right.at[:, pl.ds(0, LOCAL)], right.at[:, pl.ds(LOCAL, 2 * LOCAL)]]
    products(left_all, rights, [(0, slice(LOCAL, HALF)), (1, slice(0, HALF))])


def add_kernel(parts, meta, one, two, out):
    block = one.shape[0] // parts
    for part in range(parts):
        at = slice(part * block, (part + 1) * block)
        one.wait(part)
        out[at, :] = one.place[at, :] + two[at, :]
        out.start(part)


def add_halves_kernel(meta, one, two, near, far):
    for half, out in ((1, far), (0, near)):
        one.wait(half)
        out[...] = one.place[half] + two[half]


BLOCK = 256
ANY = pl.BlockSpec(memory_space=pl.ANY)


def pack_kernel(gains, shifts, b_qv, b_in, out):
    for model in range(2):
        row = slice(model, model + 1)
        for j in range(2):
            out[row, j * WIDTH : (j + 1) * WIDTH] = gains[0, model, j : j + 1, :]
            out[row, BIAS_Q + j * LOCAL : BIAS_Q + (j + 1) * LOCAL] = b_qv[0, model, j : j + 1, :]
        for j in range(4):
            out[row, SHIFT[j] : SHIFT[j] + WIDTH] = shifts[0, model, j : j + 1, :]
        out[row, BIAS_IN:] = b_in[0, row, :]


def feed_final_kernel(meta, *refs):
    zero, one, got, grad_in, grad_out = refs[:2], refs[2:4], refs[4], refs[5], refs[6]
    for half in range(2):
        local = jnp.where(meta.rep == 0, half, 1 - half)
        mine = jnp.where(meta.section == 0, zero[half][...], one[half][...]).astype(F32)
        columns = pl.ds(pl.multiple_of(local * HALF, HALF), HALF)
        for model, shard in ((meta.section, mine), (1 - meta.section, got[half].astype(F32))):
            grad_out[model, :, columns] = shard[:, 0:HALF]
            grad_in[model, :, columns] = shard[:, HALF:]


def attention_final_kernel(meta, *refs):
    zero, got_zero, (one, got_one, grad_qkv, grad_o) = refs[:2], refs[2:4], refs[4:]
    for model, halves, whole in ((meta.section, zero, one), (1 - meta.section, got_zero, got_one)):
        near, far = halves[0][...], halves[1][...]
        low = jnp.where(meta.rep == 0, near, far)
        high = jnp.where(meta.rep == 0, far, near)
        low = jnp.where(meta.section == 0, low, whole[:, 0:HALF]).astype(F32)
        high = jnp.where(meta.section == 0, high, whole[:, HALF:]).astype(F32)
        grad_o[model] = low[:, 0:LOCAL]
        grad_qkv[model, 0] = low[:, LOCAL:]
        grad_qkv[model, 1] = high[:, 0:LOCAL]
        grad_qkv[model, 2] = high[:, LOCAL:]


def vector_grad_kernel(chains, meta, *refs):
    out = refs[-1]
    for layer in range(2):
        ones = refs[2 * layer * chains : (2 * layer + 1) * chains]
        twos = refs[(2 * layer + 1) * chains : (2 * layer + 2) * chains]
        rows = [
            jnp.concatenate(
                [one[:, 0:768], two[:, 0:768], one[:, 768:2304], two[:, 768:2304], one[:, 2304:], two[:, 2304:]],
                axis=1,
            )
            for one, two in zip(ones, twos)
        ]
        for model in range(2):
            total = None
            for chain in range(chains):
                row = jnp.where(meta.tag(chain) == model, rows[chain], 0.0)
                total = row if total is None else total + row
            out[layer, model : model + 1, :] = total


STEP = 1.5e9
LONG = 8

VMEM = pl.BlockSpec(memory_space=pltpu.VMEM)
SMEM = pl.BlockSpec(memory_space=pltpu.SMEM)
SAVED, PARTLY = "saved", "partly"


def pieces_of(out):
    return out[3] if len(out) > 3 else [None]


def in_hbm(value):
    return pltpu.with_memory_space_constraint(value, pltpu.HBM)


def call(body, scalars, operands, outs, scratch, name, grant, cost):
    saved_in = [value for value in operands if isinstance(value, Saved)]
    saved_out = [out for out in outs if SAVED in out]
    buffers = [pltpu.VMEM(value.shape, value.value.dtype) for value in saved_in]
    buffers += [pltpu.VMEM(out[0], out[1]) for out in saved_out]
    counts = (len(scalars), len(operands), len(outs), len(scratch))

    def kernel(*refs):
        groups = []
        for count in counts:
            groups.append(refs[:count])
            refs = refs[count:]
        numbers, ins, results, own_scratch = groups
        *places, sems = refs
        meta = Scalars(*numbers)
        given, taken, index, sem = [], [], 0, 0
        for value, ref in zip(operands, ins):
            if isinstance(value, Saved):
                source = ref if value.chain is None else ref.at[value.chain, meta.section]
                ref = Lazy(source, places[index], sems, sem, value.parts)
                ref.start()
                sem += value.parts
                index += 1
            given.append(ref)
        for out, ref in zip(outs, results):
            if SAVED in out:
                ref = Leaving(places[index], ref, sems, sem, pieces_of(out))
                sem += len(pieces_of(out))
                index += 1
            taken.append(ref)
        body(meta, *given, *taken, *own_scratch)
        for ref in taken:
            if isinstance(ref, Leaving):
                ref.start()
        for ref in given:
            if isinstance(ref, Lazy):
                ref.wait()
        for ref in taken:
            if isinstance(ref, Leaving):
                ref.wait()

    in_specs = [ANY if isinstance(value, (tuple, Saved)) else VMEM for value in operands]
    values = []
    for value in operands:
        if isinstance(value, Saved):
            value = in_hbm(value.value)
        elif isinstance(value, tuple):
            value = in_hbm(value[0])
        values.append(value)
    shapes = [
        pltpu.HBM(*out[:2]) if SAVED in out or PARTLY in out else jax.ShapeDtypeStruct(*out[:2]) for out in outs
    ]
    return pl.pallas_call(
        kernel,
        out_shape=shapes,
        in_specs=[SMEM] * len(scalars) + in_specs,
        out_specs=[ANY if SAVED in out or PARTLY in out else VMEM for out in outs],
        input_output_aliases={
            len(scalars) + out[3]: index for index, out in enumerate(outs) if PARTLY in out and len(out) > 3
        },
        scratch_shapes=[*scratch, *buffers, pltpu.SemaphoreType.DMA((max(sum(value.parts for value in saved_in) + sum(len(pieces_of(out)) for out in saved_out), 1),))],
        compiler_params=pltpu.CompilerParams(vmem_limit_bytes=grant * 1024 * 1024),
        cost_estimate=pl.CostEstimate(flops=int(cost * STEP), bytes_accessed=1, transcendentals=0),
        name=name,
    )(*scalars, *values)


def on_device(
    block_input, cotangent, lengths, tags, w_qkv, w_o, w_in, w_out, b_qv, b_in, gains, shifts
):
    micro, per, span, width = block_input.shape
    section = lax.axis_index("section")
    rep = lax.axis_index("rep")
    chains = range(micro)
    layers = range(2)

    own_q, own_o, own_i, own_d = w_qkv[0], w_o[0], w_in[0], w_out[0]
    got_q = swap(own_q, "section")
    vec_own = pl.pallas_call(
        pack_kernel, out_shape=jax.ShapeDtypeStruct((2, PACKED), F32), in_specs=[VMEM] * 4, out_specs=VMEM, name="pack"
    )(gains, shifts, b_qv, b_in)
    numbers = jnp.concatenate([lengths, tags], axis=1)
    vec_own = after(vec_own, numbers)
    vecs = [vec_own, swap(vec_own, "section")]
    got_o = swap(own_o, "section")
    later = lax.optimization_barrier((own_i, own_d, got_q, got_o, vecs[1]))
    got_i, got_d = swap(later[0], "section"), swap(later[1], "section")

    heads = LOCAL // HD
    row, saved_row = ((span, WIDTH), BF), ((span, WIDTH), BF, SAVED)
    wide, saved_wide = ((span, WIDTH), F32), ((span, WIDTH), F32, SAVED)
    half_row, long_row = ((span, HALF), BF, SAVED), ((span, HIDDEN), BF, SAVED)
    qkv_row = ((span, 3 * LOCAL), BF, SAVED)
    att_outs = [qkv_row, ((heads, span, span), BF, SAVED), ((span, LOCAL), BF, SAVED), row]
    raw = lambda values: [(value,) for value in values]
    w_qo, w_id = raw([own_q, got_q, own_o, got_o]), raw([own_i, got_i, own_d, got_d])
    qo_scratch = [
        pltpu.VMEM((3, WIDTH, LOCAL), BF),
        pltpu.VMEM((LOCAL, WIDTH), BF),
        pltpu.SemaphoreType.DMA((4,)),
    ]
    id_scratch = [
        pltpu.VMEM((span, HIDDEN), BF),
        pltpu.VMEM((WIDTH, HIDDEN), BF),
        pltpu.VMEM((HIDDEN, WIDTH), BF),
        pltpu.SemaphoreType.DMA((3,)),
    ]
    feed_scratch = id_scratch[:3] + [pltpu.VMEM((span, WIDTH), BF), pltpu.SemaphoreType.DMA((4,))]

    last = [numbers]

    def run(body, operands, outs, scratch, name, *waits, far=False, grant=14, cost=1):
        scalars = [after(numbers, last[0], *waits)] + ([far_tags] if far else [])
        results = call(body, scalars, operands, outs, scratch, name, grant, cost)
        last[0] = results[-1]
        return results

    def saved(values):
        return [Saved(value) for value in values]

    def arrived(pair):
        return list(pair)

    def owned(zero, one):
        zero, one = jnp.stack(zero), jnp.stack(one)
        mine = jnp.where(section == 0, zero, one)
        other = swap(jnp.where(section == 0, one, zero), "section")
        core = lax.broadcasted_iota(jnp.int32, (micro, per, span, width), 1)
        return jnp.where(core == section, mine[:, None], other[:, None])[None]

    table = lambda: [[None] * micro for _ in layers]
    r1s, r2s, hiddens, acts, slopes, feeds, qkvs, probs, atts = (table() for _ in range(9))
    lows, far_lows = [None, None], [None, None]
    x_now, x_saved = [[Saved(block_input, chain) for chain in chains], [None] * micro], [None] * micro
    for layer in layers:
        for chain in chains:
            body = functools.partial(attention_kernel, layer, chain)
            name = f"attention{layer}{chain}"
            if layer == 0:
                got = run(body, [x_now[0][chain], *vecs] + w_qo, att_outs, qo_scratch, name)
            else:
                operands = [*arrived(feeds[0][chain]), hiddens[0][chain], *vecs] + w_qo
                waits = []
                x_now[1][chain], x_saved[chain], r2s[0][chain], *got = run(
                    body, operands, [row, saved_row, saved_wide] + att_outs, qo_scratch, name, *waits
                )
            qkvs[layer][chain], probs[layer][chain], atts[layer][chain], branch = got
            feeds[layer][chain] = (branch, swap(branch, "mp"))
        if layer == 0:
            far_tags = swap(after(tags, last[0]), "rep")
        for chain in chains:
            body = functools.partial(feed_kernel, layer, chain)
            waits = [far_tags] if layer == 0 and chain == 2 else []
            operands = [x_now[layer][chain], *feeds[layer][chain], *vecs] + w_id
            rows_out = ((micro * span, WIDTH), BF, PARTLY)
            if chain:
                rows_out += (len(operands),)
                operands.append((lows[layer],))
            hiddens[layer][chain], r1s[layer][chain], slopes[layer][chain], acts[layer][chain], lows[layer], part = run(
                body,
                operands,
                [wide, saved_wide, long_row, half_row, rows_out, row],
                feed_scratch,
                f"feed{layer}{chain}",
                *waits,
            )
            feeds[layer][chain] = (part, swap(part, "mp"))
        far_lows[layer] = swap(lows[layer], "rep")

    rows = micro * span
    far_rows = ((rows, HALF), BF, SAVED)
    dr2s, dfs, far_dfs, dus, dhs, vec_one, vec_two, dzs, dqkvs, dr1s, dxs, ys = (table() for _ in range(12))
    far_hidden = [None, None]

    def feed_back(layer, chain, *waits, cost=1):
        if layer == 1:
            operands = [*arrived(feeds[1][chain]), hiddens[1][chain], Saved(cotangent, chain)]
        else:
            operands = [*arrived(dxs[1][chain]), Saved(dr1s[1][chain]), Saved(r2s[0][chain])]
        ys[layer][chain], dr2s[layer][chain], df, dus[layer][chain], dh, vec_two[layer][chain] = run(
            functools.partial(feed_back_kernel, layer, chain),
            operands + [*vecs, Saved(slopes[layer][chain])] + w_id,
            [saved_row, saved_wide, saved_row, half_row, row, ((1, 3 * WIDTH + HIDDEN), F32, SAVED)],
            id_scratch,
            f"feed_back{layer}{chain}",
            *waits,
            cost=cost,
        )
        dfs[layer][chain], far_dfs[layer][chain] = df, swap(df, "rep")
        dhs[layer][chain] = (dh, swap(dh, "mp"))

    def attention_back(layer, chain, *waits, cost=1):
        dr1s[layer][chain], dzs[layer][chain], dqkvs[layer][chain], dx, vec_one[layer][chain] = run(
            functools.partial(attention_back_kernel, layer, chain),
            [*arrived(dhs[layer][chain]), Saved(dr2s[layer][chain]), Saved(r1s[layer][chain]), *vecs]
            + [Saved(qkvs[layer][chain]), Saved(probs[layer][chain])]
            + w_qo,
            [saved_wide, saved_row, qkv_row, row, ((1, 3 * WIDTH + 2 * LOCAL), F32, SAVED)],
            qo_scratch,
            f"attention_back{layer}{chain}",
            *waits,
            cost=cost,
        )
        dxs[layer][chain] = (dx, swap(dx, "mp"))

    def far_part(layer, *waits):
        far_hidden[layer] = run(
            functools.partial(far_kernel, layer, micro),
            [Saved(far_lows[layer]), *vecs] + w_id[:2],
            [far_rows] * 2,
            [pltpu.VMEM((2, WIDTH, HALF), BF), pltpu.SemaphoreType.DMA((1,))],
            f"far{layer}",
            *waits,
            far=True,
            cost=1.5,
        )

    def feed_grad(layer, *waits, cost=2):
        near = dfs[layer] + acts[layer] + dus[layer] + far_dfs[layer]
        far_act, far_slope = far_hidden[layer]
        stacked = pltpu.VMEM((2 * rows, HALF), BF)
        keep, send = run(
            functools.partial(feed_grad_kernel, layer, micro),
            raw(near + [lows[layer], far_lows[layer], far_act, far_slope]) + w_id[2:],
            [((WIDTH, HIDDEN), BF, SAVED, blocks_of(WIDTH, HIDDEN, WIDTH, HALF)), ((WIDTH, HIDDEN), BF)],
            [stacked] * 4
            + [pltpu.VMEM((rows, HALF), BF), pltpu.VMEM((2, HALF, WIDTH), BF), pltpu.SemaphoreType.DMA((8 * micro + 2,))],
            f"feed_grad{layer}",
            *waits,
            far=True,
            grant=20,
            cost=cost,
        )
        return keep, swap(send, "section")

    def whole_sum(name, parts, *waits):
        (result,) = run(
            functools.partial(add_kernel, WIDTH // BLOCK),
            [Saved(parts[0], parts=WIDTH // BLOCK), parts[1]],
            [((WIDTH, HIDDEN), BF, SAVED, blocks_of(WIDTH, HIDDEN, BLOCK, HIDDEN))],
            [],
            name,
            *waits,
        )
        return result

    def attention_grad(layer, *waits):
        x_part = raw([block_input] * micro if layer == 0 else x_saved)
        narrow, stacked = pltpu.VMEM((rows, LOCAL), BF), pltpu.VMEM((rows, WIDTH), BF)
        shape = (WIDTH, HIDDEN) if layer == 1 else (2, WIDTH, HALF)
        pieces = [None] if layer == 1 else [pl.ds(0, 1), pl.ds(1, 1)]
        keep, send = run(
            functools.partial(attention_grad_kernel, layer, micro),
            raw(dzs[layer] + atts[layer]) + x_part + raw(dqkvs[layer]),
            [(shape, BF, SAVED, pieces), (shape, BF)],
            [stacked, narrow, stacked, pltpu.VMEM((rows, 3 * LOCAL), BF), pltpu.SemaphoreType.DMA((4 * micro,))],
            f"attention_grad{layer}",
            *waits,
            cost=2,
        )
        return keep, swap(send, "section")

    def attention_grad_sum(layer, parts, *waits):
        near, far = run(
            add_halves_kernel,
            [Saved(parts[0], parts=2), parts[1]],
            [((WIDTH, HALF), BF, SAVED)] * 2,
            [],
            f"attention_grad_sum{layer}",
            *waits,
        )
        return near, swap(far, "rep")

    def scattered(part):
        return lax.psum_scatter(part, "dp", scatter_dimension=0, tiled=True)

    feed_back(1, 0, far_lows[0])
    feed_back(1, 1)
    feed_back(1, 2, cost=3)
    far_part(1, dhs[1][0][1], far_dfs[1][0])
    parts = feed_grad(1, dhs[1][1][1], far_dfs[1][1])
    attention_back(1, 0, dhs[1][2][1], cost=20)
    feed_one = scattered(whole_sum("feed_grad_sum1", parts))
    attention_back(1, 1)
    attention_back(1, 2, dxs[1][0][1])
    parts = attention_grad(1, dxs[1][1][1])
    far_part(0)
    attention_one = whole_sum("attention_grad_sum1", parts)
    feed_back(0, 0)
    feed_back(0, 1, dxs[1][2][1])
    attention_one = scattered(after(attention_one, feed_one, last[0]))
    feed_back(0, 2)
    attention_back(0, 0, feed_one, far_dfs[0][0], far_dfs[0][1])
    feed_one = (feed_one, swap(feed_one, "rep"))
    parts = feed_grad(0, dhs[0][2][1], dhs[0][1][1])
    attention_back(0, 1, cost=LONG)
    summed = whole_sum("feed_grad_sum0", parts)
    attention_one = after(attention_one, summed)
    feed_zero = scattered(after(summed, attention_one))
    attention_back(0, 2, attention_one, cost=2.75)
    attention_one = (attention_one, swap(after(attention_one, summed), "rep"))
    parts = attention_grad(0, feed_one[1])
    (both,) = run(
        functools.partial(vector_grad_kernel, micro),
        saved(vec_one[0] + vec_two[0] + vec_one[1] + vec_two[1]),
        [((2, 2, PACKED), F32)],
        [],
        "vector_grad",
        attention_one[1],
        *[dx[1] for dx in dxs[0][:2]],
        cost=20,
    )
    near, far = attention_grad_sum(0, parts)
    both = after(both, near)
    both = both + swap(both, "section")
    both = lax.dynamic_index_in_dim(both, section, 0, keepdims=False)
    data = lax.axis_size("dp")
    distance = 1
    while distance < data:
        both = both + lax.ppermute(both, "dp", [(i, i ^ distance) for i in range(data)])
        distance *= 2
    def first_grad(chain, *others):
        (own, got), dr1 = dxs[0][chain], dr1s[0][chain]
        return ((after(own, *others).astype(F32) + got.astype(F32)) + dr1).astype(BF)

    firsts = [first_grad(chain, near, both) for chain in chains[:-1]]
    firsts.append(first_grad(micro - 1, *firsts))
    attention_zero = after(after(near, firsts) + far, feed_zero)
    done = attention_zero
    both = both + swap(after(both, done), "rep")
    feed_zero = (feed_zero, swap(after(feed_zero, done), "rep"))
    attention_one = (after(attention_one[0], done).astype(F32) + attention_one[1].astype(F32)).astype(BF)
    feed_zero = (feed_zero[0], after(feed_zero[1], attention_one))
    layer_outputs = owned(after(x_saved, done), ys[1])
    grad_gains = both[:, : SHIFT[0]].reshape(2, 2, WIDTH)
    grad_shifts = both[:, SHIFT[0] : BIAS_Q].reshape(2, 4, WIDTH)
    grad_b_qv = both[:, BIAS_Q:BIAS_IN].reshape(2, 2, LOCAL)
    grad_b_in = both[:, BIAS_IN:]
    attention_zero = scattered(attention_zero)

    def handed(zero, one):
        return swap(jnp.where(section == 0, jnp.stack(one), jnp.stack(zero)), "section")

    shard = feed_zero[0].shape[0]
    grad_in, grad_out = run(
        feed_final_kernel,
        [*feed_zero, *feed_one, handed(feed_zero, feed_one)],
        [((2, shard, HIDDEN), F32)] * 2,
        [],
        "feed_final",
    )
    input_grads = owned(after(firsts, done), ys[0])
    got_one = swap(attention_one, "section")
    attention_zero = after(attention_zero, input_grads, layer_outputs, got_one)
    vectors = grad_b_qv[None], grad_b_in[None], grad_gains[None], grad_shifts[None]
    far, vectors, _ = lax.optimization_barrier((swap(attention_zero, "rep"), vectors, grad_in))
    got_zero = swap(attention_zero, "section"), swap(far, "section")
    attention_zero = (attention_zero, far)
    grad_qkv, grad_o = run(
        attention_final_kernel,
        [*attention_zero, *got_zero, attention_one, got_one],
        [((2, 3, shard, LOCAL), F32), ((2, shard, LOCAL), F32)],
        [],
        "attention_final",
    )
    grad_out, grad_o = jnp.swapaxes(grad_out, 1, 2), jnp.swapaxes(grad_o, 1, 2)

    return (
        layer_outputs,
        input_grads,
        grad_qkv[None],
        grad_o[None],
        grad_in[None],
        grad_out[None],
        *vectors,
    )


def solution(mesh):
    in_specs = (
        P(None, ("dp", "rep"), None, None),
        P(None, ("dp", "rep"), None, None),
        P(None, ("dp", "rep")),
        P(None, ("dp", "rep")),
        P("section", None, None, None, "mp"),
        P("section", None, "mp", None),
        P("section", None, None, "mp"),
        P("section", None, "mp", None),
        P("section", None, None, "mp"),
        P("section", None, "mp"),
        P("section", None, None, None),
        P("section", None, None, None),
    )
    out_specs = (
        P("section", None, ("dp", "rep"), None, None),
        P("section", None, ("dp", "rep"), None, None),
        P("section", None, None, "dp", "mp"),
        P("section", None, "mp", "dp"),
        P("section", None, "dp", "mp"),
        P("section", None, "mp", "dp"),
        P("section", None, None, "mp"),
        P("section", None, "mp"),
        P("section", None, None, None),
        P("section", None, None, None),
    )
    return jax.shard_map(
        on_device, mesh=mesh, in_specs=in_specs, out_specs=out_specs, check_vma=False
    )
```

```python
import functools

import jax
import jax.numpy as jnp
from jax import lax
from jax.experimental import pallas as pl
from jax.experimental.pallas import tpu as pltpu
from jax.sharding import PartitionSpec as P

HD = 64
EPS = 1e-05
BF = jnp.bfloat16
F32 = jnp.float32

GAIN_ONE, GAIN_TWO = 0, 768
SHIFT = (1536, 2304, 3072, 3840)
BIAS_Q, BIAS_V, BIAS_IN = 4608, 4992, 5376
PACKED = 6912
WIDTH, LOCAL, HIDDEN, HALF = 768, 384, 1536, 768

NN = (((1,), (0,)), ((), ()))
NT = (((1,), (1,)), ((), ()))
TN = (((0,), (0,)), ((), ()))


def mm(left, right, dims=NN):
    return lax.dot_general(left, right, dims, preferred_element_type=F32)


def swap(block, axis):
    return lax.ppermute(block, axis, [(0, 1), (1, 0)])


def after(value, *others):
    return lax.optimization_barrier((value, *others))[0]


class Lazy:
    def __init__(self, source, place, sems, first, parts):
        self.place, self.waited, self.copies = place, set(), []
        extent = place.shape[0] // parts
        for part in range(parts):
            at = pl.ds(part * extent, extent)
            near, away = (place, source) if parts == 1 else (place.at[at], source.at[at])
            self.copies.append(pltpu.make_async_copy(away, near, sems.at[first + part]))

    shape = property(lambda self: self.place.shape)

    def start(self):
        for copy in self.copies:
            copy.start()

    def wait(self, part=None):
        for index in range(len(self.copies)) if part is None else (part,):
            if index not in self.waited:
                self.copies[index].wait()
                self.waited.add(index)

    def __getitem__(self, at):
        self.wait()
        return self.place[at]


class Leaving:
    def __init__(self, place, target, sems, first, pieces):
        self.place, self.started, self.copies = place, set(), []
        for index, at in enumerate(pieces):
            near, away = (place, target) if at is None else (place.at[at], target.at[at])
            self.copies.append(pltpu.make_async_copy(near, away, sems.at[first + index]))

    shape = property(lambda self: self.place.shape)

    def start(self, piece=None):
        for index in range(len(self.copies)) if piece is None else (piece,):
            if index not in self.started:
                self.copies[index].start()
                self.started.add(index)

    def wait(self):
        for copy in self.copies:
            copy.wait()

    def __getitem__(self, at):
        return self.place[at]

    def __setitem__(self, at, value):
        self.place[at] = value
        if at is Ellipsis:
            self.start()


def blocks_of(rows, columns, row_step, column_step):
    return [
        (pl.ds(row, row_step), pl.ds(column, column_step))
        for column in range(0, columns, column_step)
        for row in range(0, rows, row_step)
    ]


class Saved:
    def __init__(self, value, chain=None, parts=1):
        self.value, self.chain, self.parts = value, chain, parts
        self.shape = value.shape if chain is None else value.shape[2:]


class Scalars:
    def __init__(self, numbers, far_tags=None):
        self.section, self.rep = lax.axis_index("section"), lax.axis_index("rep")
        self.numbers, self.far_tags = numbers, far_tags

    def length(self, chain):
        return self.numbers[chain, self.section]

    def tag(self, chain):
        return self.numbers[chain, 2 + self.section]

    def far_tag(self, chain):
        return self.far_tags[chain, self.section]


def layer_norm(resid):
    mean = jnp.mean(resid, -1, keepdims=True)
    centred = resid - mean
    inverse = lax.rsqrt(jnp.mean(centred * centred, -1, keepdims=True) + EPS)
    return centred * inverse, inverse


def layer_norm_back(grad, gain, normed, inverse):
    scaled = grad * gain
    return inverse * (
        scaled
        - jnp.mean(scaled, -1, keepdims=True)
        - normed * jnp.mean(scaled * normed, -1, keepdims=True)
    )


class Weights:
    def __init__(self, own, got, is_own, pieces, place, sems, first=0):
        self.place, self.copies, self.waited = place, {}, set()
        for index, (name, source, target) in enumerate(pieces):
            target = place.at[target] if target is not None else place
            near = pltpu.make_async_copy(own.at[source], target, sems.at[first + index])
            away = pltpu.make_async_copy(got.at[source], target, sems.at[first + index])
            self.copies[name] = near
            pl.when(is_own)(near.start)
            pl.when(jnp.logical_not(is_own))(away.start)

    def __call__(self, name=0):
        self.copies[name].wait()
        return self.place


def in_halves(tag, axis):
    pieces = []
    for half in range(2):
        at = pl.ds(half * HALF, HALF)
        at = (at,) if axis == 0 else (slice(None), at)
        pieces.append((half, (tag, *at), at))
    return pieces


def vec_reader(vecs, is_own, tag):
    own, got = vecs

    def read(at, extent=WIDTH):
        span = slice(at, at + extent) if isinstance(at, int) else pl.ds(at, extent)
        return jnp.where(is_own, own[pl.ds(tag, 1), span], got[pl.ds(tag, 1), span])

    return read


def gelu_and_slope(pre):
    cdf = 0.5 + 0.5 * lax.erf(pre * 0.7071067811865476)
    pdf = jnp.exp(pre * pre * -0.5) * 0.3989422804014327
    return (pre * cdf).astype(BF), (cdf + pre * pdf).astype(BF)


def column_sum(values):
    return jnp.sum(values, axis=0, keepdims=True)


def half_mask(values, which):
    lanes = lax.broadcasted_iota(jnp.int32, values.shape, 1)
    keep = (lanes < HD) if which == 0 else (lanes >= HD)
    return jnp.where(keep, values, jnp.zeros_like(values))


def attend(x, vector, length, wq, out_qkv, out_probs, out_att):
    span = x.shape[0]
    parts = []
    for j in range(3):
        value = mm(x, wq(j)[j])
        if j == 0:
            value = value + vector(BIAS_Q, LOCAL)
        if j == 2:
            value = value + vector(BIAS_V, LOCAL)
        value = value.astype(BF)
        out_qkv[:, j * LOCAL : (j + 1) * LOCAL] = value
        parts.append(value)
    out_qkv.start()
    query, key, value = parts
    keys = lax.broadcasted_iota(jnp.int32, (span, span), 0)
    usable = keys < length
    mixed = []
    for pair in range(LOCAL // 128):
        at = slice(pair * 128, pair * 128 + 128)
        total = None
        for which in range(2):
            scores = mm(half_mask(key[:, at], which), query[:, at], NT) * 0.125
            scores = jnp.where(usable, scores, -1e30)
            raised = jnp.exp(scores - jnp.max(scores, axis=0, keepdims=True))
            probs = (raised * (1.0 / jnp.sum(raised, axis=0, keepdims=True))).astype(BF)
            out_probs[2 * pair + which] = probs
            term = mm(probs, half_mask(value[:, at], which), TN)
            total = term if total is None else total + term
        mixed.append(total.astype(BF))
    out_probs.start()
    att = jnp.concatenate(mixed, axis=1)
    out_att[...] = att
    return att


def attention_kernel(layer, chain, meta, *refs):
    if layer == 0:
        x_ref, *vecs = refs[:3]
        refs = refs[3:]
    else:
        feed_own, feed_got, hidden, *vecs = refs[:5]
        refs = refs[5:]
    own_q, got_q, own_o, got_o, *refs, wq, wo, sems = refs
    if layer == 0:
        out_qkv, out_probs, out_att, out_branch = refs
    else:
        out_x, out_x_saved, out_r2, out_qkv, out_probs, out_att, out_branch = refs
    length, tag = meta.length(chain), meta.tag(chain)
    is_own = meta.section == layer
    vector = vec_reader(vecs, is_own, tag)
    wq = Weights(own_q, got_q, is_own, [(j, (tag, j), j) for j in range(3)], wq, sems)
    wo = Weights(own_o, got_o, is_own, [(0, tag, None)], wo, sems, 3)
    if layer == 0:
        x = x_ref[...]
    else:
        before = vec_reader(vecs, meta.section == 0, tag)
        r2 = hidden[...] + ((feed_own[...].astype(F32) + feed_got[...].astype(F32)) + before(SHIFT[2]))
        out_r2[...] = r2
        normed, _ = layer_norm(r2)
        x = (normed * before(GAIN_TWO) + before(SHIFT[3])).astype(BF)
        out_x[...] = x
        out_x_saved[...] = x
    att = attend(x, vector, length, wq, out_qkv, out_probs, out_att)
    out_branch[...] = mm(att, wo()[...]).astype(BF)


def feed_kernel(layer, chain, meta, x, own, got, *refs):
    *vecs, own_i, got_i, own_d, got_d = refs[:6]
    *_, out_hidden, out_r1, out_slope, out_act, out_low, out_feed, act, wi, wd, low_rows, sems = refs[6:]
    span = x.shape[0]
    tag = meta.tag(chain)
    is_own = meta.section == layer
    wi = Weights(own_i, got_i, is_own, in_halves(tag, 1), wi, sems)
    wd = Weights(own_d, got_d, is_own, [(0, tag, None)], wd, sems, 2)
    vector = vec_reader(vecs, is_own, tag)
    branch = (own[...].astype(F32) + got[...].astype(F32)) + vector(SHIFT[0])
    r1 = x[...].astype(F32) + branch
    out_r1[...] = r1
    normed, _ = layer_norm(r1)
    hidden = normed * vector(GAIN_ONE) + vector(SHIFT[1])
    out_hidden[...] = hidden
    low = hidden.astype(BF)
    low_rows[...] = low
    low_copy = pltpu.make_async_copy(low_rows, out_low.at[pl.ds(chain * span, span)], sems.at[3])
    low_copy.start()
    for half in range(2):
        at = half * HALF
        pre = mm(low, wi(half)[:, at : at + HALF]) + vector(BIAS_IN + at, HALF)
        act[:, at : at + HALF], out_slope[:, at : at + HALF] = gelu_and_slope(pre)

        @pl.when(meta.rep == half)
        def _():
            out_act[:, :] = act[:, at : at + HALF]

    out_act.start()
    out_slope.start()
    out_feed[...] = mm(act[...], wd()[...]).astype(BF)
    low_copy.wait()


def feed_back_kernel(layer, chain, meta, own, got, *refs):
    first, second, *vecs, act_slope, own_i, got_i, own_d, got_d = refs[:9]
    out_y, out_dr2, out_df, out_du, out_dh, out_vec, du_all, wi, wd, sems = refs[9:]
    length, tag = meta.length(chain), meta.tag(chain)
    is_own = meta.section == layer
    wd = Weights(own_d, got_d, is_own, in_halves(tag, 0), wd, sems)
    wi = Weights(own_i, got_i, is_own, [(0, tag, None)], wi, sems, 2)
    vector = vec_reader(vecs, is_own, tag)
    gain = vector(GAIN_TWO)
    both = own[...].astype(F32) + got[...].astype(F32)
    if layer == 1:
        hidden, cotangent = first, second
        normed, inverse = layer_norm(hidden[...] + (both + vector(SHIFT[2])))
        out_y[...] = (normed * gain + vector(SHIFT[3])).astype(BF)
        tokens = lax.broadcasted_iota(jnp.int32, both.shape, 0)
        dy = jnp.where(tokens < length, cotangent[...].astype(F32), 0.0)
    else:
        dr1, r2 = first, second
        low = (both + dr1[...]).astype(BF)
        out_y[...] = low
        dy = low.astype(F32)
        normed, inverse = layer_norm(r2[...])
    dr2 = layer_norm_back(dy, gain, normed, inverse)
    out_dr2[...] = dr2
    df = dr2.astype(BF)
    out_df[...] = df
    out_vec[0:1, 0:768] = column_sum(dy * normed)
    out_vec[0:1, 768:1536] = column_sum(dr2)
    out_vec[0:1, 1536:2304] = column_sum(dy)
    for half in range(2):
        at = half * HALF
        du = mm(df, wd(half)[at : at + HALF, :], NT) * act_slope[:, at : at + HALF].astype(F32)
        out_vec[0:1, 2304 + at : 2304 + at + HALF] = column_sum(du)
        du_all[:, at : at + HALF] = du.astype(BF)

        @pl.when(meta.rep == half)
        def _():
            out_du[:, :] = du_all[:, at : at + HALF]

    out_du.start()
    out_dh[...] = mm(du_all[...], wi()[...], NT).astype(BF)


def attention_back_kernel(layer, chain, meta, own, got, dr2, r1, *refs):
    *vecs, qkv, probs_ref, own_q, got_q, own_o, got_o = refs[:8]
    out_dr1, out_dz, out_dqkv, out_dx, out_vec, wq, wo, sems = refs[8:]
    tag = meta.tag(chain)
    is_own = meta.section == layer
    wo = Weights(own_o, got_o, is_own, [(0, tag, None)], wo, sems, 3)
    wq = Weights(own_q, got_q, is_own, [(j, (tag, j), j) for j in range(3)], wq, sems)
    vector = vec_reader(vecs, is_own, tag)
    dh = (own[...].astype(F32) + got[...].astype(F32)) + dr2[...]
    normed, inverse = layer_norm(r1[...])
    dr1 = layer_norm_back(dh, vector(GAIN_ONE), normed, inverse)
    out_dr1[...] = dr1
    dz = dr1.astype(BF)
    out_dz[...] = dz
    out_vec[0:1, 0:768] = column_sum(dh * normed)
    out_vec[0:1, 768:1536] = column_sum(dr1)
    out_vec[0:1, 1536:2304] = column_sum(dh)
    datt = mm(dz, wo()[...], NT).astype(BF)
    query, key, value = (qkv[:, j * LOCAL : (j + 1) * LOCAL] for j in range(3))
    for pair in range(LOCAL // 128):
        at = slice(pair * 128, pair * 128 + 128)
        dv = dq = dk = None
        for which in range(2):
            probs = probs_ref[2 * pair + which]
            dv_term = mm(probs, half_mask(datt[:, at], which))
            dprobs = mm(half_mask(value[:, at], which), datt[:, at], NT)
            wide = probs.astype(F32)
            dscores = wide * (dprobs - jnp.sum(wide * dprobs, axis=0, keepdims=True))
            dscores = dscores.astype(BF)
            dk_term = mm(dscores, half_mask(query[:, at], which))
            dq_term = mm(dscores, half_mask(key[:, at], which), TN)
            dv = dv_term if dv is None else dv + dv_term
            dk = dk_term if dk is None else dk + dk_term
            dq = dq_term if dq is None else dq + dq_term
        dq = dq * 0.125
        dk = dk * 0.125
        low = pair * 128
        out_vec[0:1, 2304 + low : 2304 + low + 128] = column_sum(dq)
        out_vec[0:1, 2688 + low : 2688 + low + 128] = column_sum(dv)
        out_dqkv[:, low : low + 128] = dq.astype(BF)
        out_dqkv[:, LOCAL + low : LOCAL + low + 128] = dk.astype(BF)
        out_dqkv[:, 2 * LOCAL + low : 2 * LOCAL + low + 128] = dv.astype(BF)
    out_dqkv.start()
    dx = None
    for j in range(3):
        term = mm(out_dqkv[:, j * LOCAL : (j + 1) * LOCAL], wq(j)[j], NT)
        dx = term if dx is None else dx + term
    out_dx[...] = dx.astype(BF)


def far_kernel(layer, chains, meta, *refs):
    low, *vecs, own_i, got_i, out_act, out_slope, wi, sems = refs
    span = low.shape[0] // chains
    is_own = meta.section == layer
    half = pl.ds(pl.multiple_of(meta.rep * HALF, HALF), HALF)
    wi = Weights(own_i, got_i, is_own, [(0, (slice(None), slice(None), half), None)], wi, sems)()
    for chain in range(chains):
        tag = meta.far_tag(chain)
        at = slice(chain * span, (chain + 1) * span)
        bias = vec_reader(vecs, is_own, tag)(pl.multiple_of(BIAS_IN + meta.rep * HALF, HALF), HALF)
        pre = mm(low[at, :], wi[tag]) + bias
        out_act[at, :], out_slope[at, :] = gelu_and_slope(pre)


def order_of(tags, section):
    mine = [(tag == section).astype(jnp.int32) for tag in tags]
    count = sum(mine)
    places, before = [], 0
    for index, one in enumerate(mine):
        places.append(jnp.where(one == 1, before, count + index - before))
        before = before + one
    return places, count


class Gathered:
    def __init__(self, sources, places, target, sems, first):
        self.place, self.copies = target, []
        for index, (source, place) in enumerate(zip(sources, places)):
            extent = source.shape[0]
            at = pl.ds(pl.multiple_of(place * extent, extent), extent)
            copy = pltpu.make_async_copy(source, target.at[at], sems.at[first + index])
            copy.start()
            self.copies.append(copy)

    def wait(self):
        for copy in self.copies:
            copy.wait()
        return self.place


def both_models(count, chains, span, left, rights, stores):
    def branch(number):
        def products():
            cut = number * span
            for right, store in zip(rights, stores):
                columns = right.shape[1]
                for keeping, rows in ((False, slice(cut, chains * span)), (True, slice(0, cut))):
                    if rows.start == rows.stop:
                        store(keeping, jnp.zeros((left.shape[0], columns), BF))
                    else:
                        store(keeping, mm(left[:, rows], right[rows, :]).astype(BF))

        return products

    for number in range(chains + 1):
        pl.when(count == number)(branch(number))


def feed_grad_kernel(layer, chains, meta, *refs):
    df, act, du, far_df = (refs[i * chains : (i + 1) * chains] for i in range(4))
    low, far_low, far_act, slope_from, own_d, got_d, *refs = refs[4 * chains :]
    keep, send, df_all, act_all, low_all, du_all, far_slope, wd, sems = refs
    span = df[0].shape[0]
    half = pl.ds(pl.multiple_of(meta.rep * HALF, HALF), HALF)
    is_own = meta.section == layer
    tags = [meta.tag(chain) for chain in range(chains)] + [meta.far_tag(chain) for chain in range(chains)]
    places, count = order_of(tags, meta.section)
    split = lambda rows: [rows.at[pl.ds(chain * span, span)] for chain in range(chains)]
    df_all = Gathered([*df, *far_df], places, df_all, sems, 0)
    act_all = Gathered([*act, *split(far_act)], places, act_all, sems, 2 * chains)
    wd = Weights(own_d, got_d, is_own, [(0, (slice(None), half), None)], wd, sems, 8 * chains)
    far_slope = Lazy(slope_from, far_slope, sems, 8 * chains + 1, 1)
    far_slope.start()
    du_all = Gathered(du, places, du_all, sems, 4 * chains)
    low_all = Gathered([*split(low), *split(far_low)], places, low_all, sems, 6 * chains)

    def products(left_all, at, right):
        def column_block(index, carry):
            rows = pl.ds(pl.multiple_of(index * BLOCK, BLOCK), BLOCK)
            left = left_all[:, rows].T

            def store(keeping, value):
                out = keep.place if keeping else send
                out[rows, at : at + HALF] = value

            both_models(count, 2 * chains, span, left, [right], [store])
            return carry

        lax.fori_loop(0, WIDTH // BLOCK, column_block, 0)
        keep.start(at // HALF)

    lefts = df_all.wait()
    products(lefts, 0, act_all.wait())
    rights = du_all.wait()
    weights = wd()
    for chain in range(chains):
        at = slice(chain * span, (chain + 1) * span)
        there = pl.ds(pl.multiple_of(places[chains + chain] * span, span), span)
        value = mm(lefts[there, :], weights[meta.far_tag(chain)], NT) * far_slope[at, :].astype(F32)
        rights[there, :] = value.astype(BF)
    products(low_all.wait(), HALF, rights)


def attention_grad_kernel(layer, chains, meta, *refs):
    dz, att, x, dqkv = (refs[i * chains : (i + 1) * chains] for i in range(4))
    keep, send, dz_all, att_all, x_all, dqkv_all, sems = refs[4 * chains :]
    span = dz[0].shape[0]
    if layer == 0:
        x = [ref.at[chain, meta.section] for chain, ref in enumerate(x)]
    places, count = order_of([meta.tag(chain) for chain in range(chains)], meta.section)
    dz_all = Gathered(dz, places, dz_all, sems, 0)
    att_all = Gathered(att, places, att_all, sems, chains)
    x_all = Gathered(x, places, x_all, sems, 2 * chains)
    dqkv_all = Gathered(dqkv, places, dqkv_all, sems, 3 * chains)

    def products(left_all, rights, targets):
        def column_block(index, carry):
            rows = pl.ds(pl.multiple_of(index * BLOCK, BLOCK), BLOCK)
            left = left_all[:, rows].T

            def store_at(slot, columns):
                def store(keeping, value):
                    out = keep.place if keeping else send
                    if layer == 1:
                        out[rows, columns.start + slot * HALF : columns.stop + slot * HALF] = value
                    else:
                        out[jnp.where(meta.rep == 0, slot, 1 - slot), rows, columns] = value

                return store

            both_models(count, chains, span, left, rights, [store_at(*target) for target in targets])
            return carry

        lax.fori_loop(0, WIDTH // BLOCK, column_block, 0)

    left_all, right = dz_all.wait(), att_all.wait()
    products(left_all, [right], [(0, slice(0, LOCAL))])
    left_all, right = x_all.wait(), dqkv_all.wait()
    rights = [right.at[:, pl.ds(0, LOCAL)], right.at[:, pl.ds(LOCAL, 2 * LOCAL)]]
    products(left_all, rights, [(0, slice(LOCAL, HALF)), (1, slice(0, HALF))])


def add_kernel(parts, meta, one, two, out):
    block = one.shape[0] // parts
    for part in range(parts):
        at = slice(part * block, (part + 1) * block)
        one.wait(part)
        out[at, :] = one.place[at, :] + two[at, :]
        out.start(part)


def add_halves_kernel(meta, one, two, near, far):
    for half, out in ((1, far), (0, near)):
        one.wait(half)
        out[...] = one.place[half] + two[half]


BLOCK = 256
ANY = pl.BlockSpec(memory_space=pl.ANY)


def pack_kernel(gains, shifts, b_qv, b_in, out):
    for model in range(2):
        row = slice(model, model + 1)
        for j in range(2):
            out[row, j * WIDTH : (j + 1) * WIDTH] = gains[0, model, j : j + 1, :]
            out[row, BIAS_Q + j * LOCAL : BIAS_Q + (j + 1) * LOCAL] = b_qv[0, model, j : j + 1, :]
        for j in range(4):
            out[row, SHIFT[j] : SHIFT[j] + WIDTH] = shifts[0, model, j : j + 1, :]
        out[row, BIAS_IN:] = b_in[0, row, :]


def feed_final_kernel(meta, *refs):
    zero, one, got, grad_in, grad_out = refs[:2], refs[2:4], refs[4], refs[5], refs[6]
    for half in range(2):
        local = jnp.where(meta.rep == 0, half, 1 - half)
        mine = jnp.where(meta.section == 0, zero[half][...], one[half][...]).astype(F32)
        columns = pl.ds(pl.multiple_of(local * HALF, HALF), HALF)
        for model, shard in ((meta.section, mine), (1 - meta.section, got[half].astype(F32))):
            grad_out[model, :, columns] = shard[:, 0:HALF]
            grad_in[model, :, columns] = shard[:, HALF:]


def attention_final_kernel(meta, *refs):
    zero, got_zero, (one, got_one, grad_qkv, grad_o) = refs[:2], refs[2:4], refs[4:]
    for model, halves, whole in ((meta.section, zero, one), (1 - meta.section, got_zero, got_one)):
        near, far = halves[0][...], halves[1][...]
        low = jnp.where(meta.rep == 0, near, far)
        high = jnp.where(meta.rep == 0, far, near)
        low = jnp.where(meta.section == 0, low, whole[:, 0:HALF]).astype(F32)
        high = jnp.where(meta.section == 0, high, whole[:, HALF:]).astype(F32)
        grad_o[model] = low[:, 0:LOCAL]
        grad_qkv[model, 0] = low[:, LOCAL:]
        grad_qkv[model, 1] = high[:, 0:LOCAL]
        grad_qkv[model, 2] = high[:, LOCAL:]


def vector_grad_kernel(chains, meta, *refs):
    out = refs[-1]
    for layer in range(2):
        ones = refs[2 * layer * chains : (2 * layer + 1) * chains]
        twos = refs[(2 * layer + 1) * chains : (2 * layer + 2) * chains]
        rows = [
            jnp.concatenate(
                [one[0:1, 0:768], two[0:1, 0:768], one[0:1, 768:2304], two[0:1, 768:2304], one[0:1, 2304:], two[0:1, 2304:]],
                axis=1,
            )
            for one, two in zip(ones, twos)
        ]
        for model in range(2):
            total = None
            for chain in range(chains):
                row = jnp.where(meta.tag(chain) == model, rows[chain], 0.0)
                total = row if total is None else total + row
            out[layer, model : model + 1, :] = total


STEP = 1.5e9
LONG = 8

VMEM = pl.BlockSpec(memory_space=pltpu.VMEM)
SMEM = pl.BlockSpec(memory_space=pltpu.SMEM)
SAVED, PARTLY = "saved", "partly"


def pieces_of(out):
    return out[3] if len(out) > 3 else [None]


def in_hbm(value):
    return pltpu.with_memory_space_constraint(value, pltpu.HBM)


def call(body, scalars, operands, outs, scratch, name, grant, cost):
    saved_in = [value for value in operands if isinstance(value, Saved)]
    saved_out = [out for out in outs if SAVED in out]
    buffers = [pltpu.VMEM(value.shape, value.value.dtype) for value in saved_in]
    buffers += [pltpu.VMEM(out[0], out[1]) for out in saved_out]
    counts = (len(scalars), len(operands), len(outs), len(scratch))

    def kernel(*refs):
        groups = []
        for count in counts:
            groups.append(refs[:count])
            refs = refs[count:]
        numbers, ins, results, own_scratch = groups
        *places, sems = refs
        meta = Scalars(*numbers)
        given, taken, index, sem = [], [], 0, 0
        for value, ref in zip(operands, ins):
            if isinstance(value, Saved):
                source = ref if value.chain is None else ref.at[value.chain, meta.section]
                ref = Lazy(source, places[index], sems, sem, value.parts)
                ref.start()
                sem += value.parts
                index += 1
            given.append(ref)
        for out, ref in zip(outs, results):
            if SAVED in out:
                ref = Leaving(places[index], ref, sems, sem, pieces_of(out))
                sem += len(pieces_of(out))
                index += 1
            taken.append(ref)
        body(meta, *given, *taken, *own_scratch)
        for ref in taken:
            if isinstance(ref, Leaving):
                ref.start()
        for ref in given:
            if isinstance(ref, Lazy):
                ref.wait()
        for ref in taken:
            if isinstance(ref, Leaving):
                ref.wait()

    in_specs = [ANY if isinstance(value, (tuple, Saved)) else VMEM for value in operands]
    values = []
    for value in operands:
        if isinstance(value, Saved):
            value = in_hbm(value.value)
        elif isinstance(value, tuple):
            value = in_hbm(value[0])
        values.append(value)
    shapes = [
        pltpu.HBM(*out[:2]) if SAVED in out or PARTLY in out else jax.ShapeDtypeStruct(*out[:2]) for out in outs
    ]
    return pl.pallas_call(
        kernel,
        out_shape=shapes,
        in_specs=[SMEM] * len(scalars) + in_specs,
        out_specs=[ANY if SAVED in out or PARTLY in out else VMEM for out in outs],
        input_output_aliases={
            len(scalars) + out[3]: index for index, out in enumerate(outs) if PARTLY in out and len(out) > 3
        },
        scratch_shapes=[*scratch, *buffers, pltpu.SemaphoreType.DMA((max(sum(value.parts for value in saved_in) + sum(len(pieces_of(out)) for out in saved_out), 1),))],
        compiler_params=pltpu.CompilerParams(vmem_limit_bytes=grant * 1024 * 1024),
        cost_estimate=pl.CostEstimate(flops=int(cost * STEP), bytes_accessed=1, transcendentals=0),
        name=name,
    )(*scalars, *values)


def on_device(
    block_input, cotangent, lengths, tags, w_qkv, w_o, w_in, w_out, b_qv, b_in, gains, shifts
):
    micro, per, span, width = block_input.shape
    section = lax.axis_index("section")
    rep = lax.axis_index("rep")
    chains = range(micro)
    layers = range(2)

    own_q, own_o, own_i, own_d = w_qkv[0], w_o[0], w_in[0], w_out[0]
    got_q = swap(own_q, "section")
    vec_own = pl.pallas_call(
        pack_kernel, out_shape=jax.ShapeDtypeStruct((2, PACKED), F32), in_specs=[VMEM] * 4, out_specs=VMEM, name="pack"
    )(gains, shifts, b_qv, b_in)
    numbers = jnp.concatenate([lengths, tags], axis=1)
    vec_own = after(vec_own, numbers)
    vecs = [vec_own, swap(vec_own, "section")]
    got_o = swap(own_o, "section")
    later = lax.optimization_barrier((own_i, own_d, got_q, got_o, vecs[1]))
    got_i, got_d = swap(later[0], "section"), swap(later[1], "section")

    heads = LOCAL // HD
    row, saved_row = ((span, WIDTH), BF), ((span, WIDTH), BF, SAVED)
    wide, saved_wide = ((span, WIDTH), F32), ((span, WIDTH), F32, SAVED)
    half_row, long_row = ((span, HALF), BF, SAVED), ((span, HIDDEN), BF, SAVED)
    qkv_row = ((span, 3 * LOCAL), BF, SAVED)
    att_outs = [qkv_row, ((heads, span, span), BF, SAVED), ((span, LOCAL), BF, SAVED), row]
    raw = lambda values: [(value,) for value in values]
    w_qo, w_id = raw([own_q, got_q, own_o, got_o]), raw([own_i, got_i, own_d, got_d])
    qo_scratch = [
        pltpu.VMEM((3, WIDTH, LOCAL), BF),
        pltpu.VMEM((LOCAL, WIDTH), BF),
        pltpu.SemaphoreType.DMA((4,)),
    ]
    id_scratch = [
        pltpu.VMEM((span, HIDDEN), BF),
        pltpu.VMEM((WIDTH, HIDDEN), BF),
        pltpu.VMEM((HIDDEN, WIDTH), BF),
        pltpu.SemaphoreType.DMA((3,)),
    ]
    feed_scratch = id_scratch[:3] + [pltpu.VMEM((span, WIDTH), BF), pltpu.SemaphoreType.DMA((4,))]

    last = [numbers]

    def run(body, operands, outs, scratch, name, *waits, far=False, grant=14, cost=1):
        scalars = [after(numbers, last[0], *waits)] + ([far_tags] if far else [])
        results = call(body, scalars, operands, outs, scratch, name, grant, cost)
        last[0] = results[-1]
        return results

    def saved(values):
        return [Saved(value) for value in values]

    def arrived(pair):
        return list(pair)

    def owned(zero, one):
        zero, one = jnp.stack(zero), jnp.stack(one)
        mine = jnp.where(section == 0, zero, one)
        other = swap(jnp.where(section == 0, one, zero), "section")
        core = lax.broadcasted_iota(jnp.int32, (micro, per, span, width), 1)
        return jnp.where(core == section, mine[:, None], other[:, None])[None]

    table = lambda: [[None] * micro for _ in layers]
    r1s, r2s, hiddens, acts, slopes, feeds, qkvs, probs, atts = (table() for _ in range(9))
    lows, far_lows = [None, None], [None, None]
    x_now, x_saved = [[Saved(block_input, chain) for chain in chains], [None] * micro], [None] * micro
    for layer in layers:
        for chain in chains:
            body = functools.partial(attention_kernel, layer, chain)
            name = f"attention{layer}{chain}"
            if layer == 0:
                got = run(body, [x_now[0][chain], *vecs] + w_qo, att_outs, qo_scratch, name)
            else:
                operands = [*arrived(feeds[0][chain]), hiddens[0][chain], *vecs] + w_qo
                waits = []
                x_now[1][chain], x_saved[chain], r2s[0][chain], *got = run(
                    body, operands, [row, saved_row, saved_wide] + att_outs, qo_scratch, name, *waits
                )
            qkvs[layer][chain], probs[layer][chain], atts[layer][chain], branch = got
            feeds[layer][chain] = (branch, swap(branch, "mp"))
        if layer == 0:
            far_tags = swap(after(tags, last[0]), "rep")
        for chain in chains:
            body = functools.partial(feed_kernel, layer, chain)
            waits = [far_tags] if layer == 0 and chain == 2 else []
            operands = [x_now[layer][chain], *feeds[layer][chain], *vecs] + w_id
            rows_out = ((micro * span, WIDTH), BF, PARTLY)
            if chain:
                rows_out += (len(operands),)
                operands.append((lows[layer],))
            hiddens[layer][chain], r1s[layer][chain], slopes[layer][chain], acts[layer][chain], lows[layer], part = run(
                body,
                operands,
                [wide, saved_wide, long_row, half_row, rows_out, row],
                feed_scratch,
                f"feed{layer}{chain}",
                *waits,
            )
            feeds[layer][chain] = (part, swap(part, "mp"))
        far_lows[layer] = swap(lows[layer], "rep")

    rows = micro * span
    far_rows = ((rows, HALF), BF, SAVED)
    dr2s, dfs, far_dfs, dus, dhs, vec_one, vec_two, dzs, dqkvs, dr1s, dxs, ys = (table() for _ in range(12))
    far_hidden = [None, None]

    def feed_back(layer, chain, *waits, cost=1):
        if layer == 1:
            operands = [*arrived(feeds[1][chain]), hiddens[1][chain], Saved(cotangent, chain)]
        else:
            operands = [*arrived(dxs[1][chain]), Saved(dr1s[1][chain]), Saved(r2s[0][chain])]
        ys[layer][chain], dr2s[layer][chain], df, dus[layer][chain], dh, vec_two[layer][chain] = run(
            functools.partial(feed_back_kernel, layer, chain),
            operands + [*vecs, Saved(slopes[layer][chain])] + w_id,
            [saved_row, saved_wide, saved_row, half_row, row, ((8, 3 * WIDTH + HIDDEN), F32, SAVED)],
            id_scratch,
            f"feed_back{layer}{chain}",
            *waits,
            cost=cost,
        )
        dfs[layer][chain], far_dfs[layer][chain] = df, swap(df, "rep")
        dhs[layer][chain] = (dh, swap(dh, "mp"))

    def attention_back(layer, chain, *waits, cost=1):
        dr1s[layer][chain], dzs[layer][chain], dqkvs[layer][chain], dx, vec_one[layer][chain] = run(
            functools.partial(attention_back_kernel, layer, chain),
            [*arrived(dhs[layer][chain]), Saved(dr2s[layer][chain]), Saved(r1s[layer][chain]), *vecs]
            + [Saved(qkvs[layer][chain]), Saved(probs[layer][chain])]
            + w_qo,
            [saved_wide, saved_row, qkv_row, row, ((8, 3 * WIDTH + 2 * LOCAL), F32, SAVED)],
            qo_scratch,
            f"attention_back{layer}{chain}",
            *waits,
            cost=cost,
        )
        dxs[layer][chain] = (dx, swap(dx, "mp"))

    def far_part(layer, *waits):
        far_hidden[layer] = run(
            functools.partial(far_kernel, layer, micro),
            [Saved(far_lows[layer]), *vecs] + w_id[:2],
            [far_rows] * 2,
            [pltpu.VMEM((2, WIDTH, HALF), BF), pltpu.SemaphoreType.DMA((1,))],
            f"far{layer}",
            *waits,
            far=True,
            cost=1.5,
        )

    def feed_grad(layer, *waits, cost=2):
        near = dfs[layer] + acts[layer] + dus[layer] + far_dfs[layer]
        far_act, far_slope = far_hidden[layer]
        stacked = pltpu.VMEM((2 * rows, HALF), BF)
        keep, send = run(
            functools.partial(feed_grad_kernel, layer, micro),
            raw(near + [lows[layer], far_lows[layer], far_act, far_slope]) + w_id[2:],
            [((WIDTH, HIDDEN), BF, SAVED, blocks_of(WIDTH, HIDDEN, WIDTH, HALF)), ((WIDTH, HIDDEN), BF)],
            [stacked] * 4
            + [pltpu.VMEM((rows, HALF), BF), pltpu.VMEM((2, HALF, WIDTH), BF), pltpu.SemaphoreType.DMA((8 * micro + 2,))],
            f"feed_grad{layer}",
            *waits,
            far=True,
            grant=20,
            cost=cost,
        )
        return keep, swap(send, "section")

    def whole_sum(name, parts, *waits):
        (result,) = run(
            functools.partial(add_kernel, WIDTH // BLOCK),
            [Saved(parts[0], parts=WIDTH // BLOCK), parts[1]],
            [((WIDTH, HIDDEN), BF, SAVED, blocks_of(WIDTH, HIDDEN, BLOCK, HIDDEN))],
            [],
            name,
            *waits,
        )
        return result

    def attention_grad(layer, *waits):
        x_part = raw([block_input] * micro if layer == 0 else x_saved)
        narrow, stacked = pltpu.VMEM((rows, LOCAL), BF), pltpu.VMEM((rows, WIDTH), BF)
        shape = (WIDTH, HIDDEN) if layer == 1 else (2, WIDTH, HALF)
        pieces = [None] if layer == 1 else [pl.ds(0, 1), pl.ds(1, 1)]
        keep, send = run(
            functools.partial(attention_grad_kernel, layer, micro),
            raw(dzs[layer] + atts[layer]) + x_part + raw(dqkvs[layer]),
            [(shape, BF, SAVED, pieces), (shape, BF)],
            [stacked, narrow, stacked, pltpu.VMEM((rows, 3 * LOCAL), BF), pltpu.SemaphoreType.DMA((4 * micro,))],
            f"attention_grad{layer}",
            *waits,
            cost=2,
        )
        return keep, swap(send, "section")

    def attention_grad_sum(layer, parts, *waits):
        near, far = run(
            add_halves_kernel,
            [Saved(parts[0], parts=2), parts[1]],
            [((WIDTH, HALF), BF, SAVED)] * 2,
            [],
            f"attention_grad_sum{layer}",
            *waits,
        )
        return near, swap(far, "rep")

    def scattered(part):
        return lax.psum_scatter(part, "dp", scatter_dimension=0, tiled=True)

    feed_back(1, 0, far_lows[0])
    feed_back(1, 1)
    feed_back(1, 2, cost=3)
    far_part(1, dhs[1][0][1], far_dfs[1][0])
    parts = feed_grad(1, dhs[1][1][1], far_dfs[1][1])
    attention_back(1, 0, dhs[1][2][1], cost=20)
    feed_one = scattered(whole_sum("feed_grad_sum1", parts))
    attention_back(1, 1)
    attention_back(1, 2, dxs[1][0][1])
    parts = attention_grad(1, dxs[1][1][1])
    far_part(0)
    attention_one = whole_sum("attention_grad_sum1", parts)
    feed_back(0, 0)
    feed_back(0, 1, dxs[1][2][1])
    attention_one = scattered(after(attention_one, feed_one, last[0]))
    feed_back(0, 2)
    attention_back(0, 0, feed_one, far_dfs[0][0], far_dfs[0][1])
    feed_one = (feed_one, swap(feed_one, "rep"))
    parts = feed_grad(0, dhs[0][2][1], dhs[0][1][1])
    attention_back(0, 1, cost=LONG)
    summed = whole_sum("feed_grad_sum0", parts)
    attention_one = after(attention_one, summed)
    feed_zero = scattered(after(summed, attention_one))
    attention_back(0, 2, attention_one, cost=2.75)
    attention_one = (attention_one, swap(after(attention_one, summed), "rep"))
    parts = attention_grad(0, feed_one[1])
    (both,) = run(
        functools.partial(vector_grad_kernel, micro),
        saved(vec_one[0] + vec_two[0] + vec_one[1] + vec_two[1]),
        [((2, 2, PACKED), F32)],
        [],
        "vector_grad",
        attention_one[1],
        *[dx[1] for dx in dxs[0][:2]],
        cost=20,
    )
    near, far = attention_grad_sum(0, parts)
    both = after(both, near)
    both = both + swap(both, "section")
    both = lax.dynamic_index_in_dim(both, section, 0, keepdims=False)
    data = lax.axis_size("dp")
    distance = 1
    while distance < data:
        both = both + lax.ppermute(both, "dp", [(i, i ^ distance) for i in range(data)])
        distance *= 2
    def first_grad(chain, *others):
        (own, got), dr1 = dxs[0][chain], dr1s[0][chain]
        return ((after(own, *others).astype(F32) + got.astype(F32)) + dr1).astype(BF)

    firsts = [first_grad(chain, near, both) for chain in chains[:-1]]
    firsts.append(first_grad(micro - 1, *firsts))
    attention_zero = after(after(near, firsts) + far, feed_zero)
    done = attention_zero
    both = both + swap(after(both, done), "rep")
    feed_zero = (feed_zero, swap(after(feed_zero, done), "rep"))
    attention_one = (after(attention_one[0], done).astype(F32) + attention_one[1].astype(F32)).astype(BF)
    feed_zero = (feed_zero[0], after(feed_zero[1], attention_one))
    layer_outputs = owned(after(x_saved, done), ys[1])
    grad_gains = both[:, : SHIFT[0]].reshape(2, 2, WIDTH)
    grad_shifts = both[:, SHIFT[0] : BIAS_Q].reshape(2, 4, WIDTH)
    grad_b_qv = both[:, BIAS_Q:BIAS_IN].reshape(2, 2, LOCAL)
    grad_b_in = both[:, BIAS_IN:]
    attention_zero = scattered(attention_zero)

    def handed(zero, one):
        return swap(jnp.where(section == 0, jnp.stack(one), jnp.stack(zero)), "section")

    shard = feed_zero[0].shape[0]
    grad_in, grad_out = run(
        feed_final_kernel,
        [*feed_zero, *feed_one, handed(feed_zero, feed_one)],
        [((2, shard, HIDDEN), F32)] * 2,
        [],
        "feed_final",
    )
    input_grads = owned(after(firsts, done), ys[0])
    got_one = swap(attention_one, "section")
    attention_zero = after(attention_zero, input_grads, layer_outputs, got_one)
    vectors = grad_b_qv[None], grad_b_in[None], grad_gains[None], grad_shifts[None]
    far, vectors, _ = lax.optimization_barrier((swap(attention_zero, "rep"), vectors, grad_in))
    got_zero = swap(attention_zero, "section"), swap(far, "section")
    attention_zero = (attention_zero, far)
    grad_qkv, grad_o = run(
        attention_final_kernel,
        [*attention_zero, *got_zero, attention_one, got_one],
        [((2, 3, shard, LOCAL), F32), ((2, shard, LOCAL), F32)],
        [],
        "attention_final",
    )
    grad_out, grad_o = jnp.swapaxes(grad_out, 1, 2), jnp.swapaxes(grad_o, 1, 2)

    return (
        layer_outputs,
        input_grads,
        grad_qkv[None],
        grad_o[None],
        grad_in[None],
        grad_out[None],
        *vectors,
    )


def solution(mesh):
    in_specs = (
        P(None, ("dp", "rep"), None, None),
        P(None, ("dp", "rep"), None, None),
        P(None, ("dp", "rep")),
        P(None, ("dp", "rep")),
        P("section", None, None, None, "mp"),
        P("section", None, "mp", None),
        P("section", None, None, "mp"),
        P("section", None, "mp", None),
        P("section", None, None, "mp"),
        P("section", None, "mp"),
        P("section", None, None, None),
        P("section", None, None, None),
    )
    out_specs = (
        P("section", None, ("dp", "rep"), None, None),
        P("section", None, ("dp", "rep"), None, None),
        P("section", None, None, "dp", "mp"),
        P("section", None, "mp", "dp"),
        P("section", None, "dp", "mp"),
        P("section", None, "mp", "dp"),
        P("section", None, None, "mp"),
        P("section", None, "mp"),
        P("section", None, None, None),
        P("section", None, None, None),
    )
    return jax.shard_map(
        on_device, mesh=mesh, in_specs=in_specs, out_specs=out_specs, check_vma=False
    )
```

```python
import functools

import jax
import jax.numpy as jnp
from jax import lax
from jax.experimental import pallas as pl
from jax.experimental.pallas import tpu as pltpu
from jax.sharding import PartitionSpec as P

HD = 64
EPS = 1e-05
BF = jnp.bfloat16
F32 = jnp.float32

GAIN_ONE, GAIN_TWO = 0, 768
SHIFT = (1536, 2304, 3072, 3840)
BIAS_Q, BIAS_V, BIAS_IN = 4608, 4992, 5376
PACKED = 6912
WIDTH, LOCAL, HIDDEN, HALF = 768, 384, 1536, 768

NN = (((1,), (0,)), ((), ()))
NT = (((1,), (1,)), ((), ()))
TN = (((0,), (0,)), ((), ()))


def mm(left, right, dims=NN):
    return lax.dot_general(left, right, dims, preferred_element_type=F32)


def swap(block, axis):
    return lax.ppermute(block, axis, [(0, 1), (1, 0)])


def after(value, *others):
    return lax.optimization_barrier((value, *others))[0]


class Lazy:
    def __init__(self, source, place, sems, first, parts):
        self.place, self.waited, self.copies = place, set(), []
        extent = place.shape[0] // parts
        for part in range(parts):
            at = pl.ds(part * extent, extent)
            near, away = (place, source) if parts == 1 else (place.at[at], source.at[at])
            self.copies.append(pltpu.make_async_copy(away, near, sems.at[first + part]))

    shape = property(lambda self: self.place.shape)

    def start(self):
        for copy in self.copies:
            copy.start()

    def wait(self, part=None):
        for index in range(len(self.copies)) if part is None else (part,):
            if index not in self.waited:
                self.copies[index].wait()
                self.waited.add(index)

    def __getitem__(self, at):
        self.wait()
        return self.place[at]


class Leaving:
    def __init__(self, place, target, sems, first, pieces):
        self.place, self.started, self.copies = place, set(), []
        for index, at in enumerate(pieces):
            near, away = (place, target) if at is None else (place.at[at], target.at[at])
            self.copies.append(pltpu.make_async_copy(near, away, sems.at[first + index]))

    shape = property(lambda self: self.place.shape)

    def start(self, piece=None):
        for index in range(len(self.copies)) if piece is None else (piece,):
            if index not in self.started:
                self.copies[index].start()
                self.started.add(index)

    def wait(self):
        for copy in self.copies:
            copy.wait()

    def __getitem__(self, at):
        return self.place[at]

    def __setitem__(self, at, value):
        self.place[at] = value
        if at is Ellipsis:
            self.start()


def blocks_of(rows, columns, row_step, column_step):
    return [
        (pl.ds(row, row_step), pl.ds(column, column_step))
        for column in range(0, columns, column_step)
        for row in range(0, rows, row_step)
    ]


class Saved:
    def __init__(self, value, chain=None, parts=1):
        self.value, self.chain, self.parts = value, chain, parts
        self.shape = value.shape if chain is None else value.shape[2:]


class Scalars:
    def __init__(self, numbers, far_tags=None):
        self.section, self.rep = lax.axis_index("section"), lax.axis_index("rep")
        self.numbers, self.far_tags = numbers, far_tags

    def length(self, chain):
        return self.numbers[chain, self.section]

    def tag(self, chain):
        return self.numbers[chain, 2 + self.section]

    def far_tag(self, chain):
        return self.far_tags[chain, self.section]


def layer_norm(resid):
    mean = jnp.mean(resid, -1, keepdims=True)
    centred = resid - mean
    inverse = lax.rsqrt(jnp.mean(centred * centred, -1, keepdims=True) + EPS)
    return centred * inverse, inverse


def layer_norm_back(grad, gain, normed, inverse):
    scaled = grad * gain
    return inverse * (
        scaled
        - jnp.mean(scaled, -1, keepdims=True)
        - normed * jnp.mean(scaled * normed, -1, keepdims=True)
    )


class Weights:
    def __init__(self, own, got, is_own, pieces, place, sems, first=0):
        self.place, self.copies, self.waited = place, {}, set()
        for index, (name, source, target) in enumerate(pieces):
            target = place.at[target] if target is not None else place
            near = pltpu.make_async_copy(own.at[source], target, sems.at[first + index])
            away = pltpu.make_async_copy(got.at[source], target, sems.at[first + index])
            self.copies[name] = near
            pl.when(is_own)(near.start)
            pl.when(jnp.logical_not(is_own))(away.start)

    def __call__(self, name=0):
        self.copies[name].wait()
        return self.place


def in_halves(tag, axis):
    pieces = []
    for half in range(2):
        at = pl.ds(half * HALF, HALF)
        at = (at,) if axis == 0 else (slice(None), at)
        pieces.append((half, (tag, *at), at))
    return pieces


def vec_reader(vecs, is_own, tag):
    own, got = vecs

    def read(at, extent=WIDTH):
        span = slice(at, at + extent) if isinstance(at, int) else pl.ds(at, extent)
        return jnp.where(is_own, own[pl.ds(tag, 1), span], got[pl.ds(tag, 1), span])

    return read


def gelu_and_slope(pre):
    cdf = 0.5 + 0.5 * lax.erf(pre * 0.7071067811865476)
    pdf = jnp.exp(pre * pre * -0.5) * 0.3989422804014327
    return (pre * cdf).astype(BF), (cdf + pre * pdf).astype(BF)


def column_sum(values):
    return jnp.sum(values, axis=0, keepdims=True)


def half_mask(values, which):
    lanes = lax.broadcasted_iota(jnp.int32, values.shape, 1)
    keep = (lanes < HD) if which == 0 else (lanes >= HD)
    return jnp.where(keep, values, jnp.zeros_like(values))


def attend(x, vector, length, wq, out_qkv, out_probs, out_att):
    span = x.shape[0]
    parts = []
    for j in range(3):
        value = mm(x, wq(j)[j])
        if j == 0:
            value = value + vector(BIAS_Q, LOCAL)
        if j == 2:
            value = value + vector(BIAS_V, LOCAL)
        value = value.astype(BF)
        out_qkv[:, j * LOCAL : (j + 1) * LOCAL] = value
        parts.append(value)
    out_qkv.start()
    query, key, value = parts
    keys = lax.broadcasted_iota(jnp.int32, (span, span), 0)
    usable = keys < length
    mixed = []
    for pair in range(LOCAL // 128):
        at = slice(pair * 128, pair * 128 + 128)
        total = None
        for which in range(2):
            scores = mm(half_mask(key[:, at], which), query[:, at], NT) * 0.125
            scores = jnp.where(usable, scores, -1e30)
            raised = jnp.exp(scores - jnp.max(scores, axis=0, keepdims=True))
            probs = (raised * (1.0 / jnp.sum(raised, axis=0, keepdims=True))).astype(BF)
            out_probs[2 * pair + which] = probs
            term = mm(probs, half_mask(value[:, at], which), TN)
            total = term if total is None else total + term
        mixed.append(total.astype(BF))
    out_probs.start()
    att = jnp.concatenate(mixed, axis=1)
    out_att[...] = att
    return att


def attention_kernel(layer, chain, meta, *refs):
    if layer == 0:
        x_ref, *vecs = refs[:3]
        refs = refs[3:]
    else:
        feed_own, feed_got, hidden, *vecs = refs[:5]
        refs = refs[5:]
    own_q, got_q, own_o, got_o, *refs, wq, wo, sems = refs
    if layer == 0:
        out_qkv, out_probs, out_att, out_branch = refs
    else:
        out_x, out_x_saved, out_r2, out_qkv, out_probs, out_att, out_branch = refs
    length, tag = meta.length(chain), meta.tag(chain)
    is_own = meta.section == layer
    vector = vec_reader(vecs, is_own, tag)
    wq = Weights(own_q, got_q, is_own, [(j, (tag, j), j) for j in range(3)], wq, sems)
    wo = Weights(own_o, got_o, is_own, [(0, tag, None)], wo, sems, 3)
    if layer == 0:
        x = x_ref[...]
    else:
        before = vec_reader(vecs, meta.section == 0, tag)
        r2 = hidden[...] + ((feed_own[...].astype(F32) + feed_got[...].astype(F32)) + before(SHIFT[2]))
        out_r2[...] = r2
        normed, _ = layer_norm(r2)
        x = (normed * before(GAIN_TWO) + before(SHIFT[3])).astype(BF)
        out_x[...] = x
        out_x_saved[...] = x
    att = attend(x, vector, length, wq, out_qkv, out_probs, out_att)
    out_branch[...] = mm(att, wo()[...]).astype(BF)


def feed_kernel(layer, chain, meta, x, own, got, *refs):
    *vecs, own_i, got_i, own_d, got_d = refs[:6]
    *_, out_hidden, out_r1, out_slope, out_act, out_low, out_feed, act, wi, wd, low_rows, sems = refs[6:]
    span = x.shape[0]
    tag = meta.tag(chain)
    is_own = meta.section == layer
    wi = Weights(own_i, got_i, is_own, in_halves(tag, 1), wi, sems)
    wd = Weights(own_d, got_d, is_own, [(0, tag, None)], wd, sems, 2)
    vector = vec_reader(vecs, is_own, tag)
    branch = (own[...].astype(F32) + got[...].astype(F32)) + vector(SHIFT[0])
    r1 = x[...].astype(F32) + branch
    out_r1[...] = r1
    normed, _ = layer_norm(r1)
    hidden = normed * vector(GAIN_ONE) + vector(SHIFT[1])
    out_hidden[...] = hidden
    low = hidden.astype(BF)
    low_rows[...] = low
    low_copy = pltpu.make_async_copy(low_rows, out_low.at[pl.ds(chain * span, span)], sems.at[3])
    low_copy.start()
    for half in range(2):
        at = half * HALF
        pre = mm(low, wi(half)[:, at : at + HALF]) + vector(BIAS_IN + at, HALF)
        act[:, at : at + HALF], out_slope[:, at : at + HALF] = gelu_and_slope(pre)

        @pl.when(meta.rep == half)
        def _():
            out_act[:, :] = act[:, at : at + HALF]

    out_act.start()
    out_slope.start()
    out_feed[...] = mm(act[...], wd()[...]).astype(BF)
    low_copy.wait()


def feed_back_kernel(layer, chain, meta, own, got, *refs):
    first, second, *vecs, act_slope, own_i, got_i, own_d, got_d = refs[:9]
    out_y, out_dr2, out_df, out_du, out_dh, out_vec, du_all, wi, wd, sems = refs[9:]
    length, tag = meta.length(chain), meta.tag(chain)
    is_own = meta.section == layer
    wd = Weights(own_d, got_d, is_own, in_halves(tag, 0), wd, sems)
    wi = Weights(own_i, got_i, is_own, [(0, tag, None)], wi, sems, 2)
    vector = vec_reader(vecs, is_own, tag)
    gain = vector(GAIN_TWO)
    both = own[...].astype(F32) + got[...].astype(F32)
    if layer == 1:
        hidden, cotangent = first, second
        normed, inverse = layer_norm(hidden[...] + (both + vector(SHIFT[2])))
        out_y[...] = (normed * gain + vector(SHIFT[3])).astype(BF)
        tokens = lax.broadcasted_iota(jnp.int32, both.shape, 0)
        dy = jnp.where(tokens < length, cotangent[...].astype(F32), 0.0)
    else:
        dr1, r2 = first, second
        low = (both + dr1[...]).astype(BF)
        out_y[...] = low
        dy = low.astype(F32)
        normed, inverse = layer_norm(r2[...])
    dr2 = layer_norm_back(dy, gain, normed, inverse)
    out_dr2[...] = dr2
    df = dr2.astype(BF)
    out_df[...] = df
    out_vec[0:1, 0:768] = column_sum(dy * normed)
    out_vec[0:1, 768:1536] = column_sum(dr2)
    out_vec[0:1, 1536:2304] = column_sum(dy)
    for half in range(2):
        at = half * HALF
        du = mm(df, wd(half)[at : at + HALF, :], NT) * act_slope[:, at : at + HALF].astype(F32)
        out_vec[0:1, 2304 + at : 2304 + at + HALF] = column_sum(du)
        du_all[:, at : at + HALF] = du.astype(BF)

        @pl.when(meta.rep == half)
        def _():
            out_du[:, :] = du_all[:, at : at + HALF]

    out_du.start()
    out_dh[...] = mm(du_all[...], wi()[...], NT).astype(BF)


def attention_back_kernel(layer, chain, meta, own, got, dr2, r1, *refs):
    *vecs, qkv, probs_ref, own_q, got_q, own_o, got_o = refs[:8]
    out_dr1, out_dz, out_dqkv, out_dx, out_vec, wq, wo, sems = refs[8:]
    tag = meta.tag(chain)
    is_own = meta.section == layer
    wo = Weights(own_o, got_o, is_own, [(0, tag, None)], wo, sems, 3)
    wq = Weights(own_q, got_q, is_own, [(j, (tag, j), j) for j in range(3)], wq, sems)
    vector = vec_reader(vecs, is_own, tag)
    dh = (own[...].astype(F32) + got[...].astype(F32)) + dr2[...]
    normed, inverse = layer_norm(r1[...])
    dr1 = layer_norm_back(dh, vector(GAIN_ONE), normed, inverse)
    out_dr1[...] = dr1
    dz = dr1.astype(BF)
    out_dz[...] = dz
    out_vec[0:1, 0:768] = column_sum(dh * normed)
    out_vec[0:1, 768:1536] = column_sum(dr1)
    out_vec[0:1, 1536:2304] = column_sum(dh)
    datt = mm(dz, wo()[...], NT).astype(BF)
    query, key, value = (qkv[:, j * LOCAL : (j + 1) * LOCAL] for j in range(3))
    for pair in range(LOCAL // 128):
        at = slice(pair * 128, pair * 128 + 128)
        dv = dq = dk = None
        for which in range(2):
            probs = probs_ref[2 * pair + which]
            dv_term = mm(probs, half_mask(datt[:, at], which))
            dprobs = mm(half_mask(value[:, at], which), datt[:, at], NT)
            wide = probs.astype(F32)
            dscores = wide * (dprobs - jnp.sum(wide * dprobs, axis=0, keepdims=True))
            dscores = dscores.astype(BF)
            dk_term = mm(dscores, half_mask(query[:, at], which))
            dq_term = mm(dscores, half_mask(key[:, at], which), TN)
            dv = dv_term if dv is None else dv + dv_term
            dk = dk_term if dk is None else dk + dk_term
            dq = dq_term if dq is None else dq + dq_term
        dq = dq * 0.125
        dk = dk * 0.125
        low = pair * 128
        out_vec[0:1, 2304 + low : 2304 + low + 128] = column_sum(dq)
        out_vec[0:1, 2688 + low : 2688 + low + 128] = column_sum(dv)
        out_dqkv[:, low : low + 128] = dq.astype(BF)
        out_dqkv[:, LOCAL + low : LOCAL + low + 128] = dk.astype(BF)
        out_dqkv[:, 2 * LOCAL + low : 2 * LOCAL + low + 128] = dv.astype(BF)
    out_dqkv.start()
    dx = None
    for j in range(3):
        term = mm(out_dqkv[:, j * LOCAL : (j + 1) * LOCAL], wq(j)[j], NT)
        dx = term if dx is None else dx + term
    out_dx[...] = dx.astype(BF)


def far_kernel(layer, chains, meta, *refs):
    low, *vecs, own_i, got_i, out_act, out_slope, wi, sems = refs
    span = low.shape[0] // chains
    is_own = meta.section == layer
    half = pl.ds(pl.multiple_of(meta.rep * HALF, HALF), HALF)
    wi = Weights(own_i, got_i, is_own, [(0, (slice(None), slice(None), half), None)], wi, sems)()
    for chain in range(chains):
        tag = meta.far_tag(chain)
        at = slice(chain * span, (chain + 1) * span)
        bias = vec_reader(vecs, is_own, tag)(pl.multiple_of(BIAS_IN + meta.rep * HALF, HALF), HALF)
        pre = mm(low[at, :], wi[tag]) + bias
        out_act[at, :], out_slope[at, :] = gelu_and_slope(pre)


def order_of(tags, section):
    mine = [(tag == section).astype(jnp.int32) for tag in tags]
    count = sum(mine)
    places, before = [], 0
    for index, one in enumerate(mine):
        places.append(jnp.where(one == 1, before, count + index - before))
        before = before + one
    return places, count


class Gathered:
    def __init__(self, sources, places, target, sems, first):
        self.place, self.copies = target, []
        for index, (source, place) in enumerate(zip(sources, places)):
            extent = source.shape[0]
            at = pl.ds(pl.multiple_of(place * extent, extent), extent)
            copy = pltpu.make_async_copy(source, target.at[at], sems.at[first + index])
            copy.start()
            self.copies.append(copy)

    def wait(self):
        for copy in self.copies:
            copy.wait()
        return self.place


def both_models(count, chains, span, left, rights, stores):
    def branch(number):
        def products():
            cut = number * span
            for right, store in zip(rights, stores):
                columns = right.shape[1]
                for keeping, rows in ((False, slice(cut, chains * span)), (True, slice(0, cut))):
                    if rows.start == rows.stop:
                        store(keeping, jnp.zeros((left.shape[0], columns), BF))
                    else:
                        store(keeping, mm(left[:, rows], right[rows, :]).astype(BF))

        return products

    for number in range(chains + 1):
        pl.when(count == number)(branch(number))


def feed_grad_kernel(layer, chains, meta, *refs):
    df, act, du, far_df = (refs[i * chains : (i + 1) * chains] for i in range(4))
    low, far_low, far_act, slope_from, own_d, got_d, *refs = refs[4 * chains :]
    keep, send, df_all, act_all, low_all, du_all, far_slope, wd, sems = refs
    span = df[0].shape[0]
    half = pl.ds(pl.multiple_of(meta.rep * HALF, HALF), HALF)
    is_own = meta.section == layer
    tags = [meta.tag(chain) for chain in range(chains)] + [meta.far_tag(chain) for chain in range(chains)]
    places, count = order_of(tags, meta.section)
    split = lambda rows: [rows.at[pl.ds(chain * span, span)] for chain in range(chains)]
    df_all = Gathered([*df, *far_df], places, df_all, sems, 0)
    act_all = Gathered([*act, *split(far_act)], places, act_all, sems, 2 * chains)
    wd = Weights(own_d, got_d, is_own, [(0, (slice(None), half), None)], wd, sems, 8 * chains)
    far_slope = Lazy(slope_from, far_slope, sems, 8 * chains + 1, 1)
    far_slope.start()
    du_all = Gathered(du, places, du_all, sems, 4 * chains)
    low_all = Gathered([*split(low), *split(far_low)], places, low_all, sems, 6 * chains)

    def products(left_all, at, right):
        def column_block(index, carry):
            rows = pl.ds(pl.multiple_of(index * BLOCK, BLOCK), BLOCK)
            left = left_all[:, rows].T

            def store(keeping, value):
                out = keep.place if keeping else send
                out[rows, at : at + HALF] = value

            both_models(count, 2 * chains, span, left, [right], [store])
            return carry

        lax.fori_loop(0, WIDTH // BLOCK, column_block, 0)
        keep.start(at // HALF)

    lefts = df_all.wait()
    products(lefts, 0, act_all.wait())
    rights = du_all.wait()
    weights = wd()
    for chain in range(chains):
        at = slice(chain * span, (chain + 1) * span)
        there = pl.ds(pl.multiple_of(places[chains + chain] * span, span), span)
        value = mm(lefts[there, :], weights[meta.far_tag(chain)], NT) * far_slope[at, :].astype(F32)
        rights[there, :] = value.astype(BF)
    products(low_all.wait(), HALF, rights)


def attention_grad_kernel(layer, chains, meta, *refs):
    dz, att, x, dqkv = (refs[i * chains : (i + 1) * chains] for i in range(4))
    keep, send, dz_all, att_all, x_all, dqkv_all, sems = refs[4 * chains :]
    span = dz[0].shape[0]
    if layer == 0:
        x = [ref.at[chain, meta.section] for chain, ref in enumerate(x)]
    places, count = order_of([meta.tag(chain) for chain in range(chains)], meta.section)
    dz_all = Gathered(dz, places, dz_all, sems, 0)
    att_all = Gathered(att, places, att_all, sems, chains)
    x_all = Gathered(x, places, x_all, sems, 2 * chains)
    dqkv_all = Gathered(dqkv, places, dqkv_all, sems, 3 * chains)

    def products(left_all, rights, targets):
        def column_block(index, carry):
            rows = pl.ds(pl.multiple_of(index * BLOCK, BLOCK), BLOCK)
            left = left_all[:, rows].T

            def store_at(slot, columns):
                def store(keeping, value):
                    out = keep.place if keeping else send
                    if layer == 1:
                        out[rows, columns.start + slot * HALF : columns.stop + slot * HALF] = value
                    else:
                        out[jnp.where(meta.rep == 0, slot, 1 - slot), rows, columns] = value

                return store

            both_models(count, chains, span, left, rights, [store_at(*target) for target in targets])
            return carry

        lax.fori_loop(0, WIDTH // BLOCK, column_block, 0)

    left_all, right = dz_all.wait(), att_all.wait()
    products(left_all, [right], [(0, slice(0, LOCAL))])
    left_all, right = x_all.wait(), dqkv_all.wait()
    rights = [right.at[:, pl.ds(0, LOCAL)], right.at[:, pl.ds(LOCAL, 2 * LOCAL)]]
    products(left_all, rights, [(0, slice(LOCAL, HALF)), (1, slice(0, HALF))])


def add_kernel(parts, meta, one, two, out):
    block = one.shape[0] // parts
    for part in range(parts):
        at = slice(part * block, (part + 1) * block)
        one.wait(part)
        out[at, :] = one.place[at, :] + two[at, :]
        out.start(part)


def add_halves_kernel(meta, one, two, near, far):
    for half, out in ((1, far), (0, near)):
        one.wait(half)
        out[...] = one.place[half] + two[half]


BLOCK = 256
ANY = pl.BlockSpec(memory_space=pl.ANY)


def pack_kernel(gains, shifts, b_qv, b_in, out):
    for model in range(2):
        row = slice(model, model + 1)
        for j in range(2):
            out[row, j * WIDTH : (j + 1) * WIDTH] = gains[0, model, j : j + 1, :]
            out[row, BIAS_Q + j * LOCAL : BIAS_Q + (j + 1) * LOCAL] = b_qv[0, model, j : j + 1, :]
        for j in range(4):
            out[row, SHIFT[j] : SHIFT[j] + WIDTH] = shifts[0, model, j : j + 1, :]
        out[row, BIAS_IN:] = b_in[0, row, :]


def feed_final_kernel(meta, *refs):
    zero, one, got, grad_in, grad_out = refs[:2], refs[2:4], refs[4], refs[5], refs[6]
    for half in range(2):
        local = jnp.where(meta.rep == 0, half, 1 - half)
        mine = jnp.where(meta.section == 0, zero[half][...], one[half][...]).astype(F32)
        columns = pl.ds(pl.multiple_of(local * HALF, HALF), HALF)
        for model, shard in ((meta.section, mine), (1 - meta.section, got[half].astype(F32))):
            grad_out[model, :, columns] = shard[:, 0:HALF]
            grad_in[model, :, columns] = shard[:, HALF:]


def attention_final_kernel(meta, *refs):
    zero, got_zero, (one, got_one, grad_qkv, grad_o) = refs[:2], refs[2:4], refs[4:]
    for model, halves, whole in ((meta.section, zero, one), (1 - meta.section, got_zero, got_one)):
        near, far = halves[0][...], halves[1][...]
        low = jnp.where(meta.rep == 0, near, far)
        high = jnp.where(meta.rep == 0, far, near)
        low = jnp.where(meta.section == 0, low, whole[:, 0:HALF]).astype(F32)
        high = jnp.where(meta.section == 0, high, whole[:, HALF:]).astype(F32)
        grad_o[model] = low[:, 0:LOCAL]
        grad_qkv[model, 0] = low[:, LOCAL:]
        grad_qkv[model, 1] = high[:, 0:LOCAL]
        grad_qkv[model, 2] = high[:, LOCAL:]


def vector_grad_kernel(chains, meta, *refs):
    out = refs[-1]
    for layer in range(2):
        ones = refs[2 * layer * chains : (2 * layer + 1) * chains]
        twos = refs[(2 * layer + 1) * chains : (2 * layer + 2) * chains]
        rows = [
            jnp.concatenate(
                [one[0:1, 0:768], two[0:1, 0:768], one[0:1, 768:2304], two[0:1, 768:2304], one[0:1, 2304:], two[0:1, 2304:]],
                axis=1,
            )
            for one, two in zip(ones, twos)
        ]
        for model in range(2):
            total = None
            for chain in range(chains):
                row = jnp.where(meta.tag(chain) == model, rows[chain], 0.0)
                total = row if total is None else total + row
            out[layer, model : model + 1, :] = total


STEP = 1.5e9
LONG = 8

VMEM = pl.BlockSpec(memory_space=pltpu.VMEM)
SMEM = pl.BlockSpec(memory_space=pltpu.SMEM)
SAVED, PARTLY = "saved", "partly"


def pieces_of(out):
    return out[3] if len(out) > 3 else [None]


def in_hbm(value):
    return pltpu.with_memory_space_constraint(value, pltpu.HBM)


def call(body, scalars, operands, outs, scratch, name, grant, cost):
    saved_in = [value for value in operands if isinstance(value, Saved)]
    saved_out = [out for out in outs if SAVED in out]
    buffers = [pltpu.VMEM(value.shape, value.value.dtype) for value in saved_in]
    buffers += [pltpu.VMEM(out[0], out[1]) for out in saved_out]
    counts = (len(scalars), len(operands), len(outs), len(scratch))

    def kernel(*refs):
        groups = []
        for count in counts:
            groups.append(refs[:count])
            refs = refs[count:]
        numbers, ins, results, own_scratch = groups
        *places, sems = refs
        meta = Scalars(*numbers)
        given, taken, index, sem = [], [], 0, 0
        for value, ref in zip(operands, ins):
            if isinstance(value, Saved):
                source = ref if value.chain is None else ref.at[value.chain, meta.section]
                ref = Lazy(source, places[index], sems, sem, value.parts)
                ref.start()
                sem += value.parts
                index += 1
            given.append(ref)
        for out, ref in zip(outs, results):
            if SAVED in out:
                ref = Leaving(places[index], ref, sems, sem, pieces_of(out))
                sem += len(pieces_of(out))
                index += 1
            taken.append(ref)
        body(meta, *given, *taken, *own_scratch)
        for ref in taken:
            if isinstance(ref, Leaving):
                ref.start()
        for ref in given:
            if isinstance(ref, Lazy):
                ref.wait()
        for ref in taken:
            if isinstance(ref, Leaving):
                ref.wait()

    in_specs = [ANY if isinstance(value, (tuple, Saved)) else VMEM for value in operands]
    values = []
    for value in operands:
        if isinstance(value, Saved):
            value = in_hbm(value.value)
        elif isinstance(value, tuple):
            value = in_hbm(value[0])
        values.append(value)
    shapes = [
        pltpu.HBM(*out[:2]) if SAVED in out or PARTLY in out else jax.ShapeDtypeStruct(*out[:2]) for out in outs
    ]
    return pl.pallas_call(
        kernel,
        out_shape=shapes,
        in_specs=[SMEM] * len(scalars) + in_specs,
        out_specs=[ANY if SAVED in out or PARTLY in out else VMEM for out in outs],
        input_output_aliases={
            len(scalars) + out[3]: index for index, out in enumerate(outs) if PARTLY in out and len(out) > 3
        },
        scratch_shapes=[*scratch, *buffers, pltpu.SemaphoreType.DMA((max(sum(value.parts for value in saved_in) + sum(len(pieces_of(out)) for out in saved_out), 1),))],
        compiler_params=pltpu.CompilerParams(vmem_limit_bytes=grant * 1024 * 1024),
        cost_estimate=pl.CostEstimate(flops=int(cost * STEP), bytes_accessed=1, transcendentals=0),
        name=name,
    )(*scalars, *values)


def on_device(
    block_input, cotangent, lengths, tags, w_qkv, w_o, w_in, w_out, b_qv, b_in, gains, shifts
):
    micro, per, span, width = block_input.shape
    section = lax.axis_index("section")
    rep = lax.axis_index("rep")
    chains = range(micro)
    layers = range(2)

    own_q, own_o, own_i, own_d = w_qkv[0], w_o[0], w_in[0], w_out[0]
    got_q = swap(own_q, "section")
    vec_own = pl.pallas_call(
        pack_kernel, out_shape=jax.ShapeDtypeStruct((2, PACKED), F32), in_specs=[VMEM] * 4, out_specs=VMEM, name="pack"
    )(gains, shifts, b_qv, b_in)
    numbers = jnp.concatenate([lengths, tags], axis=1)
    vec_own = after(vec_own, numbers)
    vecs = [vec_own, swap(vec_own, "section")]
    got_o = swap(own_o, "section")
    later = lax.optimization_barrier((own_i, own_d, got_q, got_o, vecs[1]))
    got_i, got_d = swap(later[0], "section"), swap(later[1], "section")

    heads = LOCAL // HD
    row, saved_row = ((span, WIDTH), BF), ((span, WIDTH), BF, SAVED)
    wide, saved_wide = ((span, WIDTH), F32), ((span, WIDTH), F32, SAVED)
    half_row, long_row = ((span, HALF), BF, SAVED), ((span, HIDDEN), BF, SAVED)
    qkv_row = ((span, 3 * LOCAL), BF, SAVED)
    att_outs = [qkv_row, ((heads, span, span), BF, SAVED), ((span, LOCAL), BF, SAVED), row]
    raw = lambda values: [(value,) for value in values]
    w_qo, w_id = raw([own_q, got_q, own_o, got_o]), raw([own_i, got_i, own_d, got_d])
    qo_scratch = [
        pltpu.VMEM((3, WIDTH, LOCAL), BF),
        pltpu.VMEM((LOCAL, WIDTH), BF),
        pltpu.SemaphoreType.DMA((4,)),
    ]
    id_scratch = [
        pltpu.VMEM((span, HIDDEN), BF),
        pltpu.VMEM((WIDTH, HIDDEN), BF),
        pltpu.VMEM((HIDDEN, WIDTH), BF),
        pltpu.SemaphoreType.DMA((3,)),
    ]
    feed_scratch = id_scratch[:3] + [pltpu.VMEM((span, WIDTH), BF), pltpu.SemaphoreType.DMA((4,))]

    last = [numbers]

    def run(body, operands, outs, scratch, name, *waits, far=False, grant=14, cost=1):
        scalars = [after(numbers, last[0], *waits)] + ([far_tags] if far else [])
        results = call(body, scalars, operands, outs, scratch, name, grant, cost)
        last[0] = results[-1]
        return results

    def saved(values):
        return [Saved(value) for value in values]

    def arrived(pair):
        return list(pair)

    def owned(zero, one):
        zero, one = jnp.stack(zero), jnp.stack(one)
        mine = jnp.where(section == 0, zero, one)
        other = swap(jnp.where(section == 0, one, zero), "section")
        core = lax.broadcasted_iota(jnp.int32, (micro, per, span, width), 1)
        return jnp.where(core == section, mine[:, None], other[:, None])[None]

    table = lambda: [[None] * micro for _ in layers]
    r1s, r2s, hiddens, acts, slopes, feeds, qkvs, probs, atts = (table() for _ in range(9))
    lows, far_lows = [None, None], [None, None]
    x_now, x_saved = [[Saved(block_input, chain) for chain in chains], [None] * micro], [None] * micro
    for layer in layers:
        for chain in chains:
            body = functools.partial(attention_kernel, layer, chain)
            name = f"attention{layer}{chain}"
            if layer == 0:
                got = run(body, [x_now[0][chain], *vecs] + w_qo, att_outs, qo_scratch, name)
            else:
                operands = [*arrived(feeds[0][chain]), hiddens[0][chain], *vecs] + w_qo
                waits = []
                x_now[1][chain], x_saved[chain], r2s[0][chain], *got = run(
                    body, operands, [row, saved_row, saved_wide] + att_outs, qo_scratch, name, *waits
                )
            qkvs[layer][chain], probs[layer][chain], atts[layer][chain], branch = got
            feeds[layer][chain] = (branch, swap(branch, "mp"))
        if layer == 0:
            far_tags = swap(after(tags, last[0]), "rep")
        for chain in chains:
            body = functools.partial(feed_kernel, layer, chain)
            waits = [far_tags] if layer == 0 and chain == 2 else []
            operands = [x_now[layer][chain], *feeds[layer][chain], *vecs] + w_id
            rows_out = ((micro * span, WIDTH), BF, PARTLY)
            if chain:
                rows_out += (len(operands),)
                operands.append((lows[layer],))
            hiddens[layer][chain], r1s[layer][chain], slopes[layer][chain], acts[layer][chain], lows[layer], part = run(
                body,
                operands,
                [wide, saved_wide, long_row, half_row, rows_out, row],
                feed_scratch,
                f"feed{layer}{chain}",
                *waits,
            )
            feeds[layer][chain] = (part, swap(part, "mp"))
        far_lows[layer] = swap(lows[layer], "rep")

    rows = micro * span
    far_rows = ((rows, HALF), BF, SAVED)
    dr2s, dfs, far_dfs, dus, dhs, vec_one, vec_two, dzs, dqkvs, dr1s, dxs, ys = (table() for _ in range(12))
    far_hidden = [None, None]

    def feed_back(layer, chain, *waits, cost=1):
        if layer == 1:
            operands = [*arrived(feeds[1][chain]), hiddens[1][chain], Saved(cotangent, chain)]
        else:
            operands = [*arrived(dxs[1][chain]), Saved(dr1s[1][chain]), Saved(r2s[0][chain])]
        ys[layer][chain], dr2s[layer][chain], df, dus[layer][chain], dh, vec_two[layer][chain] = run(
            functools.partial(feed_back_kernel, layer, chain),
            operands + [*vecs, Saved(slopes[layer][chain])] + w_id,
            [saved_row, saved_wide, saved_row, half_row, row, ((8, 3 * WIDTH + HIDDEN), F32, SAVED)],
            id_scratch,
            f"feed_back{layer}{chain}",
            *waits,
            cost=cost,
        )
        dfs[layer][chain], far_dfs[layer][chain] = df, swap(df, "rep")
        dhs[layer][chain] = (dh, swap(dh, "mp"))

    def attention_back(layer, chain, *waits, cost=1):
        dr1s[layer][chain], dzs[layer][chain], dqkvs[layer][chain], dx, vec_one[layer][chain] = run(
            functools.partial(attention_back_kernel, layer, chain),
            [*arrived(dhs[layer][chain]), Saved(dr2s[layer][chain]), Saved(r1s[layer][chain]), *vecs]
            + [Saved(qkvs[layer][chain]), Saved(probs[layer][chain])]
            + w_qo,
            [saved_wide, saved_row, qkv_row, row, ((8, 3 * WIDTH + 2 * LOCAL), F32, SAVED)],
            qo_scratch,
            f"attention_back{layer}{chain}",
            *waits,
            cost=cost,
        )
        dxs[layer][chain] = (dx, swap(dx, "mp"))

    def far_part(layer, *waits, cost=1.5):
        far_hidden[layer] = run(
            functools.partial(far_kernel, layer, micro),
            [Saved(far_lows[layer]), *vecs] + w_id[:2],
            [far_rows] * 2,
            [pltpu.VMEM((2, WIDTH, HALF), BF), pltpu.SemaphoreType.DMA((1,))],
            f"far{layer}",
            *waits,
            far=True,
            cost=cost,
        )

    def feed_grad(layer, *waits, cost=2):
        near = dfs[layer] + acts[layer] + dus[layer] + far_dfs[layer]
        far_act, far_slope = far_hidden[layer]
        stacked = pltpu.VMEM((2 * rows, HALF), BF)
        keep, send = run(
            functools.partial(feed_grad_kernel, layer, micro),
            raw(near + [lows[layer], far_lows[layer], far_act, far_slope]) + w_id[2:],
            [((WIDTH, HIDDEN), BF, SAVED, blocks_of(WIDTH, HIDDEN, WIDTH, HALF)), ((WIDTH, HIDDEN), BF)],
            [stacked] * 4
            + [pltpu.VMEM((rows, HALF), BF), pltpu.VMEM((2, HALF, WIDTH), BF), pltpu.SemaphoreType.DMA((8 * micro + 2,))],
            f"feed_grad{layer}",
            *waits,
            far=True,
            grant=20,
            cost=cost,
        )
        return keep, swap(send, "section")

    def whole_sum(name, parts, *waits):
        (result,) = run(
            functools.partial(add_kernel, WIDTH // BLOCK),
            [Saved(parts[0], parts=WIDTH // BLOCK), parts[1]],
            [((WIDTH, HIDDEN), BF, SAVED, blocks_of(WIDTH, HIDDEN, BLOCK, HIDDEN))],
            [],
            name,
            *waits,
        )
        return result

    def attention_grad(layer, *waits):
        x_part = raw([block_input] * micro if layer == 0 else x_saved)
        narrow, stacked = pltpu.VMEM((rows, LOCAL), BF), pltpu.VMEM((rows, WIDTH), BF)
        shape = (WIDTH, HIDDEN) if layer == 1 else (2, WIDTH, HALF)
        pieces = [None] if layer == 1 else [pl.ds(0, 1), pl.ds(1, 1)]
        keep, send = run(
            functools.partial(attention_grad_kernel, layer, micro),
            raw(dzs[layer] + atts[layer]) + x_part + raw(dqkvs[layer]),
            [(shape, BF, SAVED, pieces), (shape, BF)],
            [stacked, narrow, stacked, pltpu.VMEM((rows, 3 * LOCAL), BF), pltpu.SemaphoreType.DMA((4 * micro,))],
            f"attention_grad{layer}",
            *waits,
            cost=2,
        )
        return keep, swap(send, "section")

    def attention_grad_sum(layer, parts, *waits):
        near, far = run(
            add_halves_kernel,
            [Saved(parts[0], parts=2), parts[1]],
            [((WIDTH, HALF), BF, SAVED)] * 2,
            [],
            f"attention_grad_sum{layer}",
            *waits,
        )
        return near, swap(far, "rep")

    def scattered(part):
        return lax.psum_scatter(part, "dp", scatter_dimension=0, tiled=True)

    feed_back(1, 0, far_lows[0])
    feed_back(1, 1)
    feed_back(1, 2, cost=3)
    far_part(1, dhs[1][0][1], far_dfs[1][0])
    parts = feed_grad(1, dhs[1][1][1], far_dfs[1][1])
    far_part(0, dhs[1][2][1], cost=20)
    feed_one = scattered(whole_sum("feed_grad_sum1", parts))
    attention_back(1, 0)
    attention_back(1, 1)
    attention_back(1, 2, dxs[1][0][1])
    parts = attention_grad(1, dxs[1][1][1])
    feed_back(0, 0, cost=8)
    attention_one = whole_sum("attention_grad_sum1", parts)
    feed_back(0, 1, dxs[1][2][1])
    attention_one = scattered(after(attention_one, feed_one, last[0]))
    feed_back(0, 2)
    attention_back(0, 0, feed_one, far_dfs[0][0], far_dfs[0][1])
    feed_one = (feed_one, swap(feed_one, "rep"))
    parts = feed_grad(0, dhs[0][2][1], dhs[0][1][1])
    attention_back(0, 1, cost=LONG)
    summed = whole_sum("feed_grad_sum0", parts)
    attention_one = after(attention_one, summed)
    feed_zero = scattered(after(summed, attention_one))
    attention_back(0, 2, attention_one, cost=2.75)
    attention_one = (attention_one, swap(after(attention_one, summed), "rep"))
    parts = attention_grad(0, feed_one[1])
    (both,) = run(
        functools.partial(vector_grad_kernel, micro),
        saved(vec_one[0] + vec_two[0] + vec_one[1] + vec_two[1]),
        [((2, 2, PACKED), F32)],
        [],
        "vector_grad",
        attention_one[1],
        *[dx[1] for dx in dxs[0][:2]],
        cost=20,
    )
    near, far = attention_grad_sum(0, parts)
    both = after(both, near)
    both = both + swap(both, "section")
    both = lax.dynamic_index_in_dim(both, section, 0, keepdims=False)
    data = lax.axis_size("dp")
    distance = 1
    while distance < data:
        both = both + lax.ppermute(both, "dp", [(i, i ^ distance) for i in range(data)])
        distance *= 2
    def first_grad(chain, *others):
        (own, got), dr1 = dxs[0][chain], dr1s[0][chain]
        return ((after(own, *others).astype(F32) + got.astype(F32)) + dr1).astype(BF)

    firsts = [first_grad(chain, near, both) for chain in chains[:-1]]
    firsts.append(first_grad(micro - 1, *firsts))
    attention_zero = after(after(near, firsts) + far, feed_zero)
    done = attention_zero
    both = both + swap(after(both, done), "rep")
    feed_zero = (feed_zero, swap(after(feed_zero, done), "rep"))
    attention_one = (after(attention_one[0], done).astype(F32) + attention_one[1].astype(F32)).astype(BF)
    feed_zero = (feed_zero[0], after(feed_zero[1], attention_one))
    layer_outputs = owned(after(x_saved, done), ys[1])
    grad_gains = both[:, : SHIFT[0]].reshape(2, 2, WIDTH)
    grad_shifts = both[:, SHIFT[0] : BIAS_Q].reshape(2, 4, WIDTH)
    grad_b_qv = both[:, BIAS_Q:BIAS_IN].reshape(2, 2, LOCAL)
    grad_b_in = both[:, BIAS_IN:]
    attention_zero = scattered(attention_zero)

    def handed(zero, one):
        return swap(jnp.where(section == 0, jnp.stack(one), jnp.stack(zero)), "section")

    shard = feed_zero[0].shape[0]
    grad_in, grad_out = run(
        feed_final_kernel,
        [*feed_zero, *feed_one, handed(feed_zero, feed_one)],
        [((2, shard, HIDDEN), F32)] * 2,
        [],
        "feed_final",
    )
    input_grads = owned(after(firsts, done), ys[0])
    got_one = swap(attention_one, "section")
    attention_zero = after(attention_zero, input_grads, layer_outputs, got_one)
    vectors = grad_b_qv[None], grad_b_in[None], grad_gains[None], grad_shifts[None]
    far, vectors, _ = lax.optimization_barrier((swap(attention_zero, "rep"), vectors, grad_in))
    got_zero = swap(attention_zero, "section"), swap(far, "section")
    attention_zero = (attention_zero, far)
    grad_qkv, grad_o = run(
        attention_final_kernel,
        [*attention_zero, *got_zero, attention_one, got_one],
        [((2, 3, shard, LOCAL), F32), ((2, shard, LOCAL), F32)],
        [],
        "attention_final",
    )
    grad_out, grad_o = jnp.swapaxes(grad_out, 1, 2), jnp.swapaxes(grad_o, 1, 2)

    return (
        layer_outputs,
        input_grads,
        grad_qkv[None],
        grad_o[None],
        grad_in[None],
        grad_out[None],
        *vectors,
    )


def solution(mesh):
    in_specs = (
        P(None, ("dp", "rep"), None, None),
        P(None, ("dp", "rep"), None, None),
        P(None, ("dp", "rep")),
        P(None, ("dp", "rep")),
        P("section", None, None, None, "mp"),
        P("section", None, "mp", None),
        P("section", None, None, "mp"),
        P("section", None, "mp", None),
        P("section", None, None, "mp"),
        P("section", None, "mp"),
        P("section", None, None, None),
        P("section", None, None, None),
    )
    out_specs = (
        P("section", None, ("dp", "rep"), None, None),
        P("section", None, ("dp", "rep"), None, None),
        P("section", None, None, "dp", "mp"),
        P("section", None, "mp", "dp"),
        P("section", None, "dp", "mp"),
        P("section", None, "mp", "dp"),
        P("section", None, None, "mp"),
        P("section", None, "mp"),
        P("section", None, None, None),
        P("section", None, None, None),
    )
    return jax.shard_map(
        on_device, mesh=mesh, in_specs=in_specs, out_specs=out_specs, check_vma=False
    )
```
